256 devices in a mesh: seg: 8 (over y_hi, x), blk: 32 (over z, y_lo, core).
Axes of the slice: x: 4, y: 4 (y_hi: 2, y_lo: 2; y = y_hi * 2 + y_lo), z: 8, core: 2. Of those that a mesh axis runs over, the one named last changes fastest.
Arguments:
- state: float32 [256, 4, 16, 2304], P(('seg', 'blk')), may hold values from -6 to 6
- metric: float32 [256, 9, 16, 2304], P(('seg', 'blk')), may hold values from -0.4 to 3, as said below
- block_map: int32 [256], replicated, may hold values from 0 to 255, as said below
- links: int32 [256, 6, 4], replicated, may hold values from -1 to 255, as said below
Outputs:
- advanced: float32 [256, 4, 16, 2304], P(('seg', 'blk'))
The draws below stay inside these ranges and needn't reach their ends.
Inputs may be any that keep to these rules, and one draw needn't show every extreme that they name: A permutation of the block numbers; device slot d = s * 32 + p (segment s, position p along its chain) holds block block_map[d]. `links`: entries are (partner block or -1, partner face, r_i, r_x). Face 0 of the block at position p > 0 joins face 1 of the block at position p - 1 of the same segment, face 1 at p < 31 joins face 0 at p + 1, both with zero flags; faces 0 at p = 0 and 1 at p = 31 have partner -1. A block has at most one of faces 2 to 5 with a partner, and some blocks have one; that partner lies at the same position p in another segment, names this block and face back with the same flags. Unused fields of a face with partner -1 are 0. `metric`: entries 0, 4 and 8 of the second dimension are positive.
All inputs are finite; a program needn't handle non-finite values.
Results may differ from the reference program's by a relative error of at most 0.0003.
Values sent between devices are 32-bit elements; how exact they have to be, the bound alone decides.
No kernel may reach another device: no remote copies, remote signals or barrier semaphores. Data moves between devices by JAX's collectives and lax.ppermute only.
A program may use at most 64 MiB of HBM per device.

```python
import math
import jax
import jax.numpy as jnp
from jax import lax

LEN = 16
CROSS = 48
SEGS = 8
CHAIN = 32
BLOCKS = 256


def tree_layout(key):
    base = jax.random.fold_in(key, 101)
    subkeys = jax.random.split(base, 5)
    device_blocks = jax.random.permutation(subkeys[0], BLOCKS).astype(jnp.int32)
    row_keys = jax.random.split(subkeys[1], CHAIN)
    pairings = jax.vmap(lambda row_key: jax.random.permutation(row_key, SEGS))(row_keys).astype(jnp.int32)
    slot_of = jnp.argsort(pairings, axis=1).astype(jnp.int32)
    joined_draw = jax.random.randint(subkeys[2], (CHAIN, SEGS // 2), 0, 2).astype(jnp.int32)
    joined_draw = joined_draw.at[0, 0].set(1)
    face_draw = jax.random.randint(subkeys[3], (CHAIN, SEGS), 2, 6).astype(jnp.int32)
    flip_draw = jax.random.randint(subkeys[4], (CHAIN, SEGS // 2, 2), 0, 2).astype(jnp.int32)
    devices = jnp.arange(BLOCKS, dtype=jnp.int32)
    segment = devices // CHAIN
    position = devices % CHAIN
    slot_index = slot_of[position, segment]
    mate_slot = jnp.bitwise_xor(slot_index, 1)
    pair_index = slot_index // 2
    mate_device = pairings[position, mate_slot] * CHAIN + position
    joined = joined_draw[position, pair_index] == 1
    my_face = face_draw[position, slot_index]
    mate_face = face_draw[position, mate_slot]
    flip_pair = flip_draw[position, pair_index]
    zeros = jnp.zeros((BLOCKS,), jnp.int32)
    has_before = position > 0
    has_after = position < CHAIN - 1
    before = jnp.where(has_before, device_blocks[jnp.clip(devices - 1, 0, BLOCKS - 1)], -1)
    after = jnp.where(has_after, device_blocks[jnp.clip(devices + 1, 0, BLOCKS - 1)], -1)
    rows = [jnp.stack([before, jnp.where(has_before, 1, 0), zeros, zeros], axis=1), jnp.stack([after, zeros, zeros, zeros], axis=1)]
    for side in range(2, 6):
        active = joined & (my_face == side)
        rows.append(jnp.stack([jnp.where(active, device_blocks[mate_device], -1), jnp.where(active, mate_face, 0), jnp.where(active, flip_pair[:, 0], 0), jnp.where(active, flip_pair[:, 1], 0)], axis=1))
    by_device = jnp.stack(rows, axis=1).astype(jnp.int32)
    links = jnp.zeros((BLOCKS, 6, 4), jnp.int32).at[device_blocks].set(by_device)
    return (device_blocks, links)


def draw_block_map(key, part):
    return tree_layout(key)[0]


def draw_links(key, part):
    return tree_layout(key)[1]


def draw_metric(key, part):
    subkeys = jax.random.split(jax.random.fold_in(key, 202), 2)
    dims = (BLOCKS, 9, LEN, CROSS * CROSS)
    diagonal_mask = jnp.array([1, 0, 0, 0, 1, 0, 0, 0, 1], jnp.float32).reshape(1, 9, 1, 1)
    diagonal = jnp.exp(jax.random.uniform(subkeys[0], dims, jnp.float32, math.log(0.5), math.log(2.0)))
    off_diagonal = jax.random.uniform(subkeys[1], dims, jnp.float32, -0.4, 0.4)
    return diagonal_mask * diagonal + (1.0 - diagonal_mask) * off_diagonal


def steps_of(rng, shape, shards, smallest, largest):
    level, own = 1.0, jax.random.fold_in(rng, 6)
    for dim, blocks in shards:
        steps = jnp.exp(jax.random.uniform(jax.random.fold_in(own, dim), (blocks,), jnp.float32, smallest / len(shards), largest / len(shards)))
        level = level * jnp.repeat(steps, shape[dim] // blocks).reshape([-1 if axis == dim else 1 for axis in range(len(shape))])
    return level


def scatter_about(own_key, shape, scale, bound, shards=(), kind=jnp.bfloat16):
    loudness = steps_of(own_key, shape, shards, -0.22, 0.18) if shards else 1.0
    drawn = jax.random.normal(own_key, shape, jnp.float32) * scale * loudness
    return jnp.minimum(jnp.maximum(drawn, -bound), bound).astype(kind)


def setup_inputs(seed: int = 0) -> dict:
    streams_of = jax.random.split(jax.random.key(seed), 5)
    state = scatter_about(streams_of[0], (BLOCKS, 4, LEN, CROSS * CROSS), 1.0, 6.0, ((0, 256),), jnp.float32)
    metric = draw_metric(jax.random.fold_in(streams_of[4], 71), 0)
    block_map = draw_block_map(jax.random.fold_in(streams_of[4], 71), 0)
    links = draw_links(jax.random.fold_in(streams_of[4], 71), 0)
    return dict(state=state, metric=metric, block_map=block_map, links=links)


time_step = 0.05
viscosity = 0.2
compress = 1.0


def wall_mirror():
    return jnp.array([-1.0, -1.0, -1.0, 1.0], jnp.float32).reshape(4, 1, 1)


def shifted(extended, direction, offset):
    count = extended.shape[direction] - 4
    return lax.slice_in_dim(extended, offset, offset + count, axis=direction)


def slope(extended, direction):
    return (shifted(extended, direction, 0) - 8.0 * shifted(extended, direction, 1)
            + 8.0 * shifted(extended, direction, 3) - shifted(extended, direction, 4)) / 12.0


def curvature(extended, direction):
    return (-shifted(extended, direction, 0) + 16.0 * shifted(extended, direction, 1)
            - 30.0 * shifted(extended, direction, 2) + 16.0 * shifted(extended, direction, 3)
            - shifted(extended, direction, 4)) / 12.0


def rates(block_state, geometry, padded):
    slopes = [slope(padded[direction], direction + 1) for direction in range(3)]
    bends = [curvature(padded[direction], direction + 1) for direction in range(3)]
    contravariant = []
    metric_norms = []
    for direction in range(3):
        base = 3 * direction
        contravariant.append(geometry[base] * block_state[0] + geometry[base + 1] * block_state[1]
                             + geometry[base + 2] * block_state[2])
        metric_norms.append(geometry[base] * geometry[base] + geometry[base + 1] * geometry[base + 1]
                            + geometry[base + 2] * geometry[base + 2])
    results = []
    for component in range(3):
        convect = sum(contravariant[direction] * slopes[direction][component] for direction in range(3))
        gradient = sum(geometry[3 * direction + component] * slopes[direction][3] for direction in range(3))
        diffuse = sum(metric_norms[direction] * bends[direction][component] for direction in range(3))
        results.append(-convect - gradient + viscosity * diffuse)
    divergence = sum(geometry[3 * direction + component] * slopes[direction][component]
                     for direction in range(3) for component in range(3))
    results.append(-compress * divergence)
    return jnp.stack(results)


def lateral_faces(block_state):
    edge = block_state.shape[2]
    lower_j = jnp.stack([block_state[:, :, 0, :], block_state[:, :, 1, :]])
    upper_j = jnp.stack([block_state[:, :, edge - 1, :], block_state[:, :, edge - 2, :]])
    lower_k = jnp.stack([block_state[:, :, :, 0], block_state[:, :, :, 1]])
    upper_k = jnp.stack([block_state[:, :, :, edge - 1], block_state[:, :, :, edge - 2]])
    return jnp.stack([lower_j, upper_j, lower_k, upper_k])


def pad_lateral(block_state, ghost_layers):
    lower_j = jnp.stack([ghost_layers[0][1], ghost_layers[0][0]], axis=2)
    upper_j = jnp.stack([ghost_layers[1][0], ghost_layers[1][1]], axis=2)
    lower_k = jnp.stack([ghost_layers[2][1], ghost_layers[2][0]], axis=3)
    upper_k = jnp.stack([ghost_layers[3][0], ghost_layers[3][1]], axis=3)
    across_first = jnp.concatenate([lower_j, block_state, upper_j], axis=2)
    across_second = jnp.concatenate([lower_k, block_state, upper_k], axis=3)
    return across_first, across_second


def orient(layers, flip_along, flip_across):
    layers = jnp.where(flip_along == 1, jnp.flip(layers, 2), layers)
    return jnp.where(flip_across == 1, jnp.flip(layers, 3), layers)


def open_rows(block_state):
    mirror = -wall_mirror()
    lower = jnp.stack([mirror * block_state[:, 1], mirror * block_state[:, 0]], axis=1)
    upper = jnp.stack([mirror * block_state[:, -1], mirror * block_state[:, -2]], axis=1)
    return lower, upper


def device_of(block_map, block):
    return jnp.argmax(block_map == jnp.maximum(block, 0)).astype(jnp.int32)


def reference(state, metric, block_map, links):
    count = state.shape[0]
    length = state.shape[2]
    whole = state.reshape(count, 4, length, CROSS, CROSS)
    geometry_all = metric.reshape(count, 9, length, CROSS, CROSS)

    def all_rates(current):
        face_layers = jax.vmap(lateral_faces)(current)

        def per_block(device):
            block_state = current[device]
            entries = links[block_map[device]]
            open_lower, open_upper = open_rows(block_state)
            before = current[device_of(block_map, entries[0, 0])][:, length - 2:]
            after = current[device_of(block_map, entries[1, 0])][:, :2]
            lower = jnp.where(entries[0, 0] >= 0, before, open_lower)
            upper = jnp.where(entries[1, 0] >= 0, after, open_upper)
            along_vessel = jnp.concatenate([lower, block_state, upper], axis=1)
            ghost_layers = []
            for side in range(4):
                entry = entries[2 + side]
                partner = face_layers[device_of(block_map, entry[0]), jnp.clip(entry[1] - 2, 0, 3)]
                partner = orient(partner, entry[2], entry[3])
                ghost_layers.append(jnp.where(entry[0] >= 0, partner, wall_mirror() * face_layers[device, side]))
            across_first, across_second = pad_lateral(block_state, ghost_layers)
            return rates(block_state, geometry_all[device], (along_vessel, across_first, across_second))

        return lax.map(per_block, jnp.arange(count, dtype=jnp.int32))

    first_section = whole + time_step * all_rates(whole)
    advanced = 0.5 * whole + 0.5 * (first_section + time_step * all_rates(first_section))
    return advanced.reshape(state.shape)
```

```python
import functools
import jax
import jax.numpy as jnp
from jax import lax
from jax.experimental import pallas as pl
from jax.experimental.pallas import tpu as pltpu
from jax.sharding import PartitionSpec as P

LEN, CROSS, CELLS, TILES = 16, 48, 2304, 18
SEGS, CHAIN = 8, 32
time_step = 0.05
viscosity = 0.2
compress = 1.0
SIGN = (-1.0, -1.0, -1.0, 1.0)
VMEM = pl.BlockSpec(memory_space=pltpu.VMEM)
SMEM = pl.BlockSpec(memory_space=pltpu.SMEM)


def lanes_of(rows=8):
    return lax.broadcasted_iota(jnp.int32, (rows, 128), 1)


def gather_lanes(values, index):
    parts = [
        jnp.take_along_axis(values[r : r + 8], index, axis=1, mode="promise_in_bounds")
        for r in range(0, values.shape[0], 8)
    ]
    return parts[0] if len(parts) == 1 else jnp.concatenate(parts, axis=0)


def reversed_rows(values):
    index = 7 - lax.broadcasted_iota(jnp.int32, (8, 128), 0)
    flip = lambda part: jnp.take_along_axis(part, index, axis=0, mode="promise_in_bounds")
    return jnp.concatenate([flip(values[8:16]), flip(values[0:8])], axis=0)


def joined_face(device, block_map, links):
    block = block_map[device]
    face, partner, along, across = jnp.int32(0), jnp.int32(-1), jnp.int32(0), jnp.int32(0)
    for side in range(2, 6):
        other = links[side, 0, block]
        here = other >= 0
        face = jnp.where(here, side, face)
        partner = jnp.where(here, other, partner)
        along = jnp.where(here, links[side, 2, block], along)
        across = jnp.where(here, links[side, 3, block], across)
    position = lax.rem(device, CHAIN)
    segment = jnp.int32(0)
    for s in range(SEGS):
        segment = jnp.where(block_map[s * CHAIN + position] == partner, s, segment)
    return face, segment, along, across


def face_source(face, across, first_layer):
    lane = lanes_of()
    layer = jnp.where(lane >= CROSS, 1, 0)
    place = lane - layer * CROSS
    place = jnp.where(across == 1, CROSS - 1 - place, place)
    depth = first_layer + layer
    depth = jnp.where((face == 3) | (face == 5), CROSS - 1 - depth, depth)
    return jnp.where(face <= 3, depth * CROSS + place, place * CROSS + depth)


def extract_faces(load, names, source, store, along):
    for name in names:
        found = jnp.zeros((LEN, 128), jnp.float32)
        for t in range(TILES):
            local = source - 128 * t
            inside = (local >= 0) & (local < 128)
            local = jnp.clip(local, 0, 127)
            tile = load(name, t)
            picked = gather_lanes(tile, local)
            found = jnp.where(jnp.concatenate([inside, inside], axis=0), picked, found)
        found = jnp.where(along == 1, reversed_rows(found), found)
        store(name, found)


def write_joint(load, joint_ref, face, along, across):
    def store(c, values):
        joint_ref[16 * c : 16 * c + 16, :] = values

    extract_faces(load, range(4), face_source(face, across, 0), store, along)


def write_chain(field, even_ref, odd_ref, position):
    even = lax.rem(position, 2) == 0
    for c in range(4):
        low, high = field[c, 0:2, :], field[c, LEN - 2 : LEN, :]
        even_ref[2 * c : 2 * c + 2, :] = jnp.where(even, high, low)
        odd_ref[2 * c : 2 * c + 2, :] = jnp.where(even, low, high)


def first_kernel(q, block_map, links, joint_ref, even_ref, odd_ref, meta):
    segment, position = lax.axis_index("seg"), lax.axis_index("blk")
    face, partner, along, across = joined_face(segment * CHAIN + position, block_map, links)
    mate = (segment + 4) % 8
    _, mate_partner, _, _ = joined_face(mate * CHAIN + position, block_map, links)
    meta[0] = face
    meta[1] = along
    meta[2] = across
    meta[3] = jnp.where(partner // 4 == segment // 4, (partner ^ segment) & 3, 0)
    meta[4] = (mate_partner ^ segment) & 3
    block = block_map[segment * CHAIN + position]
    meta[5] = jnp.where(links[0, 0, block] >= 0, 1, 0)
    meta[6] = jnp.where(links[1, 0, block] >= 0, 1, 0)
    meta[7] = position
    write_joint(lambda c, t: q[c, :, 128 * t : 128 * t + 128], joint_ref, face, along, across)
    write_chain(q, even_ref, odd_ref, position)


def pick_kernel(own, one, two, three, meta, out):
    choice = meta[4]
    for n, ref in enumerate((own, one, two, three)):

        @pl.when(choice == n)
        def _(ref=ref):
            out[...] = ref[...]


def shifted_lanes(before, here, after, shift):
    lane = lanes_of(LEN)
    if shift > 0:
        return jnp.where(
            lane < 128 - shift, pltpu.roll(here, 128 - shift, 1), pltpu.roll(after, 128 - shift, 1)
        )
    return jnp.where(lane >= -shift, pltpu.roll(here, -shift, 1), pltpu.roll(before, -shift, 1))


def shifted_rows(padded, shift):
    return pltpu.roll(padded, (-shift) % 32, 0)[8:24]


def differences(m2, m1, here, p1, p2):
    return 8.0 * (p1 - m1) - (p2 - m2)


def bends(m2, m1, here, p1, p2):
    return 16.0 * (p1 + m1) - (p2 + m2) - 30.0 * here


def advance(stencils, geometry):
    here = [stencils[c][0][2] for c in range(4)]
    moves = [-(time_step / 12.0) * geometry[n] for n in range(9)]
    result = list(here)
    fall = None
    for a in range(3):
        g = geometry[3 * a : 3 * a + 3]
        n = moves[3 * a : 3 * a + 3]
        speed = n[0] * here[0] + n[1] * here[1] + n[2] * here[2]
        spread = (viscosity * time_step / 12.0) * (g[0] * g[0] + g[1] * g[1] + g[2] * g[2])
        drop = differences(*stencils[3][a])
        for b in range(3):
            slope = differences(*stencils[b][a])
            result[b] = result[b] + speed * slope + n[b] * drop + spread * bends(*stencils[b][a])
            term = n[b] * slope
            fall = term if fall is None else fall + term
    result[3] = result[3] + compress * fall
    return result


def section(q, metric, joint, low, high, face, store):
    lane = lanes_of(LEN)
    load = lambda c, t: q[c, :, 128 * t : 128 * t + 128]
    before_first, after_last, ghosts = [], [], []
    for c in range(4):
        received = joint(c)
        ghosts.append(received)
        source = jnp.where(face == 2, received, SIGN[c] * load(c, 0))
        before_first.append(jnp.where(lane >= 80, pltpu.roll(source, 80, 1), pltpu.roll(source, 112, 1)))
        last = SIGN[c] * load(c, TILES - 1)
        wall = jnp.where(lane < CROSS, pltpu.roll(last, 48, 1), pltpu.roll(last, 16, 1))
        after_last.append(jnp.where(face == 3, received, wall))

    def tile(c, t):
        return before_first[c] if t < 0 else after_last[c] if t >= TILES else load(c, t)

    for t in range(TILES):
        flat = 128 * t + lane
        j = flat // CROSS
        k = flat - j * CROSS
        joined = ((face == 4) & (k < 2)) | ((face == 5) & (k >= 46))
        near = j[:8]
        far = jnp.where((k == 0) | (k == 47), j + CROSS, j)[:8]
        stencils = []
        for c in range(4):
            before, here, after = tile(c, t - 1), tile(c, t), tile(c, t + 1)
            rows = jnp.concatenate([low(c, t), here, high(c, t)], axis=0)
            along_i = [shifted_rows(rows, s) for s in (-2, -1)] + [here] + [shifted_rows(rows, s) for s in (1, 2)]
            along_j = [shifted_lanes(before, here, after, CROSS * s) if s else here for s in range(-2, 3)]
            raw = [shifted_lanes(before, here, after, s) if s else here for s in range(-2, 3)]
            first = jnp.where(joined, gather_lanes(ghosts[c], near), SIGN[c] * here)
            wall = SIGN[c] * jnp.where((k == 0) | (k == 46), raw[3], raw[1])
            second = jnp.where(joined, gather_lanes(ghosts[c], far), wall)
            along_k = [
                jnp.where(k < 2, second, raw[0]),
                jnp.where(k == 0, first, raw[1]),
                here,
                jnp.where(k == 47, first, raw[3]),
                jnp.where(k >= 46, second, raw[4]),
            ]
            stencils.append((along_i, along_j, along_k))
        store(t, advance(stencils, [metric[n, :, 128 * t : 128 * t + 128] for n in range(9)]))


def chain_ghosts(q, even_ref, odd_ref, low_ref, high_ref, meta):
    even = lax.rem(meta[7], 2) == 0
    has_low, has_high = meta[5] == 1, meta[6] == 1
    for c in range(4):
        rows = slice(2 * c, 2 * c + 2)
        from_even, from_odd = even_ref[rows, :], odd_ref[rows, :]
        mirror = -SIGN[c]
        low_ref[c, 6:8, :] = jnp.where(even, from_odd, from_even)
        high_ref[c, 0:2, :] = jnp.where(even, from_even, from_odd)

        @pl.when(jnp.logical_not(has_low))
        def _():
            low_ref[c, 7:8, :] = mirror * q[c, 0:1, :]
            low_ref[c, 6:7, :] = mirror * q[c, 1:2, :]

        @pl.when(jnp.logical_not(has_high))
        def _():
            high_ref[c, 0:1, :] = mirror * q[c, LEN - 1 : LEN, :]
            high_ref[c, 1:2, :] = mirror * q[c, LEN - 2 : LEN - 1, :]


def section_kernel(last, q, first, metric, one, two, three, mate, even_in, odd_in, meta, *rest):
    if last:
        out, low_ref, high_ref, ghost_ref = rest
    else:
        out, joint_ref, even_ref, odd_ref, low_ref, high_ref, ghost_ref = rest
    choice = meta[3]
    for n, ref in enumerate((mate, one, two, three)):

        @pl.when(choice == n)
        def _(ref=ref):
            ghost_ref[...] = ref[...]

    face = meta[0]
    chain_ghosts(q, even_in, odd_in, low_ref, high_ref, meta)

    def store(t, values):
        where = slice(128 * t, 128 * t + 128)
        for c in range(4):
            out[c, :, where] = 0.5 * first[c, :, where] + 0.5 * values[c] if last else values[c]

    tile = lambda ref: lambda c, t: ref[c, :, 128 * t : 128 * t + 128]
    section(q, metric, lambda c: ghost_ref[16 * c : 16 * c + 16, :], tile(low_ref), tile(high_ref), face, store)
    if not last:
        write_joint(lambda c, t: out[c, :, 128 * t : 128 * t + 128], joint_ref, face, meta[1], meta[2])
        write_chain(out, even_ref, odd_ref, meta[7])


f32 = functools.partial(jax.ShapeDtypeStruct, dtype=jnp.float32)
PARAMS = pltpu.CompilerParams(vmem_limit_bytes=48 * 1024 * 1024)


def exchange(joint, even, odd, meta):
    one, two, three = (
        lax.ppermute(joint, "seg", [(i, i ^ s) for i in range(SEGS)]) for s in (1, 2, 3)
    )
    from_even = lax.ppermute(even, "blk", [(i, i ^ 1) for i in range(CHAIN)])
    pairs = [(i, i + 1) for i in range(1, CHAIN - 1, 2)]
    from_odd = lax.ppermute(odd, "blk", pairs + [(b, a) for a, b in pairs])
    picked = pl.pallas_call(
        pick_kernel,
        out_shape=f32(joint.shape),
        in_specs=[VMEM] * 4 + [SMEM],
        out_specs=VMEM,
        compiler_params=PARAMS,
    )(joint, one, two, three, meta)
    mate = lax.ppermute(picked, "seg", [(i, i ^ 4) for i in range(SEGS)])
    return one, two, three, mate, from_even, from_odd


def on_device(state, metric, block_map, links):
    q = state.reshape(4, LEN, CELLS)
    geometry = metric.reshape(9, LEN, CELLS)
    links = jnp.transpose(links, (1, 2, 0))
    messages = [f32((64, 128)), f32((8, CELLS)), f32((8, CELLS))]
    joint, even, odd, meta = pl.pallas_call(
        first_kernel,
        out_shape=messages + [jax.ShapeDtypeStruct((8,), jnp.int32)],
        in_specs=[VMEM, SMEM, SMEM],
        out_specs=[VMEM] * 3 + [SMEM],
        compiler_params=PARAMS,
    )(q, block_map, links)
    scratch = [
        pltpu.VMEM((4, 8, CELLS), jnp.float32),
        pltpu.VMEM((4, 8, CELLS), jnp.float32),
        pltpu.VMEM((64, 128), jnp.float32),
    ]
    received = exchange(joint, even, odd, meta)
    q1, joint, even, odd = pl.pallas_call(
        functools.partial(section_kernel, False),
        out_shape=[f32((4, LEN, CELLS))] + messages,
        in_specs=[VMEM] * 9 + [SMEM],
        out_specs=[VMEM] * 4,
        scratch_shapes=scratch,
        compiler_params=PARAMS,
    )(q, q, geometry, *received, meta)
    received = exchange(joint, even, odd, meta)
    advanced = pl.pallas_call(
        functools.partial(section_kernel, True),
        out_shape=f32((4, LEN, CELLS)),
        in_specs=[VMEM] * 9 + [SMEM],
        out_specs=VMEM,
        scratch_shapes=scratch,
        compiler_params=PARAMS,
    )(q1, q, geometry, *received, meta)
    return advanced.reshape(state.shape)


def solution(mesh):
    in_specs = (P(("seg", "blk"), None, None, None), P(("seg", "blk"), None, None, None), P(), P())
    out_specs = P(("seg", "blk"), None, None, None)
    return jax.shard_map(
        on_device, mesh=mesh, in_specs=in_specs, out_specs=out_specs, check_vma=False
    )
```

```python
import functools
import jax
import jax.numpy as jnp
from jax import lax
from jax.experimental import pallas as pl
from jax.experimental.pallas import tpu as pltpu
from jax.sharding import PartitionSpec as P

LEN, CROSS, CELLS, TILES = 16, 48, 2304, 18
HALF = 9
SEGS, CHAIN = 8, 32
time_step = 0.05
viscosity = 0.2
compress = 1.0
SIGN = (-1.0, -1.0, -1.0, 1.0)
VMEM = pl.BlockSpec(memory_space=pltpu.VMEM)
SMEM = pl.BlockSpec(memory_space=pltpu.SMEM)


def lanes_of(rows=8):
    return lax.broadcasted_iota(jnp.int32, (rows, 128), 1)


def gather_lanes(values, index):
    parts = [
        jnp.take_along_axis(values[r : r + 8], index, axis=1, mode="promise_in_bounds")
        for r in range(0, values.shape[0], 8)
    ]
    return parts[0] if len(parts) == 1 else jnp.concatenate(parts, axis=0)


def reversed_rows(values):
    index = 7 - lax.broadcasted_iota(jnp.int32, (8, 128), 0)
    flip = lambda part: jnp.take_along_axis(part, index, axis=0, mode="promise_in_bounds")
    return jnp.concatenate([flip(values[8:16]), flip(values[0:8])], axis=0)


def joined_face(device, block_map, links):
    block = block_map[device]
    face, partner, along, across = jnp.int32(0), jnp.int32(-1), jnp.int32(0), jnp.int32(0)
    for side in range(2, 6):
        other = links[side, 0, block]
        here = other >= 0
        face = jnp.where(here, side, face)
        partner = jnp.where(here, other, partner)
        along = jnp.where(here, links[side, 2, block], along)
        across = jnp.where(here, links[side, 3, block], across)
    position = lax.rem(device, CHAIN)
    segment = jnp.int32(0)
    for s in range(SEGS):
        segment = jnp.where(block_map[s * CHAIN + position] == partner, s, segment)
    return face, segment, along, across


def face_source(face, across, first_layer):
    lane = lanes_of()
    layer = jnp.where(lane >= CROSS, 1, 0)
    place = lane - layer * CROSS
    place = jnp.where(across == 1, CROSS - 1 - place, place)
    depth = first_layer + layer
    depth = jnp.where((face == 3) | (face == 5), CROSS - 1 - depth, depth)
    return jnp.where(face <= 3, depth * CROSS + place, place * CROSS + depth)


def extract_faces(load, names, source, store, along):
    for name in names:
        found = jnp.zeros((LEN, 128), jnp.float32)
        for t in range(TILES):
            local = source - 128 * t
            inside = (local >= 0) & (local < 128)
            local = jnp.clip(local, 0, 127)
            tile = load(name, t)
            picked = gather_lanes(tile, local)
            found = jnp.where(jnp.concatenate([inside, inside], axis=0), picked, found)
        found = jnp.where(along == 1, reversed_rows(found), found)
        store(name, found)


def write_joint(load, joint_ref, face, along, across):
    def store(c, values):
        joint_ref[16 * c : 16 * c + 16, :] = values

    extract_faces(load, range(4), face_source(face, across, 0), store, along)


def write_chain(field, even_ref, odd_ref, position):
    even = lax.rem(position, 2) == 0
    for c in range(4):
        low, high = field[c, 0:2, :], field[c, LEN - 2 : LEN, :]
        even_ref[2 * c : 2 * c + 2, :] = jnp.where(even, high, low)
        odd_ref[2 * c : 2 * c + 2, :] = jnp.where(even, low, high)


def first_kernel(q_hbm, map_hbm, links_hbm, joint_ref, meta, q, block_map, links, sem):
    copies = [
        pltpu.make_async_copy(source, target, sem.at[n])
        for n, (source, target) in enumerate(
            ((links_hbm, links), (map_hbm, block_map), (q_hbm, q))
        )
    ]
    for copy in copies:
        copy.start()
    segment, position = lax.axis_index("seg"), lax.axis_index("blk")
    copies[0].wait()
    copies[1].wait()
    face, partner, along, across = joined_face(segment * CHAIN + position, block_map, links)
    mate = (segment + 4) % 8
    _, mate_partner, _, _ = joined_face(mate * CHAIN + position, block_map, links)
    meta[0] = face
    meta[1] = along
    meta[2] = across
    meta[3] = jnp.where(partner // 4 == segment // 4, (partner ^ segment) & 3, 0)
    meta[4] = (mate_partner ^ segment) & 3
    block = block_map[segment * CHAIN + position]
    meta[5] = jnp.where(links[0, 0, block] >= 0, 1, 0)
    meta[6] = jnp.where(links[1, 0, block] >= 0, 1, 0)
    meta[7] = position
    copies[2].wait()
    write_joint(lambda c, t: q[c, :, 128 * t : 128 * t + 128], joint_ref, face, along, across)


def pick_kernel(own, one, two, three, meta, out):
    choice = meta[4]
    for n, ref in enumerate((own, one, two, three)):

        @pl.when(choice == n)
        def _(ref=ref):
            out[...] = ref[...]


def shifted_lanes(before, here, after, shift):
    lane = lanes_of(LEN)
    if shift > 0:
        return jnp.where(
            lane < 128 - shift, pltpu.roll(here, 128 - shift, 1), pltpu.roll(after, 128 - shift, 1)
        )
    return jnp.where(lane >= -shift, pltpu.roll(here, -shift, 1), pltpu.roll(before, -shift, 1))


def shifted_rows(padded, shift):
    return pltpu.roll(padded, (-shift) % 32, 0)[8:24]


def differences(m2, m1, here, p1, p2):
    return 8.0 * (p1 - m1) - (p2 - m2)


def bends(m2, m1, here, p1, p2):
    return 16.0 * (p1 + m1) - (p2 + m2) - 30.0 * here


def advance(stencils, geometry):
    here = [stencils[c][0][2] for c in range(4)]
    moves = [-(time_step / 12.0) * geometry[n] for n in range(9)]
    result = list(here)
    fall = None
    for a in range(3):
        g = geometry[3 * a : 3 * a + 3]
        n = moves[3 * a : 3 * a + 3]
        speed = n[0] * here[0] + n[1] * here[1] + n[2] * here[2]
        spread = (viscosity * time_step / 12.0) * (g[0] * g[0] + g[1] * g[1] + g[2] * g[2])
        drop = differences(*stencils[3][a])
        for b in range(3):
            slope = differences(*stencils[b][a])
            result[b] = result[b] + speed * slope + n[b] * drop + spread * bends(*stencils[b][a])
            term = n[b] * slope
            fall = term if fall is None else fall + term
    result[3] = result[3] + compress * fall
    return result


def bulk_kernel(last, tiles, q, metric, *rest):
    first, rest = (rest[0], rest[1:]) if last else (None, rest)
    meta, out = rest[:2]
    if len(rest) == 4:
        write_chain(q, rest[2], rest[3], meta[7])
    lane = lanes_of(LEN)
    row = lax.broadcasted_iota(jnp.int32, (8, 128), 0)
    face, ends = meta[0], (meta[5] == 0, meta[6] == 0)
    load = lambda c, t: q[c, :, 128 * t : 128 * t + 128]
    before_first, after_last = [], []
    for c in range(4):
        head = jnp.where(face == 2, 0.0, SIGN[c]) * load(c, 0)
        before_first.append(jnp.where(lane >= 80, pltpu.roll(head, 80, 1), pltpu.roll(head, 112, 1)))
        tail = jnp.where(face == 3, 0.0, SIGN[c]) * load(c, TILES - 1)
        after_last.append(jnp.where(lane < CROSS, pltpu.roll(tail, 48, 1), pltpu.roll(tail, 16, 1)))

    def tile(c, t):
        return before_first[c] if t < 0 else after_last[c] if t >= TILES else load(c, t)

    low_scale = jnp.where(face == 4, 0.0, 1.0)
    high_scale = jnp.where(face == 5, 0.0, 1.0)
    open_low = jnp.where(ends[0], 1.0, 0.0)
    open_high = jnp.where(ends[1], 1.0, 0.0)
    for t in tiles:
        flat = 128 * t + lane
        k = flat - (flat // CROSS) * CROSS
        scale = jnp.where(k < 2, low_scale, high_scale)
        stencils = []
        for c in range(4):
            before, here, after = tile(c, t - 1), tile(c, t), tile(c, t + 1)
            top, bottom = here[0:8], here[8:16]
            low = -SIGN[c] * open_low * jnp.where(row == 7, pltpu.roll(top, 7, 0), pltpu.roll(top, 5, 0))
            high = -SIGN[c] * open_high * jnp.where(row == 0, pltpu.roll(bottom, 1, 0), pltpu.roll(bottom, 3, 0))
            rows = jnp.concatenate([low, here, high], axis=0)
            along_i = [shifted_rows(rows, s) for s in (-2, -1)] + [here] + [shifted_rows(rows, s) for s in (1, 2)]
            along_j = [shifted_lanes(before, here, after, CROSS * s) if s else here for s in range(-2, 3)]
            raw = [shifted_lanes(before, here, after, s) if s else here for s in range(-2, 3)]
            factor = SIGN[c] * scale
            nearest = factor * here
            second = factor * jnp.where((k == 0) | (k == 46), raw[3], raw[1])
            along_k = [
                jnp.where(k < 2, second, raw[0]),
                jnp.where(k == 0, nearest, raw[1]),
                here,
                jnp.where(k == 47, nearest, raw[3]),
                jnp.where(k >= 46, second, raw[4]),
            ]
            stencils.append((along_i, along_j, along_k))
        where = slice(128 * t, 128 * t + 128)
        values = advance(stencils, [metric[n, :, where] for n in range(9)])
        for c in range(4):
            kept = 0.5 * first[c, :, where] + 0.5 * values[c] if last else values[c]
            out[c, :, 128 * (t - tiles[0]) : 128 * (t - tiles[0]) + 128] = kept


def edge_terms(here, geometry, slopes, curves, scale):
    moves = [-(scale * time_step / 12.0) * g for g in geometry]
    speed = moves[0] * here[0] + moves[1] * here[1] + moves[2] * here[2]
    squares = geometry[0] * geometry[0] + geometry[1] * geometry[1] + geometry[2] * geometry[2]
    spread = (scale * viscosity * time_step / 12.0) * squares
    added = [speed * slopes[b] + moves[b] * slopes[3] + spread * curves[b] for b in range(3)]
    added.append(compress * (moves[0] * slopes[0] + moves[1] * slopes[1] + moves[2] * slopes[2]))
    return added


def edge_kernel(last, left, right, q, metric, one, two, three, mate, even_in, odd_in, meta, *rest):
    if last:
        out, low_ref, high_ref, ghost_ref = rest
    else:
        out, joint_ref, low_ref, high_ref, ghost_ref = rest
    scale = 0.5 if last else 1.0
    choice = meta[3]
    for n, ref in enumerate((mate, one, two, three)):

        @pl.when(choice == n)
        def _(ref=ref):
            ghost_ref[...] = ref[...]

    face = meta[0]
    even = lax.rem(meta[7], 2) == 0
    has_low = jnp.where(meta[5] == 1, 1.0, 0.0)
    has_high = jnp.where(meta[6] == 1, 1.0, 0.0)
    for c in range(4):
        rows = slice(2 * c, 2 * c + 2)
        from_even, from_odd = even_in[rows, :], odd_in[rows, :]
        low_ref[c, 0:2, :] = has_low * jnp.where(even, from_odd, from_even)
        high_ref[c, 6:8, :] = has_high * jnp.where(even, from_even, from_odd)

    row = lax.broadcasted_iota(jnp.int32, (8, 128), 0)
    for t in range(TILES):
        where = slice(128 * t, 128 * t + 128)
        part, place = (left, where) if t < HALF else (right, slice(128 * (t - HALF), 128 * (t - HALF) + 128))
        for high in (False, True):
            half = slice(8, 16) if high else slice(0, 8)
            slopes, curves = [], []
            for c in range(4):
                if high:
                    ghost = high_ref[c, :, where]
                    first = jnp.where(row == 7, pltpu.roll(ghost, 1, 0), 0.0)
                    second = jnp.where(row >= 6, ghost, 0.0)
                    slopes.append(8.0 * first - second)
                else:
                    ghost = low_ref[c, :, where]
                    first = jnp.where(row == 0, pltpu.roll(ghost, 7, 0), 0.0)
                    second = jnp.where(row < 2, ghost, 0.0)
                    slopes.append(second - 8.0 * first)
                curves.append(16.0 * first - second)
            here = [q[c, half, where] for c in range(4)]
            added = edge_terms(here, [metric[n, half, where] for n in range(3)], slopes, curves, scale)
            for c in range(4):
                out[c, half, where] = part[c, half, place] + added[c]

    lane = lanes_of(LEN)

    def add(t, direction, slopes, curves):
        where = slice(128 * t, 128 * t + 128)
        here = [q[c, :, where] for c in range(4)]
        geometry = [metric[3 * direction + n, :, where] for n in range(3)]
        added = edge_terms(here, geometry, slopes, curves, scale)
        for c in range(4):
            out[c, :, where] = out[c, :, where] + added[c]

    ghost_of = lambda c: ghost_ref[16 * c : 16 * c + 16, :]

    @pl.when(face == 2)
    def _():
        slopes, curves = [], []
        for c in range(4):
            ghost = ghost_of(c)
            first = jnp.where(lane < CROSS, ghost, 0.0)
            second = jnp.where(lane < CROSS, pltpu.roll(ghost, 80, 1), pltpu.roll(ghost, 48, 1))
            second = jnp.where(lane < 2 * CROSS, second, 0.0)
            slopes.append(second - 8.0 * first)
            curves.append(16.0 * first - second)
        add(0, 1, slopes, curves)

    @pl.when(face == 3)
    def _():
        slopes, curves = [], []
        for c in range(4):
            ghost = ghost_of(c)
            first = jnp.where(lane >= 80, pltpu.roll(ghost, 80, 1), 0.0)
            second = jnp.where(lane >= 32, pltpu.roll(ghost, 32, 1), 0.0)
            slopes.append(8.0 * first - second)
            curves.append(16.0 * first - second)
        add(TILES - 1, 1, slopes, curves)

    @pl.when(face >= 4)
    def _():
        toward = jnp.where(face == 4, -1.0, 1.0)
        for t in range(TILES):
            flat = 128 * t + lane
            j = flat // CROSS
            k = flat - j * CROSS
            depth = jnp.where(face == 4, k, CROSS - 1 - k)
            far = jnp.where(depth == 0, j + CROSS, j)[:8]
            slopes, curves = [], []
            for c in range(4):
                ghost = ghost_of(c)
                first = jnp.where(depth == 0, gather_lanes(ghost, j[:8]), 0.0)
                second = jnp.where(depth < 2, gather_lanes(ghost, far), 0.0)
                slopes.append(toward * (8.0 * first - second))
                curves.append(16.0 * first - second)
            add(t, 2, slopes, curves)

    if not last:
        write_joint(lambda c, t: out[c, :, 128 * t : 128 * t + 128], joint_ref, face, meta[1], meta[2])


f32 = functools.partial(jax.ShapeDtypeStruct, dtype=jnp.float32)
PARAMS = pltpu.CompilerParams(vmem_limit_bytes=24 * 1024 * 1024)
WHOLE = pltpu.CompilerParams(vmem_limit_bytes=61 * 1024 * 1024)
FIELD = f32((4, LEN, CELLS))
JOINT = f32((64, 128))
CHAINS = [f32((8, CELLS))] * 2
HALO = [pltpu.VMEM((4, 8, CELLS), jnp.float32)] * 2 + [pltpu.VMEM((64, 128), jnp.float32)]


def bulk(last, tiles, *operands):
    shapes = [f32((4, LEN, 128 * len(tiles)))] + (CHAINS if tiles[0] == 0 else [])
    return pl.pallas_call(
        functools.partial(bulk_kernel, last, tiles),
        out_shape=shapes,
        in_specs=[VMEM] * (len(operands) - 1) + [SMEM],
        out_specs=[VMEM] * len(shapes),
        compiler_params=PARAMS,
        cost_estimate=pl.CostEstimate(flops=6_000_000, bytes_accessed=6_000_000, transcendentals=0),
    )(*operands)


def edges(last, *operands):
    shapes = [FIELD] + ([] if last else [JOINT])
    return pl.pallas_call(
        functools.partial(edge_kernel, last),
        out_shape=shapes,
        in_specs=[VMEM] * (len(operands) - 1) + [SMEM],
        out_specs=[VMEM] * len(shapes),
        scratch_shapes=HALO,
        compiler_params=PARAMS,
    )(*operands)


def section(last, q, geometry, joint, first, meta):
    kept = [first] if last else []
    one, two, three = (
        lax.ppermute(joint, "seg", [(i, i ^ s) for i in range(SEGS)]) for s in (1, 2, 3)
    )
    left, even, odd = bulk(last, range(HALF), q, geometry, *kept, meta)
    one, two, three, even, odd = lax.optimization_barrier((one, two, three, even, odd))
    from_even = lax.ppermute(even, "blk", [(i, i ^ 1) for i in range(CHAIN)])
    pairs = [(i, i + 1) for i in range(1, CHAIN - 1, 2)]
    from_odd = lax.ppermute(odd, "blk", pairs + [(b, a) for a, b in pairs])
    picked = pl.pallas_call(
        pick_kernel,
        out_shape=JOINT,
        in_specs=[VMEM] * 4 + [SMEM],
        out_specs=VMEM,
        compiler_params=PARAMS,
    )(joint, one, two, three, meta)
    mate = lax.ppermute(picked, "seg", [(i, i ^ 4) for i in range(SEGS)])
    (right,) = bulk(last, range(HALF, TILES), q, geometry, *kept, meta)
    return edges(last, left, right, q, geometry, one, two, three, mate, from_even, from_odd, meta)


def on_device(state, metric, block_map, links):
    HBM = pl.BlockSpec(memory_space=pltpu.HBM)
    q, geometry = state.reshape(4, LEN, CELLS), metric.reshape(9, LEN, CELLS)
    joint, meta = pl.pallas_call(
        first_kernel,
        out_shape=[JOINT, jax.ShapeDtypeStruct((8,), jnp.int32)],
        in_specs=[HBM] * 3,
        out_specs=[VMEM, SMEM],
        scratch_shapes=[
            pltpu.VMEM((4, LEN, CELLS), jnp.float32),
            pltpu.SMEM((SEGS * CHAIN,), jnp.int32),
            pltpu.SMEM((6, 4, SEGS * CHAIN), jnp.int32),
            pltpu.SemaphoreType.DMA((3,)),
        ],
        compiler_params=WHOLE,
    )(q, block_map, jnp.transpose(links, (1, 2, 0)))
    q1, joint = section(False, q, geometry, joint, None, meta)
    (advanced,) = section(True, q1, geometry, joint, q, meta)
    return advanced.reshape(state.shape)


def solution(mesh):
    in_specs = (P(("seg", "blk"), None, None, None), P(("seg", "blk"), None, None, None), P(), P())
    out_specs = P(("seg", "blk"), None, None, None)
    return jax.shard_map(
        on_device, mesh=mesh, in_specs=in_specs, out_specs=out_specs, check_vma=False
    )
```

```python
import functools
import jax
import jax.numpy as jnp
from jax import lax
from jax.experimental import pallas as pl
from jax.experimental.pallas import tpu as pltpu
from jax.sharding import PartitionSpec as P

LEN, CROSS, CELLS, TILES = 16, 48, 2304, 18
HALF = 9
SEGS, CHAIN = 8, 32
time_step = 0.05
viscosity = 0.2
compress = 1.0
SIGN = (-1.0, -1.0, -1.0, 1.0)
VMEM = pl.BlockSpec(memory_space=pltpu.VMEM)
SMEM = pl.BlockSpec(memory_space=pltpu.SMEM)


def lanes_of(rows=8):
    return lax.broadcasted_iota(jnp.int32, (rows, 128), 1)


def gather_lanes(values, index):
    parts = [
        jnp.take_along_axis(values[r : r + 8], index, axis=1, mode="promise_in_bounds")
        for r in range(0, values.shape[0], 8)
    ]
    return parts[0] if len(parts) == 1 else jnp.concatenate(parts, axis=0)


def reversed_rows(values):
    index = 7 - lax.broadcasted_iota(jnp.int32, (8, 128), 0)
    flip = lambda part: jnp.take_along_axis(part, index, axis=0, mode="promise_in_bounds")
    return jnp.concatenate([flip(values[8:16]), flip(values[0:8])], axis=0)


def joined_face(device, block_map, links):
    block = block_map[device]
    face, partner, along, across = jnp.int32(0), jnp.int32(-1), jnp.int32(0), jnp.int32(0)
    for side in range(2, 6):
        other = links[side, 0, block]
        here = other >= 0
        face = jnp.where(here, side, face)
        partner = jnp.where(here, other, partner)
        along = jnp.where(here, links[side, 2, block], along)
        across = jnp.where(here, links[side, 3, block], across)
    position = lax.rem(device, CHAIN)
    segment = jnp.int32(0)
    for s in range(SEGS):
        segment = jnp.where(block_map[s * CHAIN + position] == partner, s, segment)
    return face, segment, along, across


def face_source(face, across, first_layer):
    lane = lanes_of()
    layer = jnp.where(lane >= CROSS, 1, 0)
    place = lane - layer * CROSS
    place = jnp.where(across == 1, CROSS - 1 - place, place)
    depth = first_layer + layer
    depth = jnp.where((face == 3) | (face == 5), CROSS - 1 - depth, depth)
    return jnp.where(face <= 3, depth * CROSS + place, place * CROSS + depth)


def extract_faces(load, names, source, store, along):
    for name in names:
        found = jnp.zeros((LEN, 128), jnp.float32)
        for t in range(TILES):
            local = source - 128 * t
            inside = (local >= 0) & (local < 128)
            local = jnp.clip(local, 0, 127)
            tile = load(name, t)
            picked = gather_lanes(tile, local)
            found = jnp.where(jnp.concatenate([inside, inside], axis=0), picked, found)
        found = jnp.where(along == 1, reversed_rows(found), found)
        store(name, found)


def write_joint(load, joint_ref, face, along, across):
    def store(c, values):
        joint_ref[16 * c : 16 * c + 16, :] = values

    extract_faces(load, range(4), face_source(face, across, 0), store, along)


def write_chain(field, even_ref, odd_ref, position):
    even = lax.rem(position, 2) == 0
    for c in range(4):
        low, high = field[c, 0:2, :], field[c, LEN - 2 : LEN, :]
        even_ref[2 * c : 2 * c + 2, :] = jnp.where(even, high, low)
        odd_ref[2 * c : 2 * c + 2, :] = jnp.where(even, low, high)


def first_kernel(q_hbm, metric_hbm, map_hbm, links_hbm, q, metric, joint_ref, meta, block_map, links, sem):
    copies = [
        pltpu.make_async_copy(source, target, sem.at[n])
        for n, (source, target) in enumerate(
            ((links_hbm, links), (map_hbm, block_map), (q_hbm, q), (metric_hbm, metric))
        )
    ]
    for copy in copies:
        copy.start()
    segment, position = lax.axis_index("seg"), lax.axis_index("blk")
    copies[0].wait()
    copies[1].wait()
    face, partner, along, across = joined_face(segment * CHAIN + position, block_map, links)
    mate = (segment + 4) % 8
    _, mate_partner, _, _ = joined_face(mate * CHAIN + position, block_map, links)
    meta[0] = face
    meta[1] = along
    meta[2] = across
    meta[3] = jnp.where(partner // 4 == segment // 4, (partner ^ segment) & 3, 0)
    meta[4] = (mate_partner ^ segment) & 3
    block = block_map[segment * CHAIN + position]
    meta[5] = jnp.where(links[0, 0, block] >= 0, 1, 0)
    meta[6] = jnp.where(links[1, 0, block] >= 0, 1, 0)
    meta[7] = position
    copies[2].wait()
    write_joint(lambda c, t: q[c, :, 128 * t : 128 * t + 128], joint_ref, face, along, across)
    copies[3].wait()


def pick_kernel(own, one, two, three, meta, out):
    choice = meta[4]
    for n, ref in enumerate((own, one, two, three)):

        @pl.when(choice == n)
        def _(ref=ref):
            out[...] = ref[...]


def shifted_lanes(before, here, after, shift):
    lane = lanes_of(LEN)
    if shift > 0:
        return jnp.where(
            lane < 128 - shift, pltpu.roll(here, 128 - shift, 1), pltpu.roll(after, 128 - shift, 1)
        )
    return jnp.where(lane >= -shift, pltpu.roll(here, -shift, 1), pltpu.roll(before, -shift, 1))


def shifted_rows(padded, shift):
    return pltpu.roll(padded, (-shift) % 32, 0)[8:24]


def differences(m2, m1, here, p1, p2):
    return 8.0 * (p1 - m1) - (p2 - m2)


def bends(m2, m1, here, p1, p2):
    return 16.0 * (p1 + m1) - (p2 + m2) - 30.0 * here


def advance(stencils, geometry):
    here = [stencils[c][0][2] for c in range(4)]
    moves = [-(time_step / 12.0) * geometry[n] for n in range(9)]
    result = list(here)
    fall = None
    for a in range(3):
        g = geometry[3 * a : 3 * a + 3]
        n = moves[3 * a : 3 * a + 3]
        speed = n[0] * here[0] + n[1] * here[1] + n[2] * here[2]
        spread = (viscosity * time_step / 12.0) * (g[0] * g[0] + g[1] * g[1] + g[2] * g[2])
        drop = differences(*stencils[3][a])
        for b in range(3):
            slope = differences(*stencils[b][a])
            result[b] = result[b] + speed * slope + n[b] * drop + spread * bends(*stencils[b][a])
            term = n[b] * slope
            fall = term if fall is None else fall + term
    result[3] = result[3] + compress * fall
    return result


def bulk_kernel(last, tiles, q, metric, *rest):
    first, rest = (rest[0], rest[1:]) if last else (None, rest)
    meta, out = rest[:2]
    if len(rest) == 4:
        write_chain(q, rest[2], rest[3], meta[7])
    lane = lanes_of(LEN)
    row = lax.broadcasted_iota(jnp.int32, (8, 128), 0)
    face, ends = meta[0], (meta[5] == 0, meta[6] == 0)
    load = lambda c, t: q[c, :, 128 * t : 128 * t + 128]
    before_first, after_last = [], []
    for c in range(4):
        head = jnp.where(face == 2, 0.0, SIGN[c]) * load(c, 0)
        before_first.append(jnp.where(lane >= 80, pltpu.roll(head, 80, 1), pltpu.roll(head, 112, 1)))
        tail = jnp.where(face == 3, 0.0, SIGN[c]) * load(c, TILES - 1)
        after_last.append(jnp.where(lane < CROSS, pltpu.roll(tail, 48, 1), pltpu.roll(tail, 16, 1)))

    def tile(c, t):
        return before_first[c] if t < 0 else after_last[c] if t >= TILES else load(c, t)

    low_scale = jnp.where(face == 4, 0.0, 1.0)
    high_scale = jnp.where(face == 5, 0.0, 1.0)
    open_low = jnp.where(ends[0], 1.0, 0.0)
    open_high = jnp.where(ends[1], 1.0, 0.0)
    for t in tiles:
        flat = 128 * t + lane
        k = flat - (flat // CROSS) * CROSS
        scale = jnp.where(k < 2, low_scale, high_scale)
        stencils = []
        for c in range(4):
            before, here, after = tile(c, t - 1), tile(c, t), tile(c, t + 1)
            top, bottom = here[0:8], here[8:16]
            low = -SIGN[c] * open_low * jnp.where(row == 7, pltpu.roll(top, 7, 0), pltpu.roll(top, 5, 0))
            high = -SIGN[c] * open_high * jnp.where(row == 0, pltpu.roll(bottom, 1, 0), pltpu.roll(bottom, 3, 0))
            rows = jnp.concatenate([low, here, high], axis=0)
            along_i = [shifted_rows(rows, s) for s in (-2, -1)] + [here] + [shifted_rows(rows, s) for s in (1, 2)]
            along_j = [shifted_lanes(before, here, after, CROSS * s) if s else here for s in range(-2, 3)]
            raw = [shifted_lanes(before, here, after, s) if s else here for s in range(-2, 3)]
            factor = SIGN[c] * scale
            nearest = factor * here
            second = factor * jnp.where((k == 0) | (k == 46), raw[3], raw[1])
            along_k = [
                jnp.where(k < 2, second, raw[0]),
                jnp.where(k == 0, nearest, raw[1]),
                here,
                jnp.where(k == 47, nearest, raw[3]),
                jnp.where(k >= 46, second, raw[4]),
            ]
            stencils.append((along_i, along_j, along_k))
        where = slice(128 * t, 128 * t + 128)
        values = advance(stencils, [metric[n, :, where] for n in range(9)])
        for c in range(4):
            kept = 0.5 * first[c, :, where] + 0.5 * values[c] if last else values[c]
            out[c, :, 128 * (t - tiles[0]) : 128 * (t - tiles[0]) + 128] = kept


def edge_terms(here, geometry, slopes, curves, scale):
    moves = [-(scale * time_step / 12.0) * g for g in geometry]
    speed = moves[0] * here[0] + moves[1] * here[1] + moves[2] * here[2]
    squares = geometry[0] * geometry[0] + geometry[1] * geometry[1] + geometry[2] * geometry[2]
    spread = (scale * viscosity * time_step / 12.0) * squares
    added = [speed * slopes[b] + moves[b] * slopes[3] + spread * curves[b] for b in range(3)]
    added.append(compress * (moves[0] * slopes[0] + moves[1] * slopes[1] + moves[2] * slopes[2]))
    return added


def edge_kernel(last, left, right, q, metric, one, two, three, mate, even_in, odd_in, meta, *rest):
    if last:
        out, low_ref, high_ref, ghost_ref = rest
    else:
        out, joint_ref, low_ref, high_ref, ghost_ref = rest
    scale = 0.5 if last else 1.0
    choice = meta[3]
    for n, ref in enumerate((mate, one, two, three)):

        @pl.when(choice == n)
        def _(ref=ref):
            ghost_ref[...] = ref[...]

    face = meta[0]
    even = lax.rem(meta[7], 2) == 0
    has_low = jnp.where(meta[5] == 1, 1.0, 0.0)
    has_high = jnp.where(meta[6] == 1, 1.0, 0.0)
    for c in range(4):
        rows = slice(2 * c, 2 * c + 2)
        from_even, from_odd = even_in[rows, :], odd_in[rows, :]
        low_ref[c, 0:2, :] = has_low * jnp.where(even, from_odd, from_even)
        high_ref[c, 6:8, :] = has_high * jnp.where(even, from_even, from_odd)

    row = lax.broadcasted_iota(jnp.int32, (8, 128), 0)
    for t in range(TILES):
        where = slice(128 * t, 128 * t + 128)
        part, place = (left, where) if t < HALF else (right, slice(128 * (t - HALF), 128 * (t - HALF) + 128))
        for high in (False, True):
            half = slice(8, 16) if high else slice(0, 8)
            slopes, curves = [], []
            for c in range(4):
                if high:
                    ghost = high_ref[c, :, where]
                    first = jnp.where(row == 7, pltpu.roll(ghost, 1, 0), 0.0)
                    second = jnp.where(row >= 6, ghost, 0.0)
                    slopes.append(8.0 * first - second)
                else:
                    ghost = low_ref[c, :, where]
                    first = jnp.where(row == 0, pltpu.roll(ghost, 7, 0), 0.0)
                    second = jnp.where(row < 2, ghost, 0.0)
                    slopes.append(second - 8.0 * first)
                curves.append(16.0 * first - second)
            here = [q[c, half, where] for c in range(4)]
            added = edge_terms(here, [metric[n, half, where] for n in range(3)], slopes, curves, scale)
            for c in range(4):
                out[c, half, where] = part[c, half, place] + added[c]

    lane = lanes_of(LEN)

    def add(t, direction, slopes, curves):
        where = slice(128 * t, 128 * t + 128)
        here = [q[c, :, where] for c in range(4)]
        geometry = [metric[3 * direction + n, :, where] for n in range(3)]
        added = edge_terms(here, geometry, slopes, curves, scale)
        for c in range(4):
            out[c, :, where] = out[c, :, where] + added[c]

    ghost_of = lambda c: ghost_ref[16 * c : 16 * c + 16, :]

    @pl.when(face == 2)
    def _():
        slopes, curves = [], []
        for c in range(4):
            ghost = ghost_of(c)
            first = jnp.where(lane < CROSS, ghost, 0.0)
            second = jnp.where(lane < CROSS, pltpu.roll(ghost, 80, 1), pltpu.roll(ghost, 48, 1))
            second = jnp.where(lane < 2 * CROSS, second, 0.0)
            slopes.append(second - 8.0 * first)
            curves.append(16.0 * first - second)
        add(0, 1, slopes, curves)

    @pl.when(face == 3)
    def _():
        slopes, curves = [], []
        for c in range(4):
            ghost = ghost_of(c)
            first = jnp.where(lane >= 80, pltpu.roll(ghost, 80, 1), 0.0)
            second = jnp.where(lane >= 32, pltpu.roll(ghost, 32, 1), 0.0)
            slopes.append(8.0 * first - second)
            curves.append(16.0 * first - second)
        add(TILES - 1, 1, slopes, curves)

    @pl.when(face >= 4)
    def _():
        toward = jnp.where(face == 4, -1.0, 1.0)
        for t in range(TILES):
            flat = 128 * t + lane
            j = flat // CROSS
            k = flat - j * CROSS
            depth = jnp.where(face == 4, k, CROSS - 1 - k)
            far = jnp.where(depth == 0, j + CROSS, j)[:8]
            slopes, curves = [], []
            for c in range(4):
                ghost = ghost_of(c)
                first = jnp.where(depth == 0, gather_lanes(ghost, j[:8]), 0.0)
                second = jnp.where(depth < 2, gather_lanes(ghost, far), 0.0)
                slopes.append(toward * (8.0 * first - second))
                curves.append(16.0 * first - second)
            add(t, 2, slopes, curves)

    if not last:
        write_joint(lambda c, t: out[c, :, 128 * t : 128 * t + 128], joint_ref, face, meta[1], meta[2])


f32 = functools.partial(jax.ShapeDtypeStruct, dtype=jnp.float32)
PARAMS = pltpu.CompilerParams(vmem_limit_bytes=24 * 1024 * 1024)
WHOLE = pltpu.CompilerParams(vmem_limit_bytes=61 * 1024 * 1024)
FIELD = f32((4, LEN, CELLS))
JOINT = f32((64, 128))
CHAINS = [f32((8, CELLS))] * 2
HALO = [pltpu.VMEM((4, 8, CELLS), jnp.float32)] * 2 + [pltpu.VMEM((64, 128), jnp.float32)]


def bulk(last, tiles, *operands):
    shapes = [f32((4, LEN, 128 * len(tiles)))] + (CHAINS if tiles[0] == 0 else [])
    return pl.pallas_call(
        functools.partial(bulk_kernel, last, tiles),
        out_shape=shapes,
        in_specs=[VMEM] * (len(operands) - 1) + [SMEM],
        out_specs=[VMEM] * len(shapes),
        compiler_params=PARAMS,
        cost_estimate=pl.CostEstimate(flops=6_000_000, bytes_accessed=6_000_000, transcendentals=0),
    )(*operands)


def edges(last, *operands):
    shapes = [FIELD] + ([] if last else [JOINT])
    return pl.pallas_call(
        functools.partial(edge_kernel, last),
        out_shape=shapes,
        in_specs=[VMEM] * (len(operands) - 1) + [SMEM],
        out_specs=[VMEM] * len(shapes),
        scratch_shapes=HALO,
        compiler_params=PARAMS,
    )(*operands)


def section(last, q, geometry, joint, first, meta):
    kept = [first] if last else []
    one, two, three = (
        lax.ppermute(joint, "seg", [(i, i ^ s) for i in range(SEGS)]) for s in (1, 2, 3)
    )
    left, even, odd = bulk(last, range(HALF), q, geometry, *kept, meta)
    one, two, three, even, odd = lax.optimization_barrier((one, two, three, even, odd))
    from_even = lax.ppermute(even, "blk", [(i, i ^ 1) for i in range(CHAIN)])
    pairs = [(i, i + 1) for i in range(1, CHAIN - 1, 2)]
    from_odd = lax.ppermute(odd, "blk", pairs + [(b, a) for a, b in pairs])
    picked = pl.pallas_call(
        pick_kernel,
        out_shape=JOINT,
        in_specs=[VMEM] * 4 + [SMEM],
        out_specs=VMEM,
        compiler_params=PARAMS,
    )(joint, one, two, three, meta)
    mate = lax.ppermute(picked, "seg", [(i, i ^ 4) for i in range(SEGS)])
    (right,) = bulk(last, range(HALF, TILES), q, geometry, *kept, meta)
    return edges(last, left, right, q, geometry, one, two, three, mate, from_even, from_odd, meta)


def on_device(state, metric, block_map, links):
    HBM = pl.BlockSpec(memory_space=pltpu.HBM)
    held = lambda x: pltpu.with_memory_space_constraint(x, pltpu.HBM)
    arrays = (state.reshape(4, LEN, CELLS), metric.reshape(9, LEN, CELLS), block_map, jnp.transpose(links, (1, 2, 0)))
    q, geometry, joint, meta = pl.pallas_call(
        first_kernel,
        out_shape=[FIELD, f32((9, LEN, CELLS)), JOINT, jax.ShapeDtypeStruct((8,), jnp.int32)],
        in_specs=[HBM] * 4,
        out_specs=[VMEM] * 3 + [SMEM],
        scratch_shapes=[
            pltpu.SMEM((SEGS * CHAIN,), jnp.int32),
            pltpu.SMEM((6, 4, SEGS * CHAIN), jnp.int32),
            pltpu.SemaphoreType.DMA((4,)),
        ],
        compiler_params=PARAMS,
    )(*map(held, arrays))
    q1, joint = section(False, q, geometry, joint, None, meta)
    (advanced,) = section(True, q1, geometry, joint, q, meta)
    return advanced.reshape(state.shape)


def solution(mesh):
    in_specs = (P(("seg", "blk"), None, None, None), P(("seg", "blk"), None, None, None), P(), P())
    out_specs = P(("seg", "blk"), None, None, None)
    return jax.shard_map(
        on_device, mesh=mesh, in_specs=in_specs, out_specs=out_specs, check_vma=False
    )
```

```python
import functools
import jax
import jax.numpy as jnp
from jax import lax
from jax.experimental import pallas as pl
from jax.experimental.pallas import tpu as pltpu
from jax.sharding import PartitionSpec as P

LEN, CROSS, CELLS, TILES = 16, 48, 2304, 18
HALF = 9
DEEP, GEOMETRY, BELOW, ABOVE, ROWS = 64, 128, 272, 280, 288
FACE, ALONG, ACROSS, POSITION, HAS_LOW, HAS_HIGH, OWN, MATE = 0, 1, 2, 3, 4, 5, 6, 9
PARTS = ((0, BELOW), (BELOW, ABOVE), (ABOVE, ROWS))
SEGS, CHAIN = 8, 32
time_step = 0.05
viscosity = 0.2
compress = 1.0
SIGN = (-1.0, -1.0, -1.0, 1.0)
VMEM = pl.BlockSpec(memory_space=pltpu.VMEM)
SMEM = pl.BlockSpec(memory_space=pltpu.SMEM)


def lanes_of(rows=8):
    return lax.broadcasted_iota(jnp.int32, (rows, 128), 1)


def gather_lanes(values, index):
    parts = [
        jnp.take_along_axis(values[r : r + 8], index, axis=1, mode="promise_in_bounds")
        for r in range(0, values.shape[0], 8)
    ]
    return parts[0] if len(parts) == 1 else jnp.concatenate(parts, axis=0)


def reversed_rows(values):
    index = 7 - lax.broadcasted_iota(jnp.int32, (8, 128), 0)
    flip = lambda part: jnp.take_along_axis(part, index, axis=0, mode="promise_in_bounds")
    return jnp.concatenate([flip(values[8:16]), flip(values[0:8])], axis=0)


def joined_face(device, block_map, links):
    block = block_map[device]
    face, partner, along, across = jnp.int32(0), jnp.int32(-1), jnp.int32(0), jnp.int32(0)
    for side in range(2, 6):
        other = links[side, 0, block]
        here = other >= 0
        face = jnp.where(here, side, face)
        partner = jnp.where(here, other, partner)
        along = jnp.where(here, links[side, 2, block], along)
        across = jnp.where(here, links[side, 3, block], across)
    position = lax.rem(device, CHAIN)
    segment = jnp.int32(0)
    for s in range(SEGS):
        segment = jnp.where(block_map[s * CHAIN + position] == partner, s, segment)
    return face, segment, along, across


def face_source(face, across, first_layer):
    lane = lanes_of()
    layer = jnp.where(lane >= CROSS, 1, 0)
    place = lane - layer * CROSS
    place = jnp.where(across == 1, CROSS - 1 - place, place)
    depth = first_layer + layer
    depth = jnp.where((face == 3) | (face == 5), CROSS - 1 - depth, depth)
    return jnp.where(face <= 3, depth * CROSS + place, place * CROSS + depth)


def gather_face(load, source):
    index, owner = source & 127, source >> 7
    found = None
    for t in range(TILES):
        picked = gather_lanes(load(t), index)
        if found is None:
            found = picked
        else:
            inside = owner == t
            if picked.shape[0] == LEN:
                inside = jnp.concatenate([inside, inside], axis=0)
            found = jnp.where(inside, picked, found)
    return found


def write_chain(field, even_ref, odd_ref, position):
    even = lax.rem(position, 2) == 0
    for c in range(4):
        low, high = field[c, 0:2, :], field[c, LEN - 2 : LEN, :]
        even_ref[2 * c : 2 * c + 2, 0:CELLS] = jnp.where(even, high, low)
        odd_ref[2 * c : 2 * c + 2, 0:CELLS] = jnp.where(even, low, high)


def first_kernel(q_hbm, metric_hbm, map_hbm, links_hbm, q, metric, joint_ref, meta, block_map, links, sem):
    copies = [
        pltpu.make_async_copy(source, target, sem.at[n])
        for n, (source, target) in enumerate(
            ((links_hbm, links), (map_hbm, block_map), (q_hbm, q), (metric_hbm, metric))
        )
    ]
    for copy in copies:
        copy.start()
    segment, position = lax.axis_index("seg"), lax.axis_index("blk")
    copies[0].wait()
    copies[1].wait()
    here = segment * CHAIN + position
    other = (segment ^ 4) * CHAIN + position
    before, after = jnp.where(position > 0, -1, 0), jnp.where(position < CHAIN - 1, 1, 0)
    face, partner, along, across = joined_face(here, block_map, links)
    low_face, low_partner, _, low_across = joined_face(here + before, block_map, links)
    high_face, high_partner, _, high_across = joined_face(here + after, block_map, links)
    own = (partner, low_partner, high_partner)
    mates = [joined_face(other + shift, block_map, links)[1] for shift in (0, before, after)]
    meta[FACE] = face
    meta[ALONG] = along
    meta[ACROSS] = across
    meta[POSITION] = position
    block = block_map[here]
    meta[HAS_LOW] = jnp.where(links[0, 0, block] >= 0, 1, 0)
    meta[HAS_HIGH] = jnp.where(links[1, 0, block] >= 0, 1, 0)
    for n in range(3):
        meta[OWN + n] = jnp.where(own[n] // 4 == segment // 4, (own[n] ^ segment) & 3, 0)
        meta[MATE + n] = (mates[n] ^ segment) & 3
    copies[2].wait()

    def put(start, values):
        joint_ref[start : start + LEN, :] = jnp.where(along == 1, reversed_rows(values), values)

    where = lambda t: slice(128 * t, 128 * t + 128)
    near, deep = face_source(face, across, 0), face_source(face, across, 2)
    below, above = face_source(low_face, low_across, 0), face_source(high_face, high_across, 0)
    for c in range(4):
        put(LEN * c, gather_face(lambda t: q[c, :, where(t)], near))
        put(DEEP + LEN * c, gather_face(lambda t: q[c, :, where(t)], deep))
        low_rows = gather_face(lambda t: q[c, 0:8, where(t)], below)
        joint_ref[BELOW + 2 * c : BELOW + 2 * c + 2, :] = low_rows[0:2]
        high_rows = gather_face(lambda t: q[c, 8:16, where(t)], above)
        joint_ref[ABOVE + 2 * c : ABOVE + 2 * c + 2, :] = high_rows[6:8]
    copies[3].wait()
    normal = jnp.where(face <= 3, 1, 2)
    inward = jnp.where((face == 3) | (face == 5), -1.0, 1.0)
    forward = jnp.where(along == 1, -1.0, 1.0)
    sideways = jnp.where(across == 1, -1.0, 1.0)
    for a, (row, sign) in enumerate(((0, forward), (3 * normal, inward), (3 * (3 - normal), sideways))):
        for b in range(3):
            found = gather_face(lambda t: metric[row + b, :, where(t)], near)
            put(GEOMETRY + LEN * (3 * a + b), sign * found)


def copy_part(choice, refs, rows, out):
    for n, ref in enumerate(refs):

        @pl.when(choice == n)
        def _(ref=ref):
            out[...] = ref[rows[0] : rows[1], :]


def pick_kernel(own, one, two, three, meta, out):
    for n, rows in enumerate(PARTS):
        copy_part(meta[MATE + n], (own, one, two, three), rows, out.at[rows[0] : rows[1], :])


def shifted_lanes(before, here, after, shift):
    lane = lanes_of(LEN)
    if shift > 0:
        return jnp.where(
            lane < 128 - shift, pltpu.roll(here, 128 - shift, 1), pltpu.roll(after, 128 - shift, 1)
        )
    return jnp.where(lane >= -shift, pltpu.roll(here, -shift, 1), pltpu.roll(before, -shift, 1))


def shifted_rows(padded, shift):
    return pltpu.roll(padded, (-shift) % 32, 0)[8:24]


def differences(m2, m1, here, p1, p2):
    return 8.0 * (p1 - m1) - (p2 - m2)


def bends(m2, m1, here, p1, p2):
    return 16.0 * (p1 + m1) - (p2 + m2) - 30.0 * here


def advance(stencils, geometry):
    here = [stencils[c][0][2] for c in range(4)]
    moves = [-(time_step / 12.0) * geometry[n] for n in range(9)]
    result = list(here)
    fall = None
    for a in range(3):
        g = geometry[3 * a : 3 * a + 3]
        n = moves[3 * a : 3 * a + 3]
        speed = n[0] * here[0] + n[1] * here[1] + n[2] * here[2]
        spread = (viscosity * time_step / 12.0) * (g[0] * g[0] + g[1] * g[1] + g[2] * g[2])
        drop = differences(*stencils[3][a])
        for b in range(3):
            slope = differences(*stencils[b][a])
            result[b] = result[b] + speed * slope + n[b] * drop + spread * bends(*stencils[b][a])
            term = n[b] * slope
            fall = term if fall is None else fall + term
    result[3] = result[3] + compress * fall
    return result


def bulk_kernel(last, tiles, q, metric, *rest):
    first, rest = (rest[0], rest[1:]) if last else (None, rest)
    meta, out = rest[:2]
    if len(rest) == 4:
        write_chain(q, rest[2], rest[3], meta[POSITION])
    lane = lanes_of(LEN)
    row = lax.broadcasted_iota(jnp.int32, (8, 128), 0)
    face, ends = meta[FACE], (meta[HAS_LOW] == 0, meta[HAS_HIGH] == 0)
    load = lambda c, t: q[c, :, 128 * t : 128 * t + 128]
    before_first, after_last = [], []
    for c in range(4):
        head = jnp.where(face == 2, 0.0, SIGN[c]) * load(c, 0)
        before_first.append(jnp.where(lane >= 80, pltpu.roll(head, 80, 1), pltpu.roll(head, 112, 1)))
        tail = jnp.where(face == 3, 0.0, SIGN[c]) * load(c, TILES - 1)
        after_last.append(jnp.where(lane < CROSS, pltpu.roll(tail, 48, 1), pltpu.roll(tail, 16, 1)))

    def tile(c, t):
        return before_first[c] if t < 0 else after_last[c] if t >= TILES else load(c, t)

    low_scale = jnp.where(face == 4, 0.0, 1.0)
    high_scale = jnp.where(face == 5, 0.0, 1.0)
    open_low = jnp.where(ends[0], 1.0, 0.0)
    open_high = jnp.where(ends[1], 1.0, 0.0)
    for t in tiles:
        flat = 128 * t + lane
        k = flat - (flat // CROSS) * CROSS
        scale = jnp.where(k < 2, low_scale, high_scale)
        stencils = []
        for c in range(4):
            before, here, after = tile(c, t - 1), tile(c, t), tile(c, t + 1)
            top, bottom = here[0:8], here[8:16]
            low = -SIGN[c] * open_low * jnp.where(row == 7, pltpu.roll(top, 7, 0), pltpu.roll(top, 5, 0))
            high = -SIGN[c] * open_high * jnp.where(row == 0, pltpu.roll(bottom, 1, 0), pltpu.roll(bottom, 3, 0))
            rows = jnp.concatenate([low, here, high], axis=0)
            along_i = [shifted_rows(rows, s) for s in (-2, -1)] + [here] + [shifted_rows(rows, s) for s in (1, 2)]
            along_j = [shifted_lanes(before, here, after, CROSS * s) if s else here for s in range(-2, 3)]
            raw = [shifted_lanes(before, here, after, s) if s else here for s in range(-2, 3)]
            factor = SIGN[c] * scale
            nearest = factor * here
            second = factor * jnp.where((k == 0) | (k == 46), raw[3], raw[1])
            along_k = [
                jnp.where(k < 2, second, raw[0]),
                jnp.where(k == 0, nearest, raw[1]),
                here,
                jnp.where(k == 47, nearest, raw[3]),
                jnp.where(k >= 46, second, raw[4]),
            ]
            stencils.append((along_i, along_j, along_k))
        where = slice(128 * t, 128 * t + 128)
        values = advance(stencils, [metric[n, :, where] for n in range(9)])
        for c in range(4):
            kept = 0.5 * first[c, :, where] + 0.5 * values[c] if last else values[c]
            out[c, :, 128 * (t - tiles[0]) : 128 * (t - tiles[0]) + 128] = kept


def edge_terms(here, geometry, slopes, curves, scale):
    moves = [-(scale * time_step / 12.0) * g for g in geometry]
    speed = moves[0] * here[0] + moves[1] * here[1] + moves[2] * here[2]
    squares = geometry[0] * geometry[0] + geometry[1] * geometry[1] + geometry[2] * geometry[2]
    spread = (scale * viscosity * time_step / 12.0) * squares
    added = [speed * slopes[b] + moves[b] * slopes[3] + spread * curves[b] for b in range(3)]
    added.append(compress * (moves[0] * slopes[0] + moves[1] * slopes[1] + moves[2] * slopes[2]))
    return added


def partner_face(sent, main, low_ref, high_ref, from_low, from_high, meta, ghost_ref):
    lane = lanes_of(LEN)
    place = jnp.where(lane >= CROSS, lane - CROSS, lane)
    along, across = meta[ALONG] == 1, meta[ACROSS] == 1
    missing_low = jnp.where(along, meta[HAS_HIGH], meta[HAS_LOW]) == 0
    missing_high = jnp.where(along, meta[HAS_LOW], meta[HAS_HIGH]) == 0
    mirrored = jnp.where(lane < CROSS, CROSS - 1 - lane, jnp.where(lane < 2 * CROSS, 3 * CROSS - 1 - lane, lane))[:8]
    stencils = []
    for c in range(4):
        mine = sent[LEN * c : LEN * c + LEN, :]
        mine = jnp.where(across, gather_lanes(mine, mirrored), mine)
        mine = jnp.where(along, reversed_rows(mine), mine)
        here = main[LEN * c : LEN * c + LEN, :]
        deep = main[DEEP + LEN * c : DEEP + LEN * c + LEN, :]
        below, above = from_low[2 * c : 2 * c + 2, :], from_high[2 * c : 2 * c + 2, :]
        low_ref[6:7, :] = jnp.where(missing_low, -SIGN[c] * here[1:2], jnp.where(along, above[1:2], below[0:1]))
        low_ref[7:8, :] = jnp.where(missing_low, -SIGN[c] * here[0:1], jnp.where(along, above[0:1], below[1:2]))
        high_ref[0:1, :] = jnp.where(missing_high, -SIGN[c] * here[15:16], jnp.where(along, below[1:2], above[0:1]))
        high_ref[1:2, :] = jnp.where(missing_high, -SIGN[c] * here[14:15], jnp.where(along, below[0:1], above[1:2]))
        rows = jnp.concatenate([low_ref[...], here, high_ref[...]], axis=0)
        along_i = [shifted_rows(rows, s) for s in (-2, -1)] + [here] + [shifted_rows(rows, s) for s in (1, 2)]
        outer = lane < CROSS
        normal = [
            jnp.where(outer, pltpu.roll(mine, 80, 1), pltpu.roll(mine, 48, 1)),
            jnp.where(outer, mine, pltpu.roll(here, 48, 1)),
            here,
            jnp.where(outer, pltpu.roll(here, 80, 1), pltpu.roll(deep, 48, 1)),
            deep,
        ]
        raw = [pltpu.roll(here, (-s) % 128, 1) if s else here for s in range(-2, 3)]
        wall = SIGN[c] * here
        second = SIGN[c] * jnp.where((place == 0) | (place == 46), raw[3], raw[1])
        sideways = [
            jnp.where(place < 2, second, raw[0]),
            jnp.where(place == 0, wall, raw[1]),
            here,
            jnp.where(place == 47, wall, raw[3]),
            jnp.where(place >= 46, second, raw[4]),
        ]
        stencils.append((along_i, normal, sideways))
    geometry = [main[GEOMETRY + LEN * n : GEOMETRY + LEN * n + LEN, :] for n in range(9)]
    for c, values in enumerate(advance(stencils, geometry)):
        ghost_ref[LEN * c : LEN * c + LEN, :] = values


def edge_kernel(last, q, metric, one, two, three, mate, even_in, odd_in, meta, *rest):
    face = meta[FACE]
    even = lax.rem(meta[POSITION], 2) == 0
    received = (mate, one, two, three)
    if last:
        bulk, sent, out, low_ref, high_ref, ghost_ref, main, first_low, first_high = rest
        copy_part(meta[OWN], received, PARTS[0], main)
        spare = slice(CELLS, CELLS + 128)
        from_even, from_odd = even_in[:, spare], odd_in[:, spare]
        partner_face(
            sent, main, first_low, first_high,
            jnp.where(even, from_odd, from_even), jnp.where(even, from_even, from_odd), meta, ghost_ref,
        )
    else:
        left, right, out, even_ref, odd_ref, low_ref, high_ref, ghost_ref, below, above = rest
        copy_part(meta[OWN], received, (0, DEEP), ghost_ref)
        copy_part(meta[OWN + 1], received, PARTS[1], below)
        copy_part(meta[OWN + 2], received, PARTS[2], above)
    scale = 0.5 if last else 1.0
    has_low = jnp.where(meta[HAS_LOW] == 1, 1.0, 0.0)
    has_high = jnp.where(meta[HAS_HIGH] == 1, 1.0, 0.0)
    for c in range(4):
        rows = slice(2 * c, 2 * c + 2)
        from_even, from_odd = even_in[rows, 0:CELLS], odd_in[rows, 0:CELLS]
        low_ref[c, 0:2, :] = has_low * jnp.where(even, from_odd, from_even)
        high_ref[c, 6:8, :] = has_high * jnp.where(even, from_even, from_odd)

    row = lax.broadcasted_iota(jnp.int32, (8, 128), 0)
    for t in range(TILES):
        where = slice(128 * t, 128 * t + 128)
        if last:
            part, place = bulk, where
        else:
            part, place = (left, where) if t < HALF else (right, slice(128 * (t - HALF), 128 * (t - HALF) + 128))
        for high in (False, True):
            half = slice(8, 16) if high else slice(0, 8)
            slopes, curves = [], []
            for c in range(4):
                if high:
                    ghost = high_ref[c, :, where]
                    first = jnp.where(row == 7, pltpu.roll(ghost, 1, 0), 0.0)
                    second = jnp.where(row >= 6, ghost, 0.0)
                    slopes.append(8.0 * first - second)
                else:
                    ghost = low_ref[c, :, where]
                    first = jnp.where(row == 0, pltpu.roll(ghost, 7, 0), 0.0)
                    second = jnp.where(row < 2, ghost, 0.0)
                    slopes.append(second - 8.0 * first)
                curves.append(16.0 * first - second)
            here = [q[c, half, where] for c in range(4)]
            added = edge_terms(here, [metric[n, half, where] for n in range(3)], slopes, curves, scale)
            for c in range(4):
                out[c, half, where] = part[c, half, place] + added[c]

    lane = lanes_of(LEN)

    def add(t, direction, slopes, curves):
        where = slice(128 * t, 128 * t + 128)
        here = [q[c, :, where] for c in range(4)]
        geometry = [metric[3 * direction + n, :, where] for n in range(3)]
        added = edge_terms(here, geometry, slopes, curves, scale)
        for c in range(4):
            out[c, :, where] = out[c, :, where] + added[c]

    ghost_of = lambda c: ghost_ref[16 * c : 16 * c + 16, :]

    @pl.when(face == 2)
    def _():
        slopes, curves = [], []
        for c in range(4):
            ghost = ghost_of(c)
            first = jnp.where(lane < CROSS, ghost, 0.0)
            second = jnp.where(lane < CROSS, pltpu.roll(ghost, 80, 1), pltpu.roll(ghost, 48, 1))
            second = jnp.where(lane < 2 * CROSS, second, 0.0)
            slopes.append(second - 8.0 * first)
            curves.append(16.0 * first - second)
        add(0, 1, slopes, curves)

    @pl.when(face == 3)
    def _():
        slopes, curves = [], []
        for c in range(4):
            ghost = ghost_of(c)
            first = jnp.where(lane >= 80, pltpu.roll(ghost, 80, 1), 0.0)
            second = jnp.where(lane >= 32, pltpu.roll(ghost, 32, 1), 0.0)
            slopes.append(8.0 * first - second)
            curves.append(16.0 * first - second)
        add(TILES - 1, 1, slopes, curves)

    @pl.when(face >= 4)
    def _():
        toward = jnp.where(face == 4, -1.0, 1.0)
        for t in range(TILES):
            flat = 128 * t + lane
            j = flat // CROSS
            k = flat - j * CROSS
            depth = jnp.where(face == 4, k, CROSS - 1 - k)
            far = jnp.where(depth == 0, j + CROSS, j)[:8]
            slopes, curves = [], []
            for c in range(4):
                ghost = ghost_of(c)
                first = jnp.where(depth == 0, gather_lanes(ghost, j[:8]), 0.0)
                second = jnp.where(depth < 2, gather_lanes(ghost, far), 0.0)
                slopes.append(toward * (8.0 * first - second))
                curves.append(16.0 * first - second)
            add(t, 2, slopes, curves)

    if not last:
        write_chain(out, even_ref, odd_ref, meta[POSITION])
        spare = slice(CELLS, CELLS + 128)
        even_ref[:, spare] = jnp.where(even, above[...], below[...])
        odd_ref[:, spare] = jnp.where(even, below[...], above[...])


f32 = functools.partial(jax.ShapeDtypeStruct, dtype=jnp.float32)
PARAMS = pltpu.CompilerParams(vmem_limit_bytes=24 * 1024 * 1024)
FIELD = f32((4, LEN, CELLS))
JOINT = f32((ROWS, 128))
HALO = [pltpu.VMEM((4, 8, CELLS), jnp.float32)] * 2 + [pltpu.VMEM((64, 128), jnp.float32)]
TILE = pltpu.VMEM((8, 128), jnp.float32)


def local(kernel, shapes, operands, scratch=(), flops=1_000_000):
    return pl.pallas_call(
        kernel,
        out_shape=shapes,
        in_specs=[VMEM] * (len(operands) - 1) + [SMEM],
        out_specs=[VMEM] * len(shapes),
        scratch_shapes=list(scratch),
        compiler_params=PARAMS,
        cost_estimate=pl.CostEstimate(flops=flops, bytes_accessed=flops, transcendentals=0),
    )(*operands)


def bulk(last, tiles, chains, *operands):
    shapes = [f32((4, LEN, 128 * len(tiles)))] + ([f32((8, CELLS))] * 2 if chains else [])
    kernel = functools.partial(bulk_kernel, last, tiles)
    return local(kernel, shapes, operands, flops=660_000 * len(tiles))


def along_chain(even, odd):
    from_even = lax.ppermute(even, "blk", [(i, i ^ 1) for i in range(CHAIN)])
    pairs = [(i, i + 1) for i in range(1, CHAIN - 1, 2)]
    return from_even, lax.ppermute(odd, "blk", pairs + [(b, a) for a, b in pairs])


def on_device(state, metric, block_map, links):
    HBM = pl.BlockSpec(memory_space=pltpu.HBM)
    held = lambda x: pltpu.with_memory_space_constraint(x, pltpu.HBM)
    arrays = (state.reshape(4, LEN, CELLS), metric.reshape(9, LEN, CELLS), block_map, jnp.transpose(links, (1, 2, 0)))
    q, geometry, joint, meta = pl.pallas_call(
        first_kernel,
        out_shape=[FIELD, f32((9, LEN, CELLS)), JOINT, jax.ShapeDtypeStruct((16,), jnp.int32)],
        in_specs=[HBM] * 4,
        out_specs=[VMEM] * 3 + [SMEM],
        scratch_shapes=[
            pltpu.SMEM((SEGS * CHAIN,), jnp.int32),
            pltpu.SMEM((6, 4, SEGS * CHAIN), jnp.int32),
            pltpu.SemaphoreType.DMA((4,)),
        ],
        compiler_params=PARAMS,
    )(*map(held, arrays))
    one, two, three = (
        lax.ppermute(joint, "seg", [(i, i ^ s) for i in range(SEGS)]) for s in (1, 2, 3)
    )
    left, even, odd = bulk(False, range(HALF), True, q, geometry, meta)
    one, two, three, even, odd = lax.optimization_barrier((one, two, three, even, odd))
    from_even, from_odd = along_chain(even, odd)
    (picked,) = local(pick_kernel, [JOINT], (joint, one, two, three, meta))
    mate = lax.ppermute(picked, "seg", [(i, i ^ 4) for i in range(SEGS)])
    (right,) = bulk(False, range(HALF, TILES), False, q, geometry, meta)
    kernel = functools.partial(edge_kernel, False)

    def first_edges(left, right, *operands):
        return kernel(*operands[:9], left, right, *operands[9:])

    q1, even, odd = local(
        first_edges,
        [FIELD] + [f32((8, CELLS + 128))] * 2,
        (left, right, q, geometry, one, two, three, mate, from_even, from_odd, meta),
        HALO + [TILE] * 2,
    )
    from_even, from_odd = along_chain(even, odd)
    (part,) = bulk(True, range(TILES), False, q1, geometry, q, meta)

    def last_edges(part, sent, *operands):
        return edge_kernel(True, *operands[:9], part, sent, *operands[9:])

    (advanced,) = local(
        last_edges,
        [FIELD],
        (part, joint, q1, geometry, one, two, three, mate, from_even, from_odd, meta),
        HALO + [pltpu.VMEM((BELOW, 128), jnp.float32)] + [TILE] * 2,
    )
    return advanced.reshape(state.shape)


def solution(mesh):
    in_specs = (P(("seg", "blk"), None, None, None), P(("seg", "blk"), None, None, None), P(), P())
    out_specs = P(("seg", "blk"), None, None, None)
    return jax.shard_map(
        on_device, mesh=mesh, in_specs=in_specs, out_specs=out_specs, check_vma=False
    )
```

```python
import functools
import jax
import jax.numpy as jnp
from jax import lax
from jax.experimental import pallas as pl
from jax.experimental.pallas import tpu as pltpu
from jax.sharding import PartitionSpec as P

LEN, CROSS, CELLS, TILES = 16, 48, 2304, 18
GROUP = 6
GEOMETRY, BELOW, ABOVE, ROWS = 64, 208, 216, 224
USED, SPARE = 96, 32
FACE, ALONG, ACROSS, POSITION, HAS_LOW, HAS_HIGH, OWN, MATE = 0, 1, 2, 3, 4, 5, 6, 9
PARTS = ((0, BELOW), (BELOW, ABOVE), (ABOVE, ROWS))
SEGS, CHAIN = 8, 32
time_step = 0.05
viscosity = 0.2
compress = 1.0
SIGN = (-1.0, -1.0, -1.0, 1.0)
VMEM = pl.BlockSpec(memory_space=pltpu.VMEM)
SMEM = pl.BlockSpec(memory_space=pltpu.SMEM)


def lanes_of(rows=8):
    return lax.broadcasted_iota(jnp.int32, (rows, 128), 1)


def gather_lanes(values, index):
    parts = [
        jnp.take_along_axis(values[r : r + 8], index, axis=1, mode="promise_in_bounds")
        for r in range(0, values.shape[0], 8)
    ]
    return parts[0] if len(parts) == 1 else jnp.concatenate(parts, axis=0)


def reversed_rows(values):
    index = 7 - lax.broadcasted_iota(jnp.int32, (8, 128), 0)
    flip = lambda part: jnp.take_along_axis(part, index, axis=0, mode="promise_in_bounds")
    return jnp.concatenate([flip(values[8:16]), flip(values[0:8])], axis=0)


def joined_face(device, block_map, links):
    block = block_map[device]
    face, partner, along, across = jnp.int32(0), jnp.int32(-1), jnp.int32(0), jnp.int32(0)
    for side in range(2, 6):
        other = links[side, 0, block]
        here = other >= 0
        face = jnp.where(here, side, face)
        partner = jnp.where(here, other, partner)
        along = jnp.where(here, links[side, 2, block], along)
        across = jnp.where(here, links[side, 3, block], across)
    position = lax.rem(device, CHAIN)
    segment = jnp.int32(0)
    for s in range(SEGS):
        segment = jnp.where(block_map[s * CHAIN + position] == partner, s, segment)
    return face, segment, along, across


def face_source(face, across, first_layer):
    lane = lanes_of()
    layer = jnp.where(lane >= CROSS, 1, 0)
    place = lane - layer * CROSS
    place = jnp.where(across == 1, CROSS - 1 - place, place)
    depth = first_layer + layer
    depth = jnp.where((face == 3) | (face == 5), CROSS - 1 - depth, depth)
    return jnp.where(face <= 3, depth * CROSS + place, place * CROSS + depth)


def gather_face(load, source):
    index, owner = source & 127, source >> 7
    found = None
    for t in range(TILES):
        picked = gather_lanes(load(t), index)
        if found is None:
            found = picked
        else:
            inside = owner == t
            if picked.shape[0] == LEN:
                inside = jnp.concatenate([inside, inside], axis=0)
            found = jnp.where(inside, picked, found)
    return found


def write_chain(field, even_ref, odd_ref, position):
    even = lax.rem(position, 2) == 0
    for c in range(4):
        low, high = field[c, 0:2, :], field[c, LEN - 2 : LEN, :]
        even_ref[2 * c : 2 * c + 2, 0:CELLS] = jnp.where(even, high, low)
        odd_ref[2 * c : 2 * c + 2, 0:CELLS] = jnp.where(even, low, high)


def first_kernel(q_hbm, metric_hbm, map_hbm, links_hbm, q, metric, joint_ref, meta, block_map, links, sem):
    copies = [
        pltpu.make_async_copy(source, target, sem.at[n])
        for n, (source, target) in enumerate(
            ((links_hbm, links), (map_hbm, block_map), (q_hbm, q), (metric_hbm, metric))
        )
    ]
    for copy in copies:
        copy.start()
    segment, position = lax.axis_index("seg"), lax.axis_index("blk")
    copies[0].wait()
    copies[1].wait()
    here = segment * CHAIN + position
    other = (segment ^ 4) * CHAIN + position
    before, after = jnp.where(position > 0, -1, 0), jnp.where(position < CHAIN - 1, 1, 0)
    face, partner, along, across = joined_face(here, block_map, links)
    low_face, low_partner, _, low_across = joined_face(here + before, block_map, links)
    high_face, high_partner, _, high_across = joined_face(here + after, block_map, links)
    own = (partner, low_partner, high_partner)
    mates = [joined_face(other + shift, block_map, links)[1] for shift in (0, before, after)]
    meta[FACE] = face
    meta[ALONG] = along
    meta[ACROSS] = across
    meta[POSITION] = position
    block = block_map[here]
    meta[HAS_LOW] = jnp.where(links[0, 0, block] >= 0, 1, 0)
    meta[HAS_HIGH] = jnp.where(links[1, 0, block] >= 0, 1, 0)
    for n in range(3):
        meta[OWN + n] = jnp.where(own[n] // 4 == segment // 4, (own[n] ^ segment) & 3, 0)
        meta[MATE + n] = (mates[n] ^ segment) & 3
    copies[2].wait()

    where = lambda t: slice(128 * t, 128 * t + 128)
    lane = lanes_of(LEN)
    near, deep = face_source(face, across, 0), face_source(face, across, 2)
    below, above = face_source(low_face, low_across, 0), face_source(high_face, high_across, 0)
    deeper = [gather_face(lambda t: q[c, :, where(t)], deep) for c in range(4)]

    def put(n, values):
        if n < 12:
            third = pltpu.roll(deeper[n // 3], USED - SPARE * (n % 3), 1)
            values = jnp.where(lane < USED, values, third)
        joint_ref[LEN * n : LEN * n + LEN, :] = jnp.where(along == 1, reversed_rows(values), values)

    for c in range(4):
        put(c, gather_face(lambda t: q[c, :, where(t)], near))
        low_rows = gather_face(lambda t: q[c, 0:8, where(t)], below)
        joint_ref[BELOW + 2 * c : BELOW + 2 * c + 2, :] = low_rows[0:2]
        high_rows = gather_face(lambda t: q[c, 8:16, where(t)], above)
        joint_ref[ABOVE + 2 * c : ABOVE + 2 * c + 2, :] = high_rows[6:8]
    copies[3].wait()
    normal = jnp.where(face <= 3, 1, 2)
    inward = jnp.where((face == 3) | (face == 5), -1.0, 1.0)
    forward = jnp.where(along == 1, -1.0, 1.0)
    sideways = jnp.where(across == 1, -1.0, 1.0)
    for a, (row, sign) in enumerate(((0, forward), (3 * normal, inward), (3 * (3 - normal), sideways))):
        for b in range(3):
            found = gather_face(lambda t: metric[row + b, :, where(t)], near)
            put(4 + 3 * a + b, sign * found)


def copy_part(choice, refs, rows, out):
    for n, ref in enumerate(refs):

        @pl.when(choice == n)
        def _(ref=ref):
            out[...] = ref[rows[0] : rows[1], :]


def pick_kernel(own, one, two, three, meta, out):
    for n, rows in enumerate(PARTS):
        copy_part(meta[MATE + n], (own, one, two, three), rows, out.at[rows[0] : rows[1], :])


def shifted_lanes(before, here, after, shift):
    lane = lanes_of(LEN)
    if shift > 0:
        return jnp.where(
            lane < 128 - shift, pltpu.roll(here, 128 - shift, 1), pltpu.roll(after, 128 - shift, 1)
        )
    return jnp.where(lane >= -shift, pltpu.roll(here, -shift, 1), pltpu.roll(before, -shift, 1))


def shifted_rows(padded, shift):
    return pltpu.roll(padded, (-shift) % 32, 0)[8:24]


def differences(m2, m1, here, p1, p2):
    return 8.0 * (p1 - m1) - (p2 - m2)


def bends(m2, m1, here, p1, p2):
    return 16.0 * (p1 + m1) - (p2 + m2) - 30.0 * here


def advance(stencils, geometry):
    here = [stencils[c][0][2] for c in range(4)]
    moves = [-(time_step / 12.0) * geometry[n] for n in range(9)]
    result = list(here)
    fall = None
    for a in range(3):
        g = geometry[3 * a : 3 * a + 3]
        n = moves[3 * a : 3 * a + 3]
        speed = n[0] * here[0] + n[1] * here[1] + n[2] * here[2]
        spread = (viscosity * time_step / 12.0) * (g[0] * g[0] + g[1] * g[1] + g[2] * g[2])
        drop = differences(*stencils[3][a])
        for b in range(3):
            slope = differences(*stencils[b][a])
            result[b] = result[b] + speed * slope + n[b] * drop + spread * bends(*stencils[b][a])
            term = n[b] * slope
            fall = term if fall is None else fall + term
    result[3] = result[3] + compress * fall
    return result


def bulk_kernel(last, q, metric, *rest):
    first, rest = (rest[0], rest[1:]) if last else (None, rest)
    meta, out = rest[:2]
    if len(rest) == 4:
        write_chain(q, rest[2], rest[3], meta[POSITION])
    lane = lanes_of(LEN)
    row = lax.broadcasted_iota(jnp.int32, (8, 128), 0)
    face, ends = meta[FACE], (meta[HAS_LOW] == 0, meta[HAS_HIGH] == 0)
    load = lambda c, t: q[c, :, 128 * t : 128 * t + 128]
    before_first, after_last = [], []
    for c in range(4):
        head = jnp.where(face == 2, 0.0, SIGN[c]) * load(c, 0)
        before_first.append(jnp.where(lane >= 80, pltpu.roll(head, 80, 1), pltpu.roll(head, 112, 1)))
        tail = jnp.where(face == 3, 0.0, SIGN[c]) * load(c, TILES - 1)
        after_last.append(jnp.where(lane < CROSS, pltpu.roll(tail, 48, 1), pltpu.roll(tail, 16, 1)))

    def tile(c, t):
        return before_first[c] if t < 0 else after_last[c] if t >= TILES else load(c, t)

    low_scale = jnp.where(face == 4, 0.0, 1.0)
    high_scale = jnp.where(face == 5, 0.0, 1.0)
    open_low = jnp.where(ends[0], 1.0, 0.0)
    open_high = jnp.where(ends[1], 1.0, 0.0)
    for t in range(TILES):
        flat = 128 * t + lane
        k = flat - (flat // CROSS) * CROSS
        scale = jnp.where(k < 2, low_scale, high_scale)
        stencils = []
        for c in range(4):
            before, here, after = tile(c, t - 1), tile(c, t), tile(c, t + 1)
            top, bottom = here[0:8], here[8:16]
            low = -SIGN[c] * open_low * jnp.where(row == 7, pltpu.roll(top, 7, 0), pltpu.roll(top, 5, 0))
            high = -SIGN[c] * open_high * jnp.where(row == 0, pltpu.roll(bottom, 1, 0), pltpu.roll(bottom, 3, 0))
            rows = jnp.concatenate([low, here, high], axis=0)
            along_i = [shifted_rows(rows, s) for s in (-2, -1)] + [here] + [shifted_rows(rows, s) for s in (1, 2)]
            along_j = [shifted_lanes(before, here, after, CROSS * s) if s else here for s in range(-2, 3)]
            raw = [shifted_lanes(before, here, after, s) if s else here for s in range(-2, 3)]
            factor = SIGN[c] * scale
            nearest = factor * here
            second = factor * jnp.where((k == 0) | (k == 46), raw[3], raw[1])
            along_k = [
                jnp.where(k < 2, second, raw[0]),
                jnp.where(k == 0, nearest, raw[1]),
                here,
                jnp.where(k == 47, nearest, raw[3]),
                jnp.where(k >= 46, second, raw[4]),
            ]
            stencils.append((along_i, along_j, along_k))
        where = slice(128 * t, 128 * t + 128)
        values = advance(stencils, [metric[n, :, where] for n in range(9)])
        for c in range(4):
            kept = 0.5 * first[c, :, where] + 0.5 * values[c] if last else values[c]
            out[c, :, where] = kept


def edge_terms(here, geometry, slopes, curves, scale):
    moves = [-(scale * time_step / 12.0) * g for g in geometry]
    speed = moves[0] * here[0] + moves[1] * here[1] + moves[2] * here[2]
    squares = geometry[0] * geometry[0] + geometry[1] * geometry[1] + geometry[2] * geometry[2]
    spread = (scale * viscosity * time_step / 12.0) * squares
    added = [speed * slopes[b] + moves[b] * slopes[3] + spread * curves[b] for b in range(3)]
    added.append(compress * (moves[0] * slopes[0] + moves[1] * slopes[1] + moves[2] * slopes[2]))
    return added


def partner_face(sent, main, low_ref, high_ref, from_low, from_high, meta, ghost_ref):
    lane = lanes_of(LEN)
    place = jnp.where(lane >= CROSS, lane - CROSS, lane)
    along, across = meta[ALONG] == 1, meta[ACROSS] == 1
    missing_low = jnp.where(along, meta[HAS_HIGH], meta[HAS_LOW]) == 0
    missing_high = jnp.where(along, meta[HAS_LOW], meta[HAS_HIGH]) == 0
    mirrored = jnp.where(lane < CROSS, CROSS - 1 - lane, jnp.where(lane < 2 * CROSS, 3 * CROSS - 1 - lane, lane))[:8]
    stencils = []
    for c in range(4):
        mine = sent[LEN * c : LEN * c + LEN, :]
        mine = jnp.where(across, gather_lanes(mine, mirrored), mine)
        mine = jnp.where(along, reversed_rows(mine), mine)
        here = main[LEN * c : LEN * c + LEN, :]
        thirds = [
            pltpu.roll(main[LEN * n : LEN * n + LEN, :], (SPARE * (n % 3) - USED) % 128, 1) for n in range(3 * c, 3 * c + 3)
        ]
        deep = jnp.where(lane < SPARE, thirds[0], jnp.where(lane < 2 * SPARE, thirds[1], thirds[2]))
        below, above = from_low[2 * c : 2 * c + 2, :], from_high[2 * c : 2 * c + 2, :]
        low_ref[6:7, :] = jnp.where(missing_low, -SIGN[c] * here[1:2], jnp.where(along, above[1:2], below[0:1]))
        low_ref[7:8, :] = jnp.where(missing_low, -SIGN[c] * here[0:1], jnp.where(along, above[0:1], below[1:2]))
        high_ref[0:1, :] = jnp.where(missing_high, -SIGN[c] * here[15:16], jnp.where(along, below[1:2], above[0:1]))
        high_ref[1:2, :] = jnp.where(missing_high, -SIGN[c] * here[14:15], jnp.where(along, below[0:1], above[1:2]))
        rows = jnp.concatenate([low_ref[...], here, high_ref[...]], axis=0)
        along_i = [shifted_rows(rows, s) for s in (-2, -1)] + [here] + [shifted_rows(rows, s) for s in (1, 2)]
        outer = lane < CROSS
        normal = [
            jnp.where(outer, pltpu.roll(mine, 80, 1), pltpu.roll(mine, 48, 1)),
            jnp.where(outer, mine, pltpu.roll(here, 48, 1)),
            here,
            jnp.where(outer, pltpu.roll(here, 80, 1), pltpu.roll(deep, 48, 1)),
            deep,
        ]
        raw = [pltpu.roll(here, (-s) % 128, 1) if s else here for s in range(-2, 3)]
        wall = SIGN[c] * here
        second = SIGN[c] * jnp.where((place == 0) | (place == 46), raw[3], raw[1])
        sideways = [
            jnp.where(place < 2, second, raw[0]),
            jnp.where(place == 0, wall, raw[1]),
            here,
            jnp.where(place == 47, wall, raw[3]),
            jnp.where(place >= 46, second, raw[4]),
        ]
        stencils.append((along_i, normal, sideways))
    geometry = [main[GEOMETRY + LEN * n : GEOMETRY + LEN * n + LEN, :] for n in range(9)]
    for c, values in enumerate(advance(stencils, geometry)):
        ghost_ref[LEN * c : LEN * c + LEN, :] = values


def chain_terms(q, metric, low_ref, high_ref, scale, tiles, base, out):
    row = lax.broadcasted_iota(jnp.int32, (8, 128), 0)
    for t in tiles:
        where = slice(128 * t, 128 * t + 128)
        for high in (False, True):
            half = slice(8, 16) if high else slice(0, 8)
            slopes, curves = [], []
            for c in range(4):
                if high:
                    ghost = high_ref[c, :, where]
                    first = jnp.where(row == 7, pltpu.roll(ghost, 1, 0), 0.0)
                    second = jnp.where(row >= 6, ghost, 0.0)
                    slopes.append(8.0 * first - second)
                else:
                    ghost = low_ref[c, :, where]
                    first = jnp.where(row == 0, pltpu.roll(ghost, 7, 0), 0.0)
                    second = jnp.where(row < 2, ghost, 0.0)
                    slopes.append(second - 8.0 * first)
                curves.append(16.0 * first - second)
            here = [q[c, half, where] for c in range(4)]
            added = edge_terms(here, [metric[n, half, where] for n in range(3)], slopes, curves, scale)
            for c in range(4):
                out[c, half, where] = base[c, half, where] + added[c]


def joint_terms(q, metric, ghost_ref, face, scale, tiles, out):
    lane = lanes_of(LEN)

    def add(t, direction, slopes, curves):
        where = slice(128 * t, 128 * t + 128)
        here = [q[c, :, where] for c in range(4)]
        geometry = [metric[3 * direction + n, :, where] for n in range(3)]
        added = edge_terms(here, geometry, slopes, curves, scale)
        for c in range(4):
            out[c, :, where] = out[c, :, where] + added[c]

    ghost_of = lambda c: ghost_ref[16 * c : 16 * c + 16, :]
    if tiles[0] == 0:

        @pl.when(face == 2)
        def _():
            slopes, curves = [], []
            for c in range(4):
                ghost = ghost_of(c)
                first = jnp.where(lane < CROSS, ghost, 0.0)
                second = jnp.where(lane < CROSS, pltpu.roll(ghost, 80, 1), pltpu.roll(ghost, 48, 1))
                second = jnp.where(lane < 2 * CROSS, second, 0.0)
                slopes.append(second - 8.0 * first)
                curves.append(16.0 * first - second)
            add(0, 1, slopes, curves)

    if tiles[-1] == TILES - 1:

        @pl.when(face == 3)
        def _():
            slopes, curves = [], []
            for c in range(4):
                ghost = ghost_of(c)
                first = jnp.where(lane >= 80, pltpu.roll(ghost, 80, 1), 0.0)
                second = jnp.where(lane >= 32, pltpu.roll(ghost, 32, 1), 0.0)
                slopes.append(8.0 * first - second)
                curves.append(16.0 * first - second)
            add(TILES - 1, 1, slopes, curves)

    @pl.when(face >= 4)
    def _():
        toward = jnp.where(face == 4, -1.0, 1.0)
        for t in tiles:
            flat = 128 * t + lane
            j = flat // CROSS
            k = flat - j * CROSS
            depth = jnp.where(face == 4, k, CROSS - 1 - k)
            far = jnp.where(depth == 0, j + CROSS, j)[:8]
            slopes, curves = [], []
            for c in range(4):
                ghost = ghost_of(c)
                first = jnp.where(depth == 0, gather_lanes(ghost, j[:8]), 0.0)
                second = jnp.where(depth < 2, gather_lanes(ghost, far), 0.0)
                slopes.append(toward * (8.0 * first - second))
                curves.append(16.0 * first - second)
            add(t, 2, slopes, curves)


def joint_kernel(bulk, q, metric, one, two, three, mate, meta, out, below_out, above_out, ghost_ref):
    received = (mate, one, two, three)
    copy_part(meta[OWN], received, (0, GEOMETRY), ghost_ref)
    copy_part(meta[OWN + 1], received, PARTS[1], below_out)
    copy_part(meta[OWN + 2], received, PARTS[2], above_out)
    out[...] = bulk[...]
    joint_terms(q, metric, ghost_ref, meta[FACE], 1.0, range(TILES), out)


def spread_ghosts(even_in, odd_in, meta, low_ref, high_ref):
    even = lax.rem(meta[POSITION], 2) == 0
    has_low = jnp.where(meta[HAS_LOW] == 1, 1.0, 0.0)
    has_high = jnp.where(meta[HAS_HIGH] == 1, 1.0, 0.0)
    for c in range(4):
        rows = slice(2 * c, 2 * c + 2)
        from_even, from_odd = even_in[rows, 0:CELLS], odd_in[rows, 0:CELLS]
        low_ref[c, 0:2, :] = has_low * jnp.where(even, from_odd, from_even)
        high_ref[c, 6:8, :] = has_high * jnp.where(even, from_even, from_odd)


def chain_kernel(part, q, metric, below, above, even_in, odd_in, meta, out, even_ref, odd_ref, low_ref, high_ref):
    spread_ghosts(even_in, odd_in, meta, low_ref, high_ref)
    chain_terms(q, metric, low_ref, high_ref, 1.0, range(TILES), part, out)
    write_chain(out, even_ref, odd_ref, meta[POSITION])
    even = lax.rem(meta[POSITION], 2) == 0
    spare = slice(CELLS, CELLS + 128)
    even_ref[:, spare] = jnp.where(even, above[...], below[...])
    odd_ref[:, spare] = jnp.where(even, below[...], above[...])


def last_kernel(part, sent, q, metric, one, two, three, mate, even_in, odd_in, meta, out_hbm, *scratch):
    low_ref, high_ref, ghost_ref, main, first_low, first_high, out, sem = scratch
    even = lax.rem(meta[POSITION], 2) == 0
    copy_part(meta[OWN], (mate, one, two, three), PARTS[0], main)
    spare = slice(CELLS, CELLS + 128)
    from_even, from_odd = even_in[:, spare], odd_in[:, spare]
    from_low, from_high = jnp.where(even, from_odd, from_even), jnp.where(even, from_even, from_odd)
    partner_face(sent, main, first_low, first_high, from_low, from_high, meta, ghost_ref)
    spread_ghosts(even_in, odd_in, meta, low_ref, high_ref)
    copies = []
    for n in range(TILES // GROUP):
        tiles = range(GROUP * n, GROUP * n + GROUP)
        chain_terms(q, metric, low_ref, high_ref, 0.5, tiles, part, out)
        joint_terms(q, metric, ghost_ref, meta[FACE], 0.5, tiles, out)
        where = slice(128 * GROUP * n, 128 * GROUP * (n + 1))
        copies.append(pltpu.make_async_copy(out.at[:, :, where], out_hbm.at[:, :, where], sem.at[n]))
        copies[-1].start()
    for copy in copies:
        copy.wait()


f32 = functools.partial(jax.ShapeDtypeStruct, dtype=jnp.float32)
PARAMS = pltpu.CompilerParams(vmem_limit_bytes=24 * 1024 * 1024)
FIELD = f32((4, LEN, CELLS))
JOINT = f32((ROWS, 128))
HALO = [pltpu.VMEM((4, 8, CELLS), jnp.float32)] * 2 + [pltpu.VMEM((64, 128), jnp.float32)]
TILE = pltpu.VMEM((8, 128), jnp.float32)


def local(kernel, shapes, operands, scratch=(), flops=1_000_000, **options):
    options.setdefault("out_specs", [VMEM] * len(shapes))
    return pl.pallas_call(
        kernel,
        out_shape=shapes,
        in_specs=[VMEM] * (len(operands) - 1) + [SMEM],
        scratch_shapes=list(scratch),
        compiler_params=PARAMS,
        cost_estimate=pl.CostEstimate(flops=flops, bytes_accessed=flops, transcendentals=0),
        **options,
    )(*operands)


def bulk(last, chains, *operands):
    shapes = [FIELD] + ([f32((8, CELLS))] * 2 if chains else [])
    return local(functools.partial(bulk_kernel, last), shapes, operands, flops=12_000_000)


def along_chain(even, odd):
    from_even = lax.ppermute(even, "blk", [(i, i ^ 1) for i in range(CHAIN)])
    pairs = [(i, i + 1) for i in range(1, CHAIN - 1, 2)]
    return from_even, lax.ppermute(odd, "blk", pairs + [(b, a) for a, b in pairs])


def on_device(state, metric, block_map, links):
    HBM = pl.BlockSpec(memory_space=pltpu.HBM)
    held = lambda x: pltpu.with_memory_space_constraint(x, pltpu.HBM)
    arrays = (state.reshape(4, LEN, CELLS), metric.reshape(9, LEN, CELLS), block_map, jnp.transpose(links, (1, 2, 0)))
    q, geometry, joint, meta = pl.pallas_call(
        first_kernel,
        out_shape=[FIELD, f32((9, LEN, CELLS)), JOINT, jax.ShapeDtypeStruct((16,), jnp.int32)],
        in_specs=[HBM] * 4,
        out_specs=[VMEM] * 3 + [SMEM],
        scratch_shapes=[
            pltpu.SMEM((SEGS * CHAIN,), jnp.int32),
            pltpu.SMEM((6, 4, SEGS * CHAIN), jnp.int32),
            pltpu.SemaphoreType.DMA((4,)),
        ],
        compiler_params=PARAMS,
    )(*map(held, arrays))
    one, two, three = (
        lax.ppermute(joint, "seg", [(i, i ^ s) for i in range(SEGS)]) for s in (1, 2, 3)
    )
    part, even, odd = bulk(False, True, q, geometry, meta)
    one, two, three, even, odd, part = lax.optimization_barrier((one, two, three, even, odd, part))
    (picked,) = local(pick_kernel, [JOINT], (joint, one, two, three, meta))
    mate = lax.ppermute(picked, "seg", [(i, i ^ 4) for i in range(SEGS)])
    from_even, from_odd = along_chain(even, odd)
    part, below, above = local(
        joint_kernel,
        [FIELD] + [f32((8, 128))] * 2,
        (part, q, geometry, one, two, three, mate, meta),
        HALO[2:],
    )
    q1, even, odd = local(
        chain_kernel,
        [FIELD] + [f32((8, CELLS + 128))] * 2,
        (part, q, geometry, below, above, from_even, from_odd, meta),
        HALO[:2],
    )
    from_even, from_odd = along_chain(even, odd)
    (part,) = bulk(True, False, q1, geometry, q, meta)
    (advanced,) = local(
        last_kernel,
        [FIELD],
        (part, joint, q1, geometry, one, two, three, mate, from_even, from_odd, meta),
        HALO
        + [pltpu.VMEM((BELOW, 128), jnp.float32), TILE, TILE, pltpu.VMEM((4, LEN, CELLS), jnp.float32)]
        + [pltpu.SemaphoreType.DMA((TILES // GROUP,))],
        out_specs=[HBM],
    )
    return advanced.reshape(state.shape)


def solution(mesh):
    in_specs = (P(("seg", "blk"), None, None, None), P(("seg", "blk"), None, None, None), P(), P())
    out_specs = P(("seg", "blk"), None, None, None)
    return jax.shard_map(
        on_device, mesh=mesh, in_specs=in_specs, out_specs=out_specs, check_vma=False
    )
```

```python
import functools
import jax
import jax.numpy as jnp
from jax import lax
from jax.experimental import pallas as pl
from jax.experimental.pallas import tpu as pltpu
from jax.sharding import PartitionSpec as P

LEN, CROSS, CELLS, TILES = 16, 48, 2304, 18
GROUP = 6
GEOMETRY, BELOW, ABOVE, ROWS = 64, 208, 216, 224
USED, SPARE = 96, 32
FACE, ALONG, ACROSS, POSITION, HAS_LOW, HAS_HIGH, OWN, MATE = 0, 1, 2, 3, 4, 5, 6, 9
PARTS = ((0, BELOW), (BELOW, ABOVE), (ABOVE, ROWS))
SEGS, CHAIN = 8, 32
time_step = 0.05
viscosity = 0.2
compress = 1.0
SIGN = (-1.0, -1.0, -1.0, 1.0)
VMEM = pl.BlockSpec(memory_space=pltpu.VMEM)
SMEM = pl.BlockSpec(memory_space=pltpu.SMEM)


def lanes_of(rows=8):
    return lax.broadcasted_iota(jnp.int32, (rows, 128), 1)


def gather_lanes(values, index):
    parts = [
        jnp.take_along_axis(values[r : r + 8], index, axis=1, mode="promise_in_bounds")
        for r in range(0, values.shape[0], 8)
    ]
    return parts[0] if len(parts) == 1 else jnp.concatenate(parts, axis=0)


def reversed_rows(values):
    index = 7 - lax.broadcasted_iota(jnp.int32, (8, 128), 0)
    flip = lambda part: jnp.take_along_axis(part, index, axis=0, mode="promise_in_bounds")
    return jnp.concatenate([flip(values[8:16]), flip(values[0:8])], axis=0)


def joined_face(device, block_map, links):
    block = block_map[device]
    face, partner, along, across = jnp.int32(0), jnp.int32(-1), jnp.int32(0), jnp.int32(0)
    for side in range(2, 6):
        other = links[side, 0, block]
        here = other >= 0
        face = jnp.where(here, side, face)
        partner = jnp.where(here, other, partner)
        along = jnp.where(here, links[side, 2, block], along)
        across = jnp.where(here, links[side, 3, block], across)
    position = lax.rem(device, CHAIN)
    segment = jnp.int32(0)
    for s in range(SEGS):
        segment = jnp.where(block_map[s * CHAIN + position] == partner, s, segment)
    return face, segment, along, across


def face_source(face, across, first_layer):
    lane = lanes_of()
    layer = jnp.where(lane >= CROSS, 1, 0)
    place = lane - layer * CROSS
    place = jnp.where(across == 1, CROSS - 1 - place, place)
    depth = first_layer + layer
    depth = jnp.where((face == 3) | (face == 5), CROSS - 1 - depth, depth)
    return jnp.where(face <= 3, depth * CROSS + place, place * CROSS + depth)


def gather_face(load, source):
    index, owner = source & 127, source >> 7
    found = None
    for t in range(TILES):
        picked = gather_lanes(load(t), index)
        if found is None:
            found = picked
        else:
            inside = owner == t
            if picked.shape[0] == LEN:
                inside = jnp.concatenate([inside, inside], axis=0)
            found = jnp.where(inside, picked, found)
    return found


def write_chain(field, even_ref, odd_ref, position):
    even = lax.rem(position, 2) == 0
    for c in range(4):
        low, high = field[c, 0:2, :], field[c, LEN - 2 : LEN, :]
        even_ref[2 * c : 2 * c + 2, 0:CELLS] = jnp.where(even, high, low)
        odd_ref[2 * c : 2 * c + 2, 0:CELLS] = jnp.where(even, low, high)


def first_kernel(
    q_hbm, metric_hbm, map_hbm, links_hbm, q, metric, joint_ref, even_ref, odd_ref, meta, block_map, links, sem
):
    copies = [
        pltpu.make_async_copy(source, target, sem.at[n])
        for n, (source, target) in enumerate(
            ((links_hbm, links), (map_hbm, block_map), (q_hbm, q), (metric_hbm, metric))
        )
    ]
    for copy in copies:
        copy.start()
    segment, position = lax.axis_index("seg"), lax.axis_index("blk")
    copies[0].wait()
    copies[1].wait()
    here = segment * CHAIN + position
    other = (segment ^ 4) * CHAIN + position
    before, after = jnp.where(position > 0, -1, 0), jnp.where(position < CHAIN - 1, 1, 0)
    face, partner, along, across = joined_face(here, block_map, links)
    low_face, low_partner, _, low_across = joined_face(here + before, block_map, links)
    high_face, high_partner, _, high_across = joined_face(here + after, block_map, links)
    own = (partner, low_partner, high_partner)
    mates = [joined_face(other + shift, block_map, links)[1] for shift in (0, before, after)]
    meta[FACE] = face
    meta[ALONG] = along
    meta[ACROSS] = across
    meta[POSITION] = position
    block = block_map[here]
    meta[HAS_LOW] = jnp.where(links[0, 0, block] >= 0, 1, 0)
    meta[HAS_HIGH] = jnp.where(links[1, 0, block] >= 0, 1, 0)
    for n in range(3):
        meta[OWN + n] = jnp.where(own[n] // 4 == segment // 4, (own[n] ^ segment) & 3, 0)
        meta[MATE + n] = (mates[n] ^ segment) & 3
    copies[2].wait()
    write_chain(q, even_ref, odd_ref, position)

    where = lambda t: slice(128 * t, 128 * t + 128)
    lane = lanes_of(LEN)
    near, deep = face_source(face, across, 0), face_source(face, across, 2)
    below, above = face_source(low_face, low_across, 0), face_source(high_face, high_across, 0)
    deeper = [gather_face(lambda t: q[c, :, where(t)], deep) for c in range(4)]

    def put(n, values):
        if n < 12:
            third = pltpu.roll(deeper[n // 3], USED - SPARE * (n % 3), 1)
            values = jnp.where(lane < USED, values, third)
        joint_ref[LEN * n : LEN * n + LEN, :] = jnp.where(along == 1, reversed_rows(values), values)

    for c in range(4):
        put(c, gather_face(lambda t: q[c, :, where(t)], near))
        low_rows = gather_face(lambda t: q[c, 0:8, where(t)], below)
        joint_ref[BELOW + 2 * c : BELOW + 2 * c + 2, :] = low_rows[0:2]
        high_rows = gather_face(lambda t: q[c, 8:16, where(t)], above)
        joint_ref[ABOVE + 2 * c : ABOVE + 2 * c + 2, :] = high_rows[6:8]
    copies[3].wait()
    normal = jnp.where(face <= 3, 1, 2)
    inward = jnp.where((face == 3) | (face == 5), -1.0, 1.0)
    forward = jnp.where(along == 1, -1.0, 1.0)
    sideways = jnp.where(across == 1, -1.0, 1.0)
    for a, (row, sign) in enumerate(((0, forward), (3 * normal, inward), (3 * (3 - normal), sideways))):
        for b in range(3):
            found = gather_face(lambda t: metric[row + b, :, where(t)], near)
            put(4 + 3 * a + b, sign * found)


def copy_part(choice, refs, rows, out):
    for n, ref in enumerate(refs):

        @pl.when(choice == n)
        def _(ref=ref):
            out[...] = ref[rows[0] : rows[1], :]


def pick_kernel(own, one, two, three, meta, out):
    for n, rows in enumerate(PARTS):
        copy_part(meta[MATE + n], (own, one, two, three), rows, out.at[rows[0] : rows[1], :])


def shifted_lanes(before, here, after, shift):
    lane = lanes_of(LEN)
    if shift > 0:
        return jnp.where(
            lane < 128 - shift, pltpu.roll(here, 128 - shift, 1), pltpu.roll(after, 128 - shift, 1)
        )
    return jnp.where(lane >= -shift, pltpu.roll(here, -shift, 1), pltpu.roll(before, -shift, 1))


def shifted_rows(padded, shift):
    return pltpu.roll(padded, (-shift) % 32, 0)[8:24]


def differences(m2, m1, here, p1, p2):
    return 8.0 * (p1 - m1) - (p2 - m2)


def bends(m2, m1, here, p1, p2):
    return 16.0 * (p1 + m1) - (p2 + m2) - 30.0 * here


def advance(stencils, geometry):
    here = [stencils[c][0][2] for c in range(4)]
    moves = [-(time_step / 12.0) * geometry[n] for n in range(9)]
    result = list(here)
    fall = None
    for a in range(3):
        g = geometry[3 * a : 3 * a + 3]
        n = moves[3 * a : 3 * a + 3]
        speed = n[0] * here[0] + n[1] * here[1] + n[2] * here[2]
        spread = (viscosity * time_step / 12.0) * (g[0] * g[0] + g[1] * g[1] + g[2] * g[2])
        drop = differences(*stencils[3][a])
        for b in range(3):
            slope = differences(*stencils[b][a])
            result[b] = result[b] + speed * slope + n[b] * drop + spread * bends(*stencils[b][a])
            term = n[b] * slope
            fall = term if fall is None else fall + term
    result[3] = result[3] + compress * fall
    return result


def chain_ghosts(q, even_in, odd_in, meta, low_ref, high_ref):
    even = lax.rem(meta[POSITION], 2) == 0
    for c in range(4):
        rows = slice(2 * c, 2 * c + 2)
        from_even, from_odd = even_in[rows, :], odd_in[rows, :]
        low_ref[c, 6:8, :] = jnp.where(even, from_odd, from_even)
        high_ref[c, 0:2, :] = jnp.where(even, from_even, from_odd)

    @pl.when(meta[HAS_LOW] == 0)
    def _():
        for c in range(4):
            low_ref[c, 7:8, :] = -SIGN[c] * q[c, 0:1, :]
            low_ref[c, 6:7, :] = -SIGN[c] * q[c, 1:2, :]

    @pl.when(meta[HAS_HIGH] == 0)
    def _():
        for c in range(4):
            high_ref[c, 0:1, :] = -SIGN[c] * q[c, LEN - 1 : LEN, :]
            high_ref[c, 1:2, :] = -SIGN[c] * q[c, LEN - 2 : LEN - 1, :]


def bulk_kernel(last, q, metric, *rest):
    if last:
        first, meta, out = rest
    else:
        even_in, odd_in, meta, out, low_ref, high_ref = rest
        chain_ghosts(q, even_in, odd_in, meta, low_ref, high_ref)
    lane = lanes_of(LEN)
    row = lax.broadcasted_iota(jnp.int32, (8, 128), 0)
    face, ends = meta[FACE], (meta[HAS_LOW] == 0, meta[HAS_HIGH] == 0)
    load = lambda c, t: q[c, :, 128 * t : 128 * t + 128]
    before_first, after_last = [], []
    for c in range(4):
        head = jnp.where(face == 2, 0.0, SIGN[c]) * load(c, 0)
        before_first.append(jnp.where(lane >= 80, pltpu.roll(head, 80, 1), pltpu.roll(head, 112, 1)))
        tail = jnp.where(face == 3, 0.0, SIGN[c]) * load(c, TILES - 1)
        after_last.append(jnp.where(lane < CROSS, pltpu.roll(tail, 48, 1), pltpu.roll(tail, 16, 1)))

    def tile(c, t):
        return before_first[c] if t < 0 else after_last[c] if t >= TILES else load(c, t)

    low_scale = jnp.where(face == 4, 0.0, 1.0)
    high_scale = jnp.where(face == 5, 0.0, 1.0)
    open_low = jnp.where(ends[0], 1.0, 0.0)
    open_high = jnp.where(ends[1], 1.0, 0.0)
    for t in range(TILES):
        flat = 128 * t + lane
        k = flat - (flat // CROSS) * CROSS
        scale = jnp.where(k < 2, low_scale, high_scale)
        where = slice(128 * t, 128 * t + 128)
        stencils = []
        for c in range(4):
            before, here, after = tile(c, t - 1), tile(c, t), tile(c, t + 1)
            if last:
                top, bottom = here[0:8], here[8:16]
                low = -SIGN[c] * open_low * jnp.where(row == 7, pltpu.roll(top, 7, 0), pltpu.roll(top, 5, 0))
                high = -SIGN[c] * open_high * jnp.where(row == 0, pltpu.roll(bottom, 1, 0), pltpu.roll(bottom, 3, 0))
            else:
                low, high = low_ref[c, :, where], high_ref[c, :, where]
            rows = jnp.concatenate([low, here, high], axis=0)
            along_i = [shifted_rows(rows, s) for s in (-2, -1)] + [here] + [shifted_rows(rows, s) for s in (1, 2)]
            along_j = [shifted_lanes(before, here, after, CROSS * s) if s else here for s in range(-2, 3)]
            raw = [shifted_lanes(before, here, after, s) if s else here for s in range(-2, 3)]
            factor = SIGN[c] * scale
            nearest = factor * here
            second = factor * jnp.where((k == 0) | (k == 46), raw[3], raw[1])
            along_k = [
                jnp.where(k < 2, second, raw[0]),
                jnp.where(k == 0, nearest, raw[1]),
                here,
                jnp.where(k == 47, nearest, raw[3]),
                jnp.where(k >= 46, second, raw[4]),
            ]
            stencils.append((along_i, along_j, along_k))
        values = advance(stencils, [metric[n, :, where] for n in range(9)])
        for c in range(4):
            kept = 0.5 * first[c, :, where] + 0.5 * values[c] if last else values[c]
            out[c, :, where] = kept


def edge_terms(here, geometry, slopes, curves, scale):
    moves = [-(scale * time_step / 12.0) * g for g in geometry]
    speed = moves[0] * here[0] + moves[1] * here[1] + moves[2] * here[2]
    squares = geometry[0] * geometry[0] + geometry[1] * geometry[1] + geometry[2] * geometry[2]
    spread = (scale * viscosity * time_step / 12.0) * squares
    added = [speed * slopes[b] + moves[b] * slopes[3] + spread * curves[b] for b in range(3)]
    added.append(compress * (moves[0] * slopes[0] + moves[1] * slopes[1] + moves[2] * slopes[2]))
    return added


def partner_face(sent, main, low_ref, high_ref, from_low, from_high, meta, ghost_ref):
    lane = lanes_of(LEN)
    place = jnp.where(lane >= CROSS, lane - CROSS, lane)
    along, across = meta[ALONG] == 1, meta[ACROSS] == 1
    missing_low = jnp.where(along, meta[HAS_HIGH], meta[HAS_LOW]) == 0
    missing_high = jnp.where(along, meta[HAS_LOW], meta[HAS_HIGH]) == 0
    mirrored = jnp.where(lane < CROSS, CROSS - 1 - lane, jnp.where(lane < 2 * CROSS, 3 * CROSS - 1 - lane, lane))[:8]
    stencils = []
    for c in range(4):
        mine = sent[LEN * c : LEN * c + LEN, :]
        mine = jnp.where(across, gather_lanes(mine, mirrored), mine)
        mine = jnp.where(along, reversed_rows(mine), mine)
        here = main[LEN * c : LEN * c + LEN, :]
        thirds = [
            pltpu.roll(main[LEN * n : LEN * n + LEN, :], (SPARE * (n % 3) - USED) % 128, 1) for n in range(3 * c, 3 * c + 3)
        ]
        deep = jnp.where(lane < SPARE, thirds[0], jnp.where(lane < 2 * SPARE, thirds[1], thirds[2]))
        below, above = from_low[2 * c : 2 * c + 2, :], from_high[2 * c : 2 * c + 2, :]
        low_ref[6:7, :] = jnp.where(missing_low, -SIGN[c] * here[1:2], jnp.where(along, above[1:2], below[0:1]))
        low_ref[7:8, :] = jnp.where(missing_low, -SIGN[c] * here[0:1], jnp.where(along, above[0:1], below[1:2]))
        high_ref[0:1, :] = jnp.where(missing_high, -SIGN[c] * here[15:16], jnp.where(along, below[1:2], above[0:1]))
        high_ref[1:2, :] = jnp.where(missing_high, -SIGN[c] * here[14:15], jnp.where(along, below[0:1], above[1:2]))
        rows = jnp.concatenate([low_ref[...], here, high_ref[...]], axis=0)
        along_i = [shifted_rows(rows, s) for s in (-2, -1)] + [here] + [shifted_rows(rows, s) for s in (1, 2)]
        outer = lane < CROSS
        normal = [
            jnp.where(outer, pltpu.roll(mine, 80, 1), pltpu.roll(mine, 48, 1)),
            jnp.where(outer, mine, pltpu.roll(here, 48, 1)),
            here,
            jnp.where(outer, pltpu.roll(here, 80, 1), pltpu.roll(deep, 48, 1)),
            deep,
        ]
        raw = [pltpu.roll(here, (-s) % 128, 1) if s else here for s in range(-2, 3)]
        wall = SIGN[c] * here
        second = SIGN[c] * jnp.where((place == 0) | (place == 46), raw[3], raw[1])
        sideways = [
            jnp.where(place < 2, second, raw[0]),
            jnp.where(place == 0, wall, raw[1]),
            here,
            jnp.where(place == 47, wall, raw[3]),
            jnp.where(place >= 46, second, raw[4]),
        ]
        stencils.append((along_i, normal, sideways))
    geometry = [main[GEOMETRY + LEN * n : GEOMETRY + LEN * n + LEN, :] for n in range(9)]
    for c, values in enumerate(advance(stencils, geometry)):
        ghost_ref[LEN * c : LEN * c + LEN, :] = values


def chain_terms(q, metric, chain_ref, scale, tiles, base, out):
    row = lax.broadcasted_iota(jnp.int32, (8, 128), 0)
    start = row < 4
    toward = jnp.where(start, -1.0, 1.0)
    for t in tiles:
        where = slice(128 * t, 128 * t + 128)
        ends = lambda ref, n: jnp.where(start, ref[n, 0:8, where], ref[n, 8:16, where])
        slopes, curves = [], []
        for c in range(4):
            second = chain_ref[c, :, where]
            first = jnp.where(row == 0, pltpu.roll(second, 7, 0), jnp.where(row == 7, pltpu.roll(second, 1, 0), 0.0))
            slopes.append(toward * (8.0 * first - second))
            curves.append(16.0 * first - second)
        added = edge_terms([ends(q, c) for c in range(4)], [ends(metric, n) for n in range(3)], slopes, curves, scale)
        for c in range(4):
            out[c, 0:8, where] = base[c, 0:8, where] + jnp.where(start, added[c], 0.0)
            out[c, 8:16, where] = base[c, 8:16, where] + jnp.where(start, 0.0, added[c])


def joint_terms(q, metric, ghost_ref, face, scale, tiles, out):
    lane = lanes_of(LEN)

    def add(t, direction, slopes, curves):
        where = slice(128 * t, 128 * t + 128)
        here = [q[c, :, where] for c in range(4)]
        geometry = [metric[3 * direction + n, :, where] for n in range(3)]
        added = edge_terms(here, geometry, slopes, curves, scale)
        for c in range(4):
            out[c, :, where] = out[c, :, where] + added[c]

    ghost_of = lambda c: ghost_ref[16 * c : 16 * c + 16, :]
    if tiles[0] == 0:

        @pl.when(face == 2)
        def _():
            slopes, curves = [], []
            for c in range(4):
                ghost = ghost_of(c)
                first = jnp.where(lane < CROSS, ghost, 0.0)
                second = jnp.where(lane < CROSS, pltpu.roll(ghost, 80, 1), pltpu.roll(ghost, 48, 1))
                second = jnp.where(lane < 2 * CROSS, second, 0.0)
                slopes.append(second - 8.0 * first)
                curves.append(16.0 * first - second)
            add(0, 1, slopes, curves)

    if tiles[-1] == TILES - 1:

        @pl.when(face == 3)
        def _():
            slopes, curves = [], []
            for c in range(4):
                ghost = ghost_of(c)
                first = jnp.where(lane >= 80, pltpu.roll(ghost, 80, 1), 0.0)
                second = jnp.where(lane >= 32, pltpu.roll(ghost, 32, 1), 0.0)
                slopes.append(8.0 * first - second)
                curves.append(16.0 * first - second)
            add(TILES - 1, 1, slopes, curves)

    @pl.when(face >= 4)
    def _():
        toward = jnp.where(face == 4, -1.0, 1.0)
        for t in tiles:
            flat = 128 * t + lane
            j = flat // CROSS
            k = flat - j * CROSS
            depth = jnp.where(face == 4, k, CROSS - 1 - k)
            far = jnp.where(depth == 0, j + CROSS, j)[:8]
            slopes, curves = [], []
            for c in range(4):
                ghost = ghost_of(c)
                first = jnp.where(depth == 0, gather_lanes(ghost, j[:8]), 0.0)
                second = jnp.where(depth < 2, gather_lanes(ghost, far), 0.0)
                slopes.append(toward * (8.0 * first - second))
                curves.append(16.0 * first - second)
            add(t, 2, slopes, curves)


def joint_kernel(bulk, q, metric, one, two, three, mate, meta, out, even_ref, odd_ref, ghost_ref, below, above):
    received = (mate, one, two, three)
    copy_part(meta[OWN], received, (0, GEOMETRY), ghost_ref)
    copy_part(meta[OWN + 1], received, PARTS[1], below)
    copy_part(meta[OWN + 2], received, PARTS[2], above)
    out[...] = bulk[...]
    joint_terms(q, metric, ghost_ref, meta[FACE], 1.0, range(TILES), out)
    write_chain(out, even_ref, odd_ref, meta[POSITION])
    even = lax.rem(meta[POSITION], 2) == 0
    spare = slice(CELLS, CELLS + 128)
    even_ref[:, spare] = jnp.where(even, above[...], below[...])
    odd_ref[:, spare] = jnp.where(even, below[...], above[...])


def spread_ghosts(even_in, odd_in, meta, chain_ref):
    even = lax.rem(meta[POSITION], 2) == 0
    has_low = jnp.where(meta[HAS_LOW] == 1, 1.0, 0.0)
    has_high = jnp.where(meta[HAS_HIGH] == 1, 1.0, 0.0)
    for c in range(4):
        rows = slice(2 * c, 2 * c + 2)
        from_even, from_odd = even_in[rows, 0:CELLS], odd_in[rows, 0:CELLS]
        chain_ref[c, 2:6, :] = jnp.zeros((4, CELLS), jnp.float32)
        chain_ref[c, 0:2, :] = has_low * jnp.where(even, from_odd, from_even)
        chain_ref[c, 6:8, :] = has_high * jnp.where(even, from_even, from_odd)


def last_kernel(part, sent, q, metric, one, two, three, mate, even_in, odd_in, meta, out_hbm, *scratch):
    chain_ref, ghost_ref, main, first_low, first_high, out, sem = scratch
    even = lax.rem(meta[POSITION], 2) == 0
    copy_part(meta[OWN], (mate, one, two, three), PARTS[0], main)
    spare = slice(CELLS, CELLS + 128)
    from_even, from_odd = even_in[:, spare], odd_in[:, spare]
    from_low, from_high = jnp.where(even, from_odd, from_even), jnp.where(even, from_even, from_odd)
    partner_face(sent, main, first_low, first_high, from_low, from_high, meta, ghost_ref)
    spread_ghosts(even_in, odd_in, meta, chain_ref)
    copies = []
    for n in range(TILES // GROUP):
        tiles = range(GROUP * n, GROUP * n + GROUP)
        chain_terms(q, metric, chain_ref, 0.5, tiles, part, out)
        joint_terms(q, metric, ghost_ref, meta[FACE], 0.5, tiles, out)
        where = slice(128 * GROUP * n, 128 * GROUP * (n + 1))
        copies.append(pltpu.make_async_copy(out.at[:, :, where], out_hbm.at[:, :, where], sem.at[n]))
        copies[-1].start()
    for copy in copies:
        copy.wait()


f32 = functools.partial(jax.ShapeDtypeStruct, dtype=jnp.float32)
PARAMS = pltpu.CompilerParams(vmem_limit_bytes=24 * 1024 * 1024)
FIELD = f32((4, LEN, CELLS))
JOINT = f32((ROWS, 128))
CHAIN_TILES = pltpu.VMEM((4, 8, CELLS), jnp.float32)
GHOST = pltpu.VMEM((GEOMETRY, 128), jnp.float32)
TILE = pltpu.VMEM((8, 128), jnp.float32)


def local(kernel, shapes, operands, scratch=(), flops=1_000_000, **options):
    options.setdefault("out_specs", [VMEM] * len(shapes))
    return pl.pallas_call(
        kernel,
        out_shape=shapes,
        in_specs=[VMEM] * (len(operands) - 1) + [SMEM],
        scratch_shapes=list(scratch),
        compiler_params=PARAMS,
        cost_estimate=pl.CostEstimate(flops=flops, bytes_accessed=flops, transcendentals=0),
        **options,
    )(*operands)


def bulk(last, *operands):
    kernel = functools.partial(bulk_kernel, last)
    return local(kernel, [FIELD], operands, [] if last else [CHAIN_TILES] * 2, flops=12_000_000)[0]


def along_chain(even, odd):
    pairs = [(i, i + 1) for i in range(1, CHAIN - 1, 2)]
    from_odd = lax.ppermute(odd, "blk", pairs + [(b, a) for a, b in pairs])
    return lax.ppermute(even, "blk", [(i, i ^ 1) for i in range(CHAIN)]), from_odd


def on_device(state, metric, block_map, links):
    HBM = pl.BlockSpec(memory_space=pltpu.HBM)
    held = lambda x: pltpu.with_memory_space_constraint(x, pltpu.HBM)
    arrays = (state.reshape(4, LEN, CELLS), metric.reshape(9, LEN, CELLS), block_map, jnp.transpose(links, (1, 2, 0)))
    q, geometry, joint, even, odd, meta = pl.pallas_call(
        first_kernel,
        out_shape=[FIELD, f32((9, LEN, CELLS)), JOINT] + [f32((8, CELLS))] * 2 + [jax.ShapeDtypeStruct((16,), jnp.int32)],
        in_specs=[HBM] * 4,
        out_specs=[VMEM] * 5 + [SMEM],
        scratch_shapes=[
            pltpu.SMEM((SEGS * CHAIN,), jnp.int32),
            pltpu.SMEM((6, 4, SEGS * CHAIN), jnp.int32),
            pltpu.SemaphoreType.DMA((4,)),
        ],
        compiler_params=PARAMS,
    )(*map(held, arrays))
    one, two, three = (
        lax.ppermute(joint, "seg", [(i, i ^ s) for i in range(SEGS)]) for s in (1, 2, 3)
    )
    from_even, from_odd = along_chain(even, odd)
    one, two, three, from_odd = lax.optimization_barrier((one, two, three, from_odd))
    (picked,) = local(pick_kernel, [JOINT], (joint, one, two, three, meta))
    mate = lax.ppermute(picked, "seg", [(i, i ^ 4) for i in range(SEGS)])
    from_even, from_odd, _ = lax.optimization_barrier((from_even, from_odd, picked))
    part = bulk(False, q, geometry, from_even, from_odd, meta)
    q1, even, odd = local(
        joint_kernel,
        [FIELD] + [f32((8, CELLS + 128))] * 2,
        (part, q, geometry, one, two, three, mate, meta),
        [GHOST, TILE, TILE],
    )
    from_even, from_odd = along_chain(even, odd)
    part = bulk(True, q1, geometry, q, meta)
    (advanced,) = local(
        last_kernel,
        [FIELD],
        (part, joint, q1, geometry, one, two, three, mate, from_even, from_odd, meta),
        [CHAIN_TILES, GHOST, pltpu.VMEM((BELOW, 128), jnp.float32), TILE, TILE]
        + [pltpu.VMEM((4, LEN, CELLS), jnp.float32), pltpu.SemaphoreType.DMA((TILES // GROUP,))],
        out_specs=[HBM],
    )
    return advanced.reshape(state.shape)


def solution(mesh):
    in_specs = (P(("seg", "blk"), None, None, None), P(("seg", "blk"), None, None, None), P(), P())
    out_specs = P(("seg", "blk"), None, None, None)
    return jax.shard_map(
        on_device, mesh=mesh, in_specs=in_specs, out_specs=out_specs, check_vma=False
    )
```

```python
import functools
import jax
import jax.numpy as jnp
from jax import lax
from jax.experimental import pallas as pl
from jax.experimental.pallas import tpu as pltpu
from jax.sharding import PartitionSpec as P

LEN, CROSS, CELLS, TILES = 16, 48, 2304, 18
GROUP = 6
GEOMETRY, BELOW, ABOVE, ROWS = 64, 208, 216, 224
USED, SPARE = 96, 32
FACE, ALONG, ACROSS, POSITION, HAS_LOW, HAS_HIGH, OWN, MATE = 0, 1, 2, 3, 4, 5, 6, 9
PARTS = ((0, BELOW), (BELOW, ABOVE), (ABOVE, ROWS))
SEGS, CHAIN = 8, 32
time_step = 0.05
viscosity = 0.2
compress = 1.0
SIGN = (-1.0, -1.0, -1.0, 1.0)
VMEM = pl.BlockSpec(memory_space=pltpu.VMEM)
SMEM = pl.BlockSpec(memory_space=pltpu.SMEM)


def lanes_of(rows=8):
    return lax.broadcasted_iota(jnp.int32, (rows, 128), 1)


def gather_lanes(values, index):
    parts = [
        jnp.take_along_axis(values[r : r + 8], index, axis=1, mode="promise_in_bounds")
        for r in range(0, values.shape[0], 8)
    ]
    return parts[0] if len(parts) == 1 else jnp.concatenate(parts, axis=0)


def reversed_rows(values):
    index = 7 - lax.broadcasted_iota(jnp.int32, (8, 128), 0)
    flip = lambda part: jnp.take_along_axis(part, index, axis=0, mode="promise_in_bounds")
    return jnp.concatenate([flip(values[8:16]), flip(values[0:8])], axis=0)


def joined_face(device, block_map, links):
    block = block_map[device]
    face, partner, along, across = jnp.int32(0), jnp.int32(-1), jnp.int32(0), jnp.int32(0)
    for side in range(2, 6):
        other = links[side, 0, block]
        here = other >= 0
        face = jnp.where(here, side, face)
        partner = jnp.where(here, other, partner)
        along = jnp.where(here, links[side, 2, block], along)
        across = jnp.where(here, links[side, 3, block], across)
    position = lax.rem(device, CHAIN)
    segment = jnp.int32(0)
    for s in range(SEGS):
        segment = jnp.where(block_map[s * CHAIN + position] == partner, s, segment)
    return face, segment, along, across


def face_source(face, across, first_layer):
    lane = lanes_of()
    layer = jnp.where(lane >= CROSS, 1, 0)
    place = lane - layer * CROSS
    place = jnp.where(across == 1, CROSS - 1 - place, place)
    depth = first_layer + layer
    depth = jnp.where((face == 3) | (face == 5), CROSS - 1 - depth, depth)
    return jnp.where(face <= 3, depth * CROSS + place, place * CROSS + depth)


def gather_face(load, source):
    index, owner = source & 127, source >> 7
    found = None
    for t in range(TILES):
        picked = gather_lanes(load(t), index)
        if found is None:
            found = picked
        else:
            inside = owner == t
            if picked.shape[0] == LEN:
                inside = jnp.concatenate([inside, inside], axis=0)
            found = jnp.where(inside, picked, found)
    return found


def write_chain(field, even_ref, odd_ref, position):
    even = lax.rem(position, 2) == 0
    for c in range(4):
        low, high = field[c, 0:2, :], field[c, LEN - 2 : LEN, :]
        even_ref[2 * c : 2 * c + 2, 0:CELLS] = jnp.where(even, high, low)
        odd_ref[2 * c : 2 * c + 2, 0:CELLS] = jnp.where(even, low, high)


def first_kernel(
    q_hbm, metric_hbm, map_hbm, links_hbm, q, metric, joint_ref, even_ref, odd_ref, meta, block_map, links, sem
):
    copies = [
        pltpu.make_async_copy(source, target, sem.at[n])
        for n, (source, target) in enumerate(
            ((links_hbm, links), (map_hbm, block_map), (q_hbm, q), (metric_hbm, metric))
        )
    ]
    for copy in copies:
        copy.start()
    segment, position = lax.axis_index("seg"), lax.axis_index("blk")
    copies[0].wait()
    copies[1].wait()
    here = segment * CHAIN + position
    other = (segment ^ 4) * CHAIN + position
    before, after = jnp.where(position > 0, -1, 0), jnp.where(position < CHAIN - 1, 1, 0)
    face, partner, along, across = joined_face(here, block_map, links)
    low_face, low_partner, _, low_across = joined_face(here + before, block_map, links)
    high_face, high_partner, _, high_across = joined_face(here + after, block_map, links)
    own = (partner, low_partner, high_partner)
    mates = [joined_face(other + shift, block_map, links)[1] for shift in (0, before, after)]
    meta[FACE] = face
    meta[ALONG] = along
    meta[ACROSS] = across
    meta[POSITION] = position
    block = block_map[here]
    meta[HAS_LOW] = jnp.where(links[0, 0, block] >= 0, 1, 0)
    meta[HAS_HIGH] = jnp.where(links[1, 0, block] >= 0, 1, 0)
    for n in range(3):
        meta[OWN + n] = jnp.where(own[n] // 4 == segment // 4, (own[n] ^ segment) & 3, 0)
        meta[MATE + n] = (mates[n] ^ segment) & 3
    copies[2].wait()
    write_chain(q, even_ref, odd_ref, position)

    where = lambda t: slice(128 * t, 128 * t + 128)
    lane = lanes_of(LEN)
    near, deep = face_source(face, across, 0), face_source(face, across, 2)
    below, above = face_source(low_face, low_across, 0), face_source(high_face, high_across, 0)
    deeper = [gather_face(lambda t: q[c, :, where(t)], deep) for c in range(4)]

    def put(n, values):
        if n < 12:
            third = pltpu.roll(deeper[n // 3], USED - SPARE * (n % 3), 1)
            values = jnp.where(lane < USED, values, third)
        joint_ref[LEN * n : LEN * n + LEN, :] = jnp.where(along == 1, reversed_rows(values), values)

    for c in range(4):
        put(c, gather_face(lambda t: q[c, :, where(t)], near))
        low_rows = gather_face(lambda t: q[c, 0:8, where(t)], below)
        joint_ref[BELOW + 2 * c : BELOW + 2 * c + 2, :] = low_rows[0:2]
        high_rows = gather_face(lambda t: q[c, 8:16, where(t)], above)
        joint_ref[ABOVE + 2 * c : ABOVE + 2 * c + 2, :] = high_rows[6:8]
    copies[3].wait()
    normal = jnp.where(face <= 3, 1, 2)
    inward = jnp.where((face == 3) | (face == 5), -1.0, 1.0)
    forward = jnp.where(along == 1, -1.0, 1.0)
    sideways = jnp.where(across == 1, -1.0, 1.0)
    for a, (row, sign) in enumerate(((0, forward), (3 * normal, inward), (3 * (3 - normal), sideways))):
        for b in range(3):
            found = gather_face(lambda t: metric[row + b, :, where(t)], near)
            put(4 + 3 * a + b, sign * found)


def copy_part(choice, refs, rows, out):
    for n, ref in enumerate(refs):

        @pl.when(choice == n)
        def _(ref=ref):
            out[...] = ref[rows[0] : rows[1], :]


def pick_kernel(own, one, two, three, meta, out):
    for n, rows in enumerate(PARTS):
        copy_part(meta[MATE + n], (own, one, two, three), rows, out.at[rows[0] : rows[1], :])


def shifted_lanes(before, here, after, shift):
    lane = lanes_of(LEN)
    if shift > 0:
        return jnp.where(
            lane < 128 - shift, pltpu.roll(here, 128 - shift, 1), pltpu.roll(after, 128 - shift, 1)
        )
    return jnp.where(lane >= -shift, pltpu.roll(here, -shift, 1), pltpu.roll(before, -shift, 1))


def shifted_rows(padded, shift):
    return pltpu.roll(padded, (-shift) % 32, 0)[8:24]


def differences(m2, m1, here, p1, p2):
    return 8.0 * (p1 - m1) - (p2 - m2)


def bends(m2, m1, here, p1, p2):
    return 16.0 * (p1 + m1) - (p2 + m2) - 30.0 * here


def advance(stencils, geometry):
    here = [stencils[c][0][2] for c in range(4)]
    moves = [-(time_step / 12.0) * geometry[n] for n in range(9)]
    result = list(here)
    fall = None
    for a in range(3):
        g = geometry[3 * a : 3 * a + 3]
        n = moves[3 * a : 3 * a + 3]
        speed = n[0] * here[0] + n[1] * here[1] + n[2] * here[2]
        spread = (viscosity * time_step / 12.0) * (g[0] * g[0] + g[1] * g[1] + g[2] * g[2])
        drop = differences(*stencils[3][a])
        for b in range(3):
            slope = differences(*stencils[b][a])
            result[b] = result[b] + speed * slope + n[b] * drop + spread * bends(*stencils[b][a])
            term = n[b] * slope
            fall = term if fall is None else fall + term
    result[3] = result[3] + compress * fall
    return result


def chain_ghosts(q, even_in, odd_in, meta, low_ref, high_ref):
    even = lax.rem(meta[POSITION], 2) == 0
    for c in range(4):
        rows = slice(2 * c, 2 * c + 2)
        from_even, from_odd = even_in[rows, :], odd_in[rows, :]
        low_ref[c, 6:8, :] = jnp.where(even, from_odd, from_even)
        high_ref[c, 0:2, :] = jnp.where(even, from_even, from_odd)

    @pl.when(meta[HAS_LOW] == 0)
    def _():
        for c in range(4):
            low_ref[c, 7:8, :] = -SIGN[c] * q[c, 0:1, :]
            low_ref[c, 6:7, :] = -SIGN[c] * q[c, 1:2, :]

    @pl.when(meta[HAS_HIGH] == 0)
    def _():
        for c in range(4):
            high_ref[c, 0:1, :] = -SIGN[c] * q[c, LEN - 1 : LEN, :]
            high_ref[c, 1:2, :] = -SIGN[c] * q[c, LEN - 2 : LEN - 1, :]


def bulk_kernel(last, q, metric, *rest):
    if last:
        first, meta, out = rest
    else:
        even_in, odd_in, meta, out, low_ref, high_ref = rest
        chain_ghosts(q, even_in, odd_in, meta, low_ref, high_ref)
    lane = lanes_of(LEN)
    row = lax.broadcasted_iota(jnp.int32, (8, 128), 0)
    face, ends = meta[FACE], (meta[HAS_LOW] == 0, meta[HAS_HIGH] == 0)
    load = lambda c, t: q[c, :, 128 * t : 128 * t + 128]
    before_first, after_last = [], []
    for c in range(4):
        head = jnp.where(face == 2, 0.0, SIGN[c]) * load(c, 0)
        before_first.append(jnp.where(lane >= 80, pltpu.roll(head, 80, 1), pltpu.roll(head, 112, 1)))
        tail = jnp.where(face == 3, 0.0, SIGN[c]) * load(c, TILES - 1)
        after_last.append(jnp.where(lane < CROSS, pltpu.roll(tail, 48, 1), pltpu.roll(tail, 16, 1)))

    def tile(c, t):
        return before_first[c] if t < 0 else after_last[c] if t >= TILES else load(c, t)

    low_scale = jnp.where(face == 4, 0.0, 1.0)
    high_scale = jnp.where(face == 5, 0.0, 1.0)
    open_low = jnp.where(ends[0], 1.0, 0.0)
    open_high = jnp.where(ends[1], 1.0, 0.0)
    for t in range(TILES):
        flat = 128 * t + lane
        k = flat - (flat // CROSS) * CROSS
        scale = jnp.where(k < 2, low_scale, high_scale)
        where = slice(128 * t, 128 * t + 128)
        stencils = []
        for c in range(4):
            before, here, after = tile(c, t - 1), tile(c, t), tile(c, t + 1)
            if last:
                top, bottom = here[0:8], here[8:16]
                low = -SIGN[c] * open_low * jnp.where(row == 7, pltpu.roll(top, 7, 0), pltpu.roll(top, 5, 0))
                high = -SIGN[c] * open_high * jnp.where(row == 0, pltpu.roll(bottom, 1, 0), pltpu.roll(bottom, 3, 0))
            else:
                low, high = low_ref[c, :, where], high_ref[c, :, where]
            rows = jnp.concatenate([low, here, high], axis=0)
            along_i = [shifted_rows(rows, s) for s in (-2, -1)] + [here] + [shifted_rows(rows, s) for s in (1, 2)]
            along_j = [shifted_lanes(before, here, after, CROSS * s) if s else here for s in range(-2, 3)]
            raw = [shifted_lanes(before, here, after, s) if s else here for s in range(-2, 3)]
            factor = SIGN[c] * scale
            nearest = factor * here
            second = factor * jnp.where((k == 0) | (k == 46), raw[3], raw[1])
            along_k = [
                jnp.where(k < 2, second, raw[0]),
                jnp.where(k == 0, nearest, raw[1]),
                here,
                jnp.where(k == 47, nearest, raw[3]),
                jnp.where(k >= 46, second, raw[4]),
            ]
            stencils.append((along_i, along_j, along_k))
        values = advance(stencils, [metric[n, :, where] for n in range(9)])
        for c in range(4):
            kept = 0.5 * first[c, :, where] + 0.5 * values[c] if last else values[c]
            out[c, :, where] = kept


def edge_terms(here, geometry, slopes, curves, scale):
    moves = [-(scale * time_step / 12.0) * g for g in geometry]
    speed = moves[0] * here[0] + moves[1] * here[1] + moves[2] * here[2]
    squares = geometry[0] * geometry[0] + geometry[1] * geometry[1] + geometry[2] * geometry[2]
    spread = (scale * viscosity * time_step / 12.0) * squares
    added = [speed * slopes[b] + moves[b] * slopes[3] + spread * curves[b] for b in range(3)]
    added.append(compress * (moves[0] * slopes[0] + moves[1] * slopes[1] + moves[2] * slopes[2]))
    return added


def partner_face(sent, main, low_ref, high_ref, from_low, from_high, meta, ghost_ref):
    lane = lanes_of(LEN)
    place = jnp.where(lane >= CROSS, lane - CROSS, lane)
    along, across = meta[ALONG] == 1, meta[ACROSS] == 1
    missing_low = jnp.where(along, meta[HAS_HIGH], meta[HAS_LOW]) == 0
    missing_high = jnp.where(along, meta[HAS_LOW], meta[HAS_HIGH]) == 0
    mirrored = jnp.where(lane < CROSS, CROSS - 1 - lane, jnp.where(lane < 2 * CROSS, 3 * CROSS - 1 - lane, lane))[:8]
    stencils = []
    for c in range(4):
        mine = sent[LEN * c : LEN * c + LEN, :]
        mine = jnp.where(across, gather_lanes(mine, mirrored), mine)
        mine = jnp.where(along, reversed_rows(mine), mine)
        here = main[LEN * c : LEN * c + LEN, :]
        thirds = [
            pltpu.roll(main[LEN * n : LEN * n + LEN, :], (SPARE * (n % 3) - USED) % 128, 1) for n in range(3 * c, 3 * c + 3)
        ]
        deep = jnp.where(lane < SPARE, thirds[0], jnp.where(lane < 2 * SPARE, thirds[1], thirds[2]))
        below, above = from_low[2 * c : 2 * c + 2, :], from_high[2 * c : 2 * c + 2, :]
        low_ref[6:7, :] = jnp.where(missing_low, -SIGN[c] * here[1:2], jnp.where(along, above[1:2], below[0:1]))
        low_ref[7:8, :] = jnp.where(missing_low, -SIGN[c] * here[0:1], jnp.where(along, above[0:1], below[1:2]))
        high_ref[0:1, :] = jnp.where(missing_high, -SIGN[c] * here[15:16], jnp.where(along, below[1:2], above[0:1]))
        high_ref[1:2, :] = jnp.where(missing_high, -SIGN[c] * here[14:15], jnp.where(along, below[0:1], above[1:2]))
        rows = jnp.concatenate([low_ref[...], here, high_ref[...]], axis=0)
        along_i = [shifted_rows(rows, s) for s in (-2, -1)] + [here] + [shifted_rows(rows, s) for s in (1, 2)]
        outer = lane < CROSS
        normal = [
            jnp.where(outer, pltpu.roll(mine, 80, 1), pltpu.roll(mine, 48, 1)),
            jnp.where(outer, mine, pltpu.roll(here, 48, 1)),
            here,
            jnp.where(outer, pltpu.roll(here, 80, 1), pltpu.roll(deep, 48, 1)),
            deep,
        ]
        raw = [pltpu.roll(here, (-s) % 128, 1) if s else here for s in range(-2, 3)]
        wall = SIGN[c] * here
        second = SIGN[c] * jnp.where((place == 0) | (place == 46), raw[3], raw[1])
        sideways = [
            jnp.where(place < 2, second, raw[0]),
            jnp.where(place == 0, wall, raw[1]),
            here,
            jnp.where(place == 47, wall, raw[3]),
            jnp.where(place >= 46, second, raw[4]),
        ]
        stencils.append((along_i, normal, sideways))
    geometry = [main[GEOMETRY + LEN * n : GEOMETRY + LEN * n + LEN, :] for n in range(9)]
    for c, values in enumerate(advance(stencils, geometry)):
        ghost_ref[LEN * c : LEN * c + LEN, :] = values


def chain_terms(q, metric, chain_ref, scale, tiles, base, out):
    row = lax.broadcasted_iota(jnp.int32, (8, 128), 0)
    start = row < 4
    toward = jnp.where(start, -1.0, 1.0)
    for t in tiles:
        where = slice(128 * t, 128 * t + 128)
        ends = lambda ref, n: jnp.where(start, ref[n, 0:8, where], ref[n, 8:16, where])
        slopes, curves = [], []
        for c in range(4):
            second = chain_ref[c, :, where]
            first = jnp.where(row == 0, pltpu.roll(second, 7, 0), jnp.where(row == 7, pltpu.roll(second, 1, 0), 0.0))
            slopes.append(toward * (8.0 * first - second))
            curves.append(16.0 * first - second)
        added = edge_terms([ends(q, c) for c in range(4)], [ends(metric, n) for n in range(3)], slopes, curves, scale)
        for c in range(4):
            out[c, 0:8, where] = base[c, 0:8, where] + jnp.where(start, added[c], 0.0)
            out[c, 8:16, where] = base[c, 8:16, where] + jnp.where(start, 0.0, added[c])


def joint_terms(q, metric, ghost_ref, face, scale, tiles, out):
    lane = lanes_of(LEN)

    def add(t, direction, slopes, curves):
        where = slice(128 * t, 128 * t + 128)
        here = [q[c, :, where] for c in range(4)]
        geometry = [metric[3 * direction + n, :, where] for n in range(3)]
        added = edge_terms(here, geometry, slopes, curves, scale)
        for c in range(4):
            out[c, :, where] = out[c, :, where] + added[c]

    ghost_of = lambda c: ghost_ref[16 * c : 16 * c + 16, :]
    if tiles[0] == 0:

        @pl.when(face == 2)
        def _():
            slopes, curves = [], []
            for c in range(4):
                ghost = ghost_of(c)
                first = jnp.where(lane < CROSS, ghost, 0.0)
                second = jnp.where(lane < CROSS, pltpu.roll(ghost, 80, 1), pltpu.roll(ghost, 48, 1))
                second = jnp.where(lane < 2 * CROSS, second, 0.0)
                slopes.append(second - 8.0 * first)
                curves.append(16.0 * first - second)
            add(0, 1, slopes, curves)

    if tiles[-1] == TILES - 1:

        @pl.when(face == 3)
        def _():
            slopes, curves = [], []
            for c in range(4):
                ghost = ghost_of(c)
                first = jnp.where(lane >= 80, pltpu.roll(ghost, 80, 1), 0.0)
                second = jnp.where(lane >= 32, pltpu.roll(ghost, 32, 1), 0.0)
                slopes.append(8.0 * first - second)
                curves.append(16.0 * first - second)
            add(TILES - 1, 1, slopes, curves)

    @pl.when(face >= 4)
    def _():
        toward = jnp.where(face == 4, -1.0, 1.0)
        for t in tiles:
            flat = 128 * t + lane
            j = flat // CROSS
            k = flat - j * CROSS
            depth = jnp.where(face == 4, k, CROSS - 1 - k)
            far = jnp.where(depth == 0, j + CROSS, j)[:8]
            slopes, curves = [], []
            for c in range(4):
                ghost = ghost_of(c)
                first = jnp.where(depth == 0, gather_lanes(ghost, j[:8]), 0.0)
                second = jnp.where(depth < 2, gather_lanes(ghost, far), 0.0)
                slopes.append(toward * (8.0 * first - second))
                curves.append(16.0 * first - second)
            add(t, 2, slopes, curves)


def joint_kernel(bulk, q, metric, one, two, three, mate, meta, out, even_ref, odd_ref, ghost_ref, below, above):
    received = (mate, one, two, three)
    copy_part(meta[OWN], received, (0, GEOMETRY), ghost_ref)
    copy_part(meta[OWN + 1], received, PARTS[1], below)
    copy_part(meta[OWN + 2], received, PARTS[2], above)
    out[...] = bulk[...]
    joint_terms(q, metric, ghost_ref, meta[FACE], 1.0, range(TILES), out)
    write_chain(out, even_ref, odd_ref, meta[POSITION])
    even = lax.rem(meta[POSITION], 2) == 0
    spare = slice(CELLS, CELLS + 128)
    even_ref[:, spare] = jnp.where(even, above[...], below[...])
    odd_ref[:, spare] = jnp.where(even, below[...], above[...])


def spread_ghosts(even_in, odd_in, meta, chain_ref):
    even = lax.rem(meta[POSITION], 2) == 0
    has_low = jnp.where(meta[HAS_LOW] == 1, 1.0, 0.0)
    has_high = jnp.where(meta[HAS_HIGH] == 1, 1.0, 0.0)
    for c in range(4):
        rows = slice(2 * c, 2 * c + 2)
        from_even, from_odd = even_in[rows, 0:CELLS], odd_in[rows, 0:CELLS]
        chain_ref[c, 2:6, :] = jnp.zeros((4, CELLS), jnp.float32)
        chain_ref[c, 0:2, :] = has_low * jnp.where(even, from_odd, from_even)
        chain_ref[c, 6:8, :] = has_high * jnp.where(even, from_even, from_odd)


def last_kernel(part, sent, q, metric, one, two, three, mate, even_in, odd_in, meta, out_hbm, *scratch):
    chain_ref, ghost_ref, main, first_low, first_high, out, sem = scratch
    even = lax.rem(meta[POSITION], 2) == 0
    copy_part(meta[OWN], (mate, one, two, three), PARTS[0], main)
    spare = slice(CELLS, CELLS + 128)
    from_even, from_odd = even_in[:, spare], odd_in[:, spare]
    from_low, from_high = jnp.where(even, from_odd, from_even), jnp.where(even, from_even, from_odd)
    partner_face(sent, main, first_low, first_high, from_low, from_high, meta, ghost_ref)
    spread_ghosts(even_in, odd_in, meta, chain_ref)
    copies = []
    for n in range(TILES // GROUP):
        tiles = range(GROUP * n, GROUP * n + GROUP)
        chain_terms(q, metric, chain_ref, 0.5, tiles, part, out)
        joint_terms(q, metric, ghost_ref, meta[FACE], 0.5, tiles, out)
        where = slice(128 * GROUP * n, 128 * GROUP * (n + 1))
        copies.append(pltpu.make_async_copy(out.at[:, :, where], out_hbm.at[:, :, where], sem.at[n]))
        copies[-1].start()
    for copy in copies:
        copy.wait()


f32 = functools.partial(jax.ShapeDtypeStruct, dtype=jnp.float32)
PARAMS = pltpu.CompilerParams(vmem_limit_bytes=24 * 1024 * 1024)
FIELD = f32((4, LEN, CELLS))
JOINT = f32((ROWS, 128))
CHAIN_TILES = pltpu.VMEM((4, 8, CELLS), jnp.float32)
GHOST = pltpu.VMEM((GEOMETRY, 128), jnp.float32)
TILE = pltpu.VMEM((8, 128), jnp.float32)


def local(kernel, shapes, operands, scratch=(), flops=1_000_000, **options):
    options.setdefault("out_specs", [VMEM] * len(shapes))
    return pl.pallas_call(
        kernel,
        out_shape=shapes,
        in_specs=[VMEM] * (len(operands) - 1) + [SMEM],
        scratch_shapes=list(scratch),
        compiler_params=PARAMS,
        cost_estimate=pl.CostEstimate(flops=flops, bytes_accessed=flops, transcendentals=0),
        **options,
    )(*operands)


def bulk(last, *operands):
    kernel = functools.partial(bulk_kernel, last)
    return local(kernel, [FIELD], operands, [] if last else [CHAIN_TILES] * 2, flops=12_000_000)[0]


def along_chain(even, odd):
    pairs = [(i, i + 1) for i in range(1, CHAIN - 1, 2)]
    from_odd = lax.ppermute(odd, "blk", pairs + [(b, a) for a, b in pairs])
    return lax.ppermute(even, "blk", [(i, i ^ 1) for i in range(CHAIN)]), from_odd


def on_device(state, metric, block_map, links):
    HBM = pl.BlockSpec(memory_space=pltpu.HBM)
    held = lambda x: pltpu.with_memory_space_constraint(x, pltpu.HBM)
    arrays = (state.reshape(4, LEN, CELLS), metric.reshape(9, LEN, CELLS), block_map, jnp.transpose(links, (1, 2, 0)))
    q, geometry, joint, even, odd, meta = pl.pallas_call(
        first_kernel,
        out_shape=[FIELD, f32((9, LEN, CELLS)), JOINT] + [f32((8, CELLS))] * 2 + [jax.ShapeDtypeStruct((16,), jnp.int32)],
        in_specs=[HBM] * 4,
        out_specs=[VMEM] * 5 + [SMEM],
        scratch_shapes=[
            pltpu.SMEM((SEGS * CHAIN,), jnp.int32),
            pltpu.SMEM((6, 4, SEGS * CHAIN), jnp.int32),
            pltpu.SemaphoreType.DMA((4,)),
        ],
        compiler_params=PARAMS,
    )(*map(held, arrays))
    across = lambda value, s: lax.ppermute(value, "seg", [(i, i ^ s) for i in range(SEGS)])
    from_even, from_odd = along_chain(even, odd)
    two, three = across(joint, 2), across(joint, 3)
    later, from_odd = lax.optimization_barrier((joint, from_odd))
    one = across(later, 1)
    one, two, three, from_even = lax.optimization_barrier((one, two, three, from_even))
    (picked,) = local(pick_kernel, [JOINT], (joint, one, two, three, meta))
    mate = lax.ppermute(picked, "seg", [(i, i ^ 4) for i in range(SEGS)])
    from_even, from_odd, _ = lax.optimization_barrier((from_even, from_odd, picked))
    part = bulk(False, q, geometry, from_even, from_odd, meta)
    q1, even, odd = local(
        joint_kernel,
        [FIELD] + [f32((8, CELLS + 128))] * 2,
        (part, q, geometry, one, two, three, mate, meta),
        [GHOST, TILE, TILE],
    )
    from_even, from_odd = along_chain(even, odd)
    part = bulk(True, q1, geometry, q, meta)
    (advanced,) = local(
        last_kernel,
        [FIELD],
        (part, joint, q1, geometry, one, two, three, mate, from_even, from_odd, meta),
        [CHAIN_TILES, GHOST, pltpu.VMEM((BELOW, 128), jnp.float32), TILE, TILE]
        + [pltpu.VMEM((4, LEN, CELLS), jnp.float32), pltpu.SemaphoreType.DMA((TILES // GROUP,))],
        out_specs=[HBM],
    )
    return advanced.reshape(state.shape)


def solution(mesh):
    in_specs = (P(("seg", "blk"), None, None, None), P(("seg", "blk"), None, None, None), P(), P())
    out_specs = P(("seg", "blk"), None, None, None)
    return jax.shard_map(
        on_device, mesh=mesh, in_specs=in_specs, out_specs=out_specs, check_vma=False
    )
```

```python
import functools
import jax
import jax.numpy as jnp
from jax import lax
from jax.experimental import pallas as pl
from jax.experimental.pallas import tpu as pltpu
from jax.sharding import PartitionSpec as P

LEN, CROSS, CELLS, TILES = 16, 48, 2304, 18
GROUP = 6
GEOMETRY, BELOW, ABOVE, ROWS = 64, 144, 152, 160
USED, SPARE = 96, 32
FACE, ALONG, ACROSS, POSITION, HAS_LOW, HAS_HIGH, OWN, MATE = 0, 1, 2, 3, 4, 5, 6, 9
PARTS = ((0, BELOW), (BELOW, ABOVE), (ABOVE, ROWS))
SEGS, CHAIN = 8, 32
time_step = 0.05
viscosity = 0.2
compress = 1.0
SIGN = (-1.0, -1.0, -1.0, 1.0)
VMEM = pl.BlockSpec(memory_space=pltpu.VMEM)
SMEM = pl.BlockSpec(memory_space=pltpu.SMEM)


def lanes_of(rows=8):
    return lax.broadcasted_iota(jnp.int32, (rows, 128), 1)


def gather_lanes(values, index):
    parts = [
        jnp.take_along_axis(values[r : r + 8], index, axis=1, mode="promise_in_bounds")
        for r in range(0, values.shape[0], 8)
    ]
    return parts[0] if len(parts) == 1 else jnp.concatenate(parts, axis=0)


def reversed_rows(values):
    index = 7 - lax.broadcasted_iota(jnp.int32, (8, 128), 0)
    flip = lambda part: jnp.take_along_axis(part, index, axis=0, mode="promise_in_bounds")
    return jnp.concatenate([flip(values[8:16]), flip(values[0:8])], axis=0)


def joined_face(device, block_map, links):
    block = block_map[device]
    face, partner, along, across = jnp.int32(0), jnp.int32(-1), jnp.int32(0), jnp.int32(0)
    for side in range(2, 6):
        other = links[side, 0, block]
        here = other >= 0
        face = jnp.where(here, side, face)
        partner = jnp.where(here, other, partner)
        along = jnp.where(here, links[side, 2, block], along)
        across = jnp.where(here, links[side, 3, block], across)
    position = lax.rem(device, CHAIN)
    segment = jnp.int32(0)
    for s in range(SEGS):
        segment = jnp.where(block_map[s * CHAIN + position] == partner, s, segment)
    return face, segment, along, across


def face_source(face, across, first_layer):
    lane = lanes_of()
    layer = jnp.where(lane >= CROSS, 1, 0)
    place = lane - layer * CROSS
    place = jnp.where(across == 1, CROSS - 1 - place, place)
    depth = first_layer + layer
    depth = jnp.where((face == 3) | (face == 5), CROSS - 1 - depth, depth)
    return jnp.where(face <= 3, depth * CROSS + place, place * CROSS + depth)


def gather_face(load, source):
    index, owner = source & 127, source >> 7
    found = None
    for t in range(TILES):
        picked = gather_lanes(load(t), index)
        if found is None:
            found = picked
        else:
            inside = owner == t
            if picked.shape[0] == LEN:
                inside = jnp.concatenate([inside, inside], axis=0)
            found = jnp.where(inside, picked, found)
    return found


def write_chain(field, even_ref, odd_ref, position):
    even = lax.rem(position, 2) == 0
    for c in range(4):
        low, high = field[c, 0:2, :], field[c, LEN - 2 : LEN, :]
        even_ref[2 * c : 2 * c + 2, 0:CELLS] = jnp.where(even, high, low)
        odd_ref[2 * c : 2 * c + 2, 0:CELLS] = jnp.where(even, low, high)


def first_kernel(
    q_hbm, metric_hbm, map_hbm, links_hbm, q, metric, joint_ref, even_ref, odd_ref, meta, block_map, links, edges, sem
):
    copies = [
        pltpu.make_async_copy(source, target, sem.at[n])
        for n, (source, target) in enumerate(
            ((links_hbm, links), (map_hbm, block_map), (q_hbm, q), (metric_hbm, metric))
        )
    ]
    for copy in copies:
        copy.start()
    segment, position = lax.axis_index("seg"), lax.axis_index("blk")
    copies[0].wait()
    copies[1].wait()
    here = segment * CHAIN + position
    other = (segment ^ 4) * CHAIN + position
    before, after = jnp.where(position > 0, -1, 0), jnp.where(position < CHAIN - 1, 1, 0)
    face, partner, along, across = joined_face(here, block_map, links)
    low_face, low_partner, _, low_across = joined_face(here + before, block_map, links)
    high_face, high_partner, _, high_across = joined_face(here + after, block_map, links)
    own = (partner, low_partner, high_partner)
    mates = [joined_face(other + shift, block_map, links)[1] for shift in (0, before, after)]
    meta[FACE] = face
    meta[ALONG] = along
    meta[ACROSS] = across
    meta[POSITION] = position
    block = block_map[here]
    meta[HAS_LOW] = jnp.where(links[0, 0, block] >= 0, 1, 0)
    meta[HAS_HIGH] = jnp.where(links[1, 0, block] >= 0, 1, 0)
    for n in range(3):
        meta[OWN + n] = jnp.where(own[n] // 4 == segment // 4, (own[n] ^ segment) & 3, 0)
        meta[MATE + n] = (mates[n] ^ segment) & 3
    copies[2].wait()
    write_chain(q, even_ref, odd_ref, position)

    where = lambda t: slice(128 * t, 128 * t + 128)
    lane = lanes_of(LEN)
    near, deep = face_source(face, across, 0), face_source(face, across, 2)
    below, above = face_source(low_face, low_across, 0), face_source(high_face, high_across, 0)
    turned = lambda values: jnp.where(along == 1, reversed_rows(values), values)
    face_q = [gather_face(lambda t: q[c, :, where(t)], near) for c in range(4)]
    deeper = [gather_face(lambda t: q[c, :, where(t)], deep) for c in range(4)]
    for c in range(4):
        low_rows = gather_face(lambda t: q[c, 0:8, where(t)], below)
        joint_ref[BELOW + 2 * c : BELOW + 2 * c + 2, :] = low_rows[0:2]
        high_rows = gather_face(lambda t: q[c, 8:16, where(t)], above)
        joint_ref[ABOVE + 2 * c : ABOVE + 2 * c + 2, :] = high_rows[6:8]
    copies[3].wait()
    normal = jnp.where(face <= 3, 1, 2)
    inward = jnp.where((face == 3) | (face == 5), -1.0, 1.0)
    forward = jnp.where(along == 1, -1.0, 1.0)
    sideways = jnp.where(across == 1, -1.0, 1.0)
    geometry = []
    for row, sign in ((0, 1.0), (3 * normal, inward), (3 * (3 - normal), sideways)):
        for b in range(3):
            geometry.append(sign * gather_face(lambda t: metric[row + b, :, where(t)], near))
    part = own_face(face_q, deeper, geometry, meta)
    edges[...] = jnp.zeros((LEN, 128), jnp.float32)
    for n in range(3):
        values = forward * turned(geometry[n])
        edges[4 * n : 4 * n + 2, :] = values[0:2]
        edges[4 * n + 2 : 4 * n + 4, :] = values[14:16]
    packed = (turned(part[2]), turned(part[3]), edges[...])
    for n, values in enumerate(face_q + geometry[3:6] + part[:2]):
        third = pltpu.roll(packed[n // 3], USED - SPARE * (n % 3), 1)
        joint_ref[LEN * n : LEN * n + LEN, :] = jnp.where(lane < USED, turned(values), third)


def unpacked(main, n):
    lane = lanes_of(LEN)
    thirds = [
        pltpu.roll(main[LEN * (3 * n + h) : LEN * (3 * n + h) + LEN, :], (SPARE * h - USED) % 128, 1) for h in range(3)
    ]
    return jnp.where(lane < SPARE, thirds[0], jnp.where(lane < 2 * SPARE, thirds[1], thirds[2]))


def own_face(face_q, deeper, geometry, meta):
    lane = lanes_of(LEN)
    row = lax.broadcasted_iota(jnp.int32, (8, 128), 0)
    place = jnp.where(lane >= CROSS, lane - CROSS, lane)
    outer = lane < CROSS
    open_low = jnp.where(meta[HAS_LOW] == 0, 1.0, 0.0)
    open_high = jnp.where(meta[HAS_HIGH] == 0, 1.0, 0.0)
    stencils = []
    for c in range(4):
        here, deep = face_q[c], deeper[c]
        top, bottom = here[0:8], here[8:16]
        low = -SIGN[c] * open_low * jnp.where(row == 7, pltpu.roll(top, 7, 0), pltpu.roll(top, 5, 0))
        high = -SIGN[c] * open_high * jnp.where(row == 0, pltpu.roll(bottom, 1, 0), pltpu.roll(bottom, 3, 0))
        rows = jnp.concatenate([low, here, high], axis=0)
        along_i = [shifted_rows(rows, s) for s in (-2, -1)] + [here] + [shifted_rows(rows, s) for s in (1, 2)]
        normal = [
            jnp.zeros((LEN, 128), jnp.float32),
            jnp.where(outer, 0.0, pltpu.roll(here, 48, 1)),
            here,
            jnp.where(outer, pltpu.roll(here, 80, 1), pltpu.roll(deep, 48, 1)),
            deep,
        ]
        raw = [pltpu.roll(here, (-s) % 128, 1) if s else here for s in range(-2, 3)]
        wall = SIGN[c] * here
        second = SIGN[c] * jnp.where((place == 0) | (place == 46), raw[3], raw[1])
        sideways = [
            jnp.where(place < 2, second, raw[0]),
            jnp.where(place == 0, wall, raw[1]),
            here,
            jnp.where(place == 47, wall, raw[3]),
            jnp.where(place >= 46, second, raw[4]),
        ]
        stencils.append((along_i, normal, sideways))
    return advance(stencils, geometry)


def copy_part(choice, refs, rows, out):
    for n, ref in enumerate(refs):

        @pl.when(choice == n)
        def _(ref=ref):
            out[...] = ref[rows[0] : rows[1], :]


def pick_kernel(own, one, two, three, meta, out):
    for n, rows in enumerate(PARTS):
        copy_part(meta[MATE + n], (own, one, two, three), rows, out.at[rows[0] : rows[1], :])


def shifted_lanes(before, here, after, shift):
    lane = lanes_of(LEN)
    if shift > 0:
        return jnp.where(
            lane < 128 - shift, pltpu.roll(here, 128 - shift, 1), pltpu.roll(after, 128 - shift, 1)
        )
    return jnp.where(lane >= -shift, pltpu.roll(here, -shift, 1), pltpu.roll(before, -shift, 1))


def shifted_rows(padded, shift):
    return pltpu.roll(padded, (-shift) % 32, 0)[8:24]


def differences(m2, m1, here, p1, p2):
    return 8.0 * (p1 - m1) - (p2 - m2)


def bends(m2, m1, here, p1, p2):
    return 16.0 * (p1 + m1) - (p2 + m2) - 30.0 * here


def advance(stencils, geometry):
    here = [stencils[c][0][2] for c in range(4)]
    moves = [-(time_step / 12.0) * geometry[n] for n in range(9)]
    result = list(here)
    fall = None
    for a in range(3):
        g = geometry[3 * a : 3 * a + 3]
        n = moves[3 * a : 3 * a + 3]
        speed = n[0] * here[0] + n[1] * here[1] + n[2] * here[2]
        spread = (viscosity * time_step / 12.0) * (g[0] * g[0] + g[1] * g[1] + g[2] * g[2])
        drop = differences(*stencils[3][a])
        for b in range(3):
            slope = differences(*stencils[b][a])
            result[b] = result[b] + speed * slope + n[b] * drop + spread * bends(*stencils[b][a])
            term = n[b] * slope
            fall = term if fall is None else fall + term
    result[3] = result[3] + compress * fall
    return result


def chain_ghosts(q, even_in, odd_in, meta, low_ref, high_ref):
    even = lax.rem(meta[POSITION], 2) == 0
    for c in range(4):
        rows = slice(2 * c, 2 * c + 2)
        from_even, from_odd = even_in[rows, :], odd_in[rows, :]
        low_ref[c, 6:8, :] = jnp.where(even, from_odd, from_even)
        high_ref[c, 0:2, :] = jnp.where(even, from_even, from_odd)

    @pl.when(meta[HAS_LOW] == 0)
    def _():
        for c in range(4):
            low_ref[c, 7:8, :] = -SIGN[c] * q[c, 0:1, :]
            low_ref[c, 6:7, :] = -SIGN[c] * q[c, 1:2, :]

    @pl.when(meta[HAS_HIGH] == 0)
    def _():
        for c in range(4):
            high_ref[c, 0:1, :] = -SIGN[c] * q[c, LEN - 1 : LEN, :]
            high_ref[c, 1:2, :] = -SIGN[c] * q[c, LEN - 2 : LEN - 1, :]


def bulk_kernel(last, q, metric, *rest):
    if last:
        first, meta, out = rest
    else:
        even_in, odd_in, meta, out, low_ref, high_ref = rest
        chain_ghosts(q, even_in, odd_in, meta, low_ref, high_ref)
    lane = lanes_of(LEN)
    row = lax.broadcasted_iota(jnp.int32, (8, 128), 0)
    face, ends = meta[FACE], (meta[HAS_LOW] == 0, meta[HAS_HIGH] == 0)
    load = lambda c, t: q[c, :, 128 * t : 128 * t + 128]
    before_first, after_last = [], []
    for c in range(4):
        head = jnp.where(face == 2, 0.0, SIGN[c]) * load(c, 0)
        before_first.append(jnp.where(lane >= 80, pltpu.roll(head, 80, 1), pltpu.roll(head, 112, 1)))
        tail = jnp.where(face == 3, 0.0, SIGN[c]) * load(c, TILES - 1)
        after_last.append(jnp.where(lane < CROSS, pltpu.roll(tail, 48, 1), pltpu.roll(tail, 16, 1)))

    def tile(c, t):
        return before_first[c] if t < 0 else after_last[c] if t >= TILES else load(c, t)

    low_scale = jnp.where(face == 4, 0.0, 1.0)
    high_scale = jnp.where(face == 5, 0.0, 1.0)
    open_low = jnp.where(ends[0], 1.0, 0.0)
    open_high = jnp.where(ends[1], 1.0, 0.0)
    for t in range(TILES):
        flat = 128 * t + lane
        k = flat - (flat // CROSS) * CROSS
        scale = jnp.where(k < 2, low_scale, high_scale)
        where = slice(128 * t, 128 * t + 128)
        stencils = []
        for c in range(4):
            before, here, after = tile(c, t - 1), tile(c, t), tile(c, t + 1)
            if last:
                top, bottom = here[0:8], here[8:16]
                low = -SIGN[c] * open_low * jnp.where(row == 7, pltpu.roll(top, 7, 0), pltpu.roll(top, 5, 0))
                high = -SIGN[c] * open_high * jnp.where(row == 0, pltpu.roll(bottom, 1, 0), pltpu.roll(bottom, 3, 0))
            else:
                low, high = low_ref[c, :, where], high_ref[c, :, where]
            rows = jnp.concatenate([low, here, high], axis=0)
            along_i = [shifted_rows(rows, s) for s in (-2, -1)] + [here] + [shifted_rows(rows, s) for s in (1, 2)]
            along_j = [shifted_lanes(before, here, after, CROSS * s) if s else here for s in range(-2, 3)]
            raw = [shifted_lanes(before, here, after, s) if s else here for s in range(-2, 3)]
            factor = SIGN[c] * scale
            nearest = factor * here
            second = factor * jnp.where((k == 0) | (k == 46), raw[3], raw[1])
            along_k = [
                jnp.where(k < 2, second, raw[0]),
                jnp.where(k == 0, nearest, raw[1]),
                here,
                jnp.where(k == 47, nearest, raw[3]),
                jnp.where(k >= 46, second, raw[4]),
            ]
            stencils.append((along_i, along_j, along_k))
        values = advance(stencils, [metric[n, :, where] for n in range(9)])
        for c in range(4):
            kept = 0.5 * first[c, :, where] + 0.5 * values[c] if last else values[c]
            out[c, :, where] = kept


def edge_terms(here, geometry, slopes, curves, scale):
    moves = [-(scale * time_step / 12.0) * g for g in geometry]
    speed = moves[0] * here[0] + moves[1] * here[1] + moves[2] * here[2]
    squares = geometry[0] * geometry[0] + geometry[1] * geometry[1] + geometry[2] * geometry[2]
    spread = (scale * viscosity * time_step / 12.0) * squares
    added = [speed * slopes[b] + moves[b] * slopes[3] + spread * curves[b] for b in range(3)]
    added.append(compress * (moves[0] * slopes[0] + moves[1] * slopes[1] + moves[2] * slopes[2]))
    return added


def partner_face(sent, main, ends_ref, from_low, from_high, meta, ghost_ref):
    lane = lanes_of(LEN)
    row = lax.broadcasted_iota(jnp.int32, (8, 128), 0)
    along, across = meta[ALONG] == 1, meta[ACROSS] == 1
    has_low = jnp.where(jnp.where(along, meta[HAS_HIGH], meta[HAS_LOW]) == 1, 1.0, 0.0)
    has_high = jnp.where(jnp.where(along, meta[HAS_LOW], meta[HAS_HIGH]) == 1, 1.0, 0.0)
    mirrored = jnp.where(lane < CROSS, CROSS - 1 - lane, jnp.where(lane < 2 * CROSS, 3 * CROSS - 1 - lane, lane))[:8]
    rows_of = lambda n: main[LEN * n : LEN * n + LEN, :]
    here = [rows_of(c) for c in range(4)]
    slopes, curves = [], []
    for c in range(4):
        mine = sent[LEN * c : LEN * c + LEN, :]
        mine = jnp.where(across, gather_lanes(mine, mirrored), mine)
        mine = jnp.where(along, reversed_rows(mine), mine)
        first = jnp.where(lane < CROSS, mine, 0.0)
        second = jnp.where(lane < CROSS, pltpu.roll(mine, 80, 1), pltpu.roll(mine, 48, 1))
        second = jnp.where(lane < 2 * CROSS, second, 0.0)
        slopes.append(second - 8.0 * first)
        curves.append(16.0 * first - second)
    added = edge_terms(here, [rows_of(4 + n) for n in range(3)], slopes, curves, 1.0)
    parts = [rows_of(7), rows_of(8), unpacked(main, 0), unpacked(main, 1)]

    ends_ref[...] = jnp.zeros((7, 8, 128), jnp.float32)
    metric_ends = unpacked(main, 2)
    for n in range(3):
        ends_ref[4 + n, 0:2, :] = metric_ends[4 * n : 4 * n + 2]
        ends_ref[4 + n, 6:8, :] = metric_ends[4 * n + 2 : 4 * n + 4]
    for c in range(4):
        below, above = from_low[2 * c : 2 * c + 2, :], from_high[2 * c : 2 * c + 2, :]
        ends_ref[c, 0:1, :] = has_low * jnp.where(along, above[1:2], below[0:1])
        ends_ref[c, 1:2, :] = has_low * jnp.where(along, above[0:1], below[1:2])
        ends_ref[c, 6:7, :] = has_high * jnp.where(along, below[1:2], above[0:1])
        ends_ref[c, 7:8, :] = has_high * jnp.where(along, below[0:1], above[1:2])
    slopes, curves = [], []
    for c in range(4):
        slope, curve = chain_stencil(ends_ref[c], row)
        slopes.append(slope)
        curves.append(curve)
    start = row < 4
    at_ends = [jnp.where(start, here[c][0:8], here[c][8:16]) for c in range(4)]
    more = edge_terms(at_ends, [ends_ref[4 + n] for n in range(3)], slopes, curves, 1.0)
    for c in range(4):
        values = parts[c] + added[c]
        ghost_ref[LEN * c : LEN * c + 8, :] = values[0:8] + jnp.where(start, more[c], 0.0)
        ghost_ref[LEN * c + 8 : LEN * c + LEN, :] = values[8:16] + jnp.where(start, 0.0, more[c])


def chain_stencil(second, row):
    first = jnp.where(row == 0, pltpu.roll(second, 7, 0), jnp.where(row == 7, pltpu.roll(second, 1, 0), 0.0))
    return jnp.where(row < 4, -1.0, 1.0) * (8.0 * first - second), 16.0 * first - second


def chain_terms(q, metric, chain_ref, scale, tiles, base, out):
    row = lax.broadcasted_iota(jnp.int32, (8, 128), 0)
    start = row < 4
    for t in tiles:
        where = slice(128 * t, 128 * t + 128)
        ends = lambda ref, n: jnp.where(start, ref[n, 0:8, where], ref[n, 8:16, where])
        slopes, curves = [], []
        for c in range(4):
            slope, curve = chain_stencil(chain_ref[c, :, where], row)
            slopes.append(slope)
            curves.append(curve)
        added = edge_terms([ends(q, c) for c in range(4)], [ends(metric, n) for n in range(3)], slopes, curves, scale)
        for c in range(4):
            out[c, 0:8, where] = base[c, 0:8, where] + jnp.where(start, added[c], 0.0)
            out[c, 8:16, where] = base[c, 8:16, where] + jnp.where(start, 0.0, added[c])


def joint_terms(q, metric, ghost_ref, face, scale, tiles, out):
    lane = lanes_of(LEN)

    def add(t, direction, slopes, curves):
        where = slice(128 * t, 128 * t + 128)
        here = [q[c, :, where] for c in range(4)]
        geometry = [metric[3 * direction + n, :, where] for n in range(3)]
        added = edge_terms(here, geometry, slopes, curves, scale)
        for c in range(4):
            out[c, :, where] = out[c, :, where] + added[c]

    ghost_of = lambda c: ghost_ref[16 * c : 16 * c + 16, :]
    if tiles[0] == 0:

        @pl.when(face == 2)
        def _():
            slopes, curves = [], []
            for c in range(4):
                ghost = ghost_of(c)
                first = jnp.where(lane < CROSS, ghost, 0.0)
                second = jnp.where(lane < CROSS, pltpu.roll(ghost, 80, 1), pltpu.roll(ghost, 48, 1))
                second = jnp.where(lane < 2 * CROSS, second, 0.0)
                slopes.append(second - 8.0 * first)
                curves.append(16.0 * first - second)
            add(0, 1, slopes, curves)

    if tiles[-1] == TILES - 1:

        @pl.when(face == 3)
        def _():
            slopes, curves = [], []
            for c in range(4):
                ghost = ghost_of(c)
                first = jnp.where(lane >= 80, pltpu.roll(ghost, 80, 1), 0.0)
                second = jnp.where(lane >= 32, pltpu.roll(ghost, 32, 1), 0.0)
                slopes.append(8.0 * first - second)
                curves.append(16.0 * first - second)
            add(TILES - 1, 1, slopes, curves)

    @pl.when(face >= 4)
    def _():
        toward = jnp.where(face == 4, -1.0, 1.0)
        for t in tiles:
            flat = 128 * t + lane
            j = flat // CROSS
            k = flat - j * CROSS
            depth = jnp.where(face == 4, k, CROSS - 1 - k)
            far = jnp.where(depth == 0, j + CROSS, j)[:8]
            slopes, curves = [], []
            for c in range(4):
                ghost = ghost_of(c)
                first = jnp.where(depth == 0, gather_lanes(ghost, j[:8]), 0.0)
                second = jnp.where(depth < 2, gather_lanes(ghost, far), 0.0)
                slopes.append(toward * (8.0 * first - second))
                curves.append(16.0 * first - second)
            add(t, 2, slopes, curves)


def joint_kernel(bulk, q, metric, one, two, three, mate, meta, out, even_ref, odd_ref, ghost_ref, below, above):
    received = (mate, one, two, three)
    copy_part(meta[OWN], received, (0, GEOMETRY), ghost_ref)
    copy_part(meta[OWN + 1], received, PARTS[1], below)
    copy_part(meta[OWN + 2], received, PARTS[2], above)
    out[...] = bulk[...]
    joint_terms(q, metric, ghost_ref, meta[FACE], 1.0, range(TILES), out)
    write_chain(out, even_ref, odd_ref, meta[POSITION])
    even = lax.rem(meta[POSITION], 2) == 0
    spare = slice(CELLS, CELLS + 128)
    even_ref[:, spare] = jnp.where(even, above[...], below[...])
    odd_ref[:, spare] = jnp.where(even, below[...], above[...])


def spread_ghosts(even_in, odd_in, meta, chain_ref):
    even = lax.rem(meta[POSITION], 2) == 0
    has_low = jnp.where(meta[HAS_LOW] == 1, 1.0, 0.0)
    has_high = jnp.where(meta[HAS_HIGH] == 1, 1.0, 0.0)
    for c in range(4):
        rows = slice(2 * c, 2 * c + 2)
        from_even, from_odd = even_in[rows, 0:CELLS], odd_in[rows, 0:CELLS]
        chain_ref[c, 2:6, :] = jnp.zeros((4, CELLS), jnp.float32)
        chain_ref[c, 0:2, :] = has_low * jnp.where(even, from_odd, from_even)
        chain_ref[c, 6:8, :] = has_high * jnp.where(even, from_even, from_odd)


def last_kernel(part, sent, q, metric, one, two, three, mate, even_in, odd_in, meta, out_hbm, *scratch):
    chain_ref, ghost_ref, main, ends_ref, out, sem = scratch
    even = lax.rem(meta[POSITION], 2) == 0
    copy_part(meta[OWN], (mate, one, two, three), PARTS[0], main)
    spare = slice(CELLS, CELLS + 128)
    from_even, from_odd = even_in[:, spare], odd_in[:, spare]
    from_low, from_high = jnp.where(even, from_odd, from_even), jnp.where(even, from_even, from_odd)
    partner_face(sent, main, ends_ref, from_low, from_high, meta, ghost_ref)
    spread_ghosts(even_in, odd_in, meta, chain_ref)
    copies = []
    for n in range(TILES // GROUP):
        tiles = range(GROUP * n, GROUP * n + GROUP)
        chain_terms(q, metric, chain_ref, 0.5, tiles, part, out)
        joint_terms(q, metric, ghost_ref, meta[FACE], 0.5, tiles, out)
        where = slice(128 * GROUP * n, 128 * GROUP * (n + 1))
        copies.append(pltpu.make_async_copy(out.at[:, :, where], out_hbm.at[:, :, where], sem.at[n]))
        copies[-1].start()
    for copy in copies:
        copy.wait()


f32 = functools.partial(jax.ShapeDtypeStruct, dtype=jnp.float32)
PARAMS = pltpu.CompilerParams(vmem_limit_bytes=24 * 1024 * 1024)
FIELD = f32((4, LEN, CELLS))
JOINT = f32((ROWS, 128))
CHAIN_TILES = pltpu.VMEM((4, 8, CELLS), jnp.float32)
GHOST = pltpu.VMEM((GEOMETRY, 128), jnp.float32)
TILE = pltpu.VMEM((8, 128), jnp.float32)


def local(kernel, shapes, operands, scratch=(), flops=1_000_000, **options):
    options.setdefault("out_specs", [VMEM] * len(shapes))
    return pl.pallas_call(
        kernel,
        out_shape=shapes,
        in_specs=[VMEM] * (len(operands) - 1) + [SMEM],
        scratch_shapes=list(scratch),
        compiler_params=PARAMS,
        cost_estimate=pl.CostEstimate(flops=flops, bytes_accessed=flops, transcendentals=0),
        **options,
    )(*operands)


def bulk(last, *operands):
    kernel = functools.partial(bulk_kernel, last)
    return local(kernel, [FIELD], operands, [] if last else [CHAIN_TILES] * 2, flops=12_000_000)[0]


def along_chain(even, odd):
    pairs = [(i, i + 1) for i in range(1, CHAIN - 1, 2)]
    from_odd = lax.ppermute(odd, "blk", pairs + [(b, a) for a, b in pairs])
    return lax.ppermute(even, "blk", [(i, i ^ 1) for i in range(CHAIN)]), from_odd


def on_device(state, metric, block_map, links):
    HBM = pl.BlockSpec(memory_space=pltpu.HBM)
    held = lambda x: pltpu.with_memory_space_constraint(x, pltpu.HBM)
    arrays = (state.reshape(4, LEN, CELLS), metric.reshape(9, LEN, CELLS), block_map, jnp.transpose(links, (1, 2, 0)))
    q, geometry, joint, even, odd, meta = pl.pallas_call(
        first_kernel,
        out_shape=[FIELD, f32((9, LEN, CELLS)), JOINT] + [f32((8, CELLS))] * 2 + [jax.ShapeDtypeStruct((16,), jnp.int32)],
        in_specs=[HBM] * 4,
        out_specs=[VMEM] * 5 + [SMEM],
        scratch_shapes=[
            pltpu.SMEM((SEGS * CHAIN,), jnp.int32),
            pltpu.SMEM((6, 4, SEGS * CHAIN), jnp.int32),
            pltpu.VMEM((LEN, 128), jnp.float32),
            pltpu.SemaphoreType.DMA((4,)),
        ],
        compiler_params=PARAMS,
    )(*map(held, arrays))
    across = lambda value, s: lax.ppermute(value, "seg", [(i, i ^ s) for i in range(SEGS)])
    from_even, from_odd = along_chain(even, odd)
    two, three = across(joint, 2), across(joint, 3)
    later, from_odd = lax.optimization_barrier((joint, from_odd))
    one = across(later, 1)
    one, two, three, from_even = lax.optimization_barrier((one, two, three, from_even))
    (picked,) = local(pick_kernel, [JOINT], (joint, one, two, three, meta))
    mate = lax.ppermute(picked, "seg", [(i, i ^ 4) for i in range(SEGS)])
    from_even, from_odd, _ = lax.optimization_barrier((from_even, from_odd, picked))
    part = bulk(False, q, geometry, from_even, from_odd, meta)
    q1, even, odd = local(
        joint_kernel,
        [FIELD] + [f32((8, CELLS + 128))] * 2,
        (part, q, geometry, one, two, three, mate, meta),
        [GHOST, TILE, TILE],
    )
    from_even, from_odd = along_chain(even, odd)
    part = bulk(True, q1, geometry, q, meta)
    (advanced,) = local(
        last_kernel,
        [FIELD],
        (part, joint, q1, geometry, one, two, three, mate, from_even, from_odd, meta),
        [CHAIN_TILES, GHOST, pltpu.VMEM((BELOW, 128), jnp.float32), pltpu.VMEM((7, 8, 128), jnp.float32)]
        + [pltpu.VMEM((4, LEN, CELLS), jnp.float32), pltpu.SemaphoreType.DMA((TILES // GROUP,))],
        out_specs=[HBM],
    )
    return advanced.reshape(state.shape)


def solution(mesh):
    in_specs = (P(("seg", "blk"), None, None, None), P(("seg", "blk"), None, None, None), P(), P())
    out_specs = P(("seg", "blk"), None, None, None)
    return jax.shard_map(
        on_device, mesh=mesh, in_specs=in_specs, out_specs=out_specs, check_vma=False
    )
```

```python
import functools
import jax
import jax.numpy as jnp
from jax import lax
from jax.experimental import pallas as pl
from jax.experimental.pallas import tpu as pltpu
from jax.sharding import PartitionSpec as P

LEN, CROSS, CELLS, TILES = 16, 48, 2304, 18
GROUP = 6
GEOMETRY, BELOW, ABOVE, ROWS = 64, 144, 152, 160
USED, SPARE = 96, 32
FACE, ALONG, ACROSS, POSITION, HAS_LOW, HAS_HIGH, OWN, MATE = 0, 1, 2, 3, 4, 5, 6, 9
PARTS = ((0, BELOW), (BELOW, ABOVE), (ABOVE, ROWS))
SEGS, CHAIN = 8, 32
time_step = 0.05
viscosity = 0.2
compress = 1.0
SIGN = (-1.0, -1.0, -1.0, 1.0)
VMEM = pl.BlockSpec(memory_space=pltpu.VMEM)
SMEM = pl.BlockSpec(memory_space=pltpu.SMEM)


def lanes_of(rows=8):
    return lax.broadcasted_iota(jnp.int32, (rows, 128), 1)


def gather_lanes(values, index):
    parts = [
        jnp.take_along_axis(values[r : r + 8], index, axis=1, mode="promise_in_bounds")
        for r in range(0, values.shape[0], 8)
    ]
    return parts[0] if len(parts) == 1 else jnp.concatenate(parts, axis=0)


def reversed_rows(values):
    index = 7 - lax.broadcasted_iota(jnp.int32, (8, 128), 0)
    flip = lambda part: jnp.take_along_axis(part, index, axis=0, mode="promise_in_bounds")
    return jnp.concatenate([flip(values[8:16]), flip(values[0:8])], axis=0)


def joined_face(device, block_map, links):
    block = block_map[device]
    face, partner, along, across = jnp.int32(0), jnp.int32(-1), jnp.int32(0), jnp.int32(0)
    for side in range(2, 6):
        other = links[side, 0, block]
        here = other >= 0
        face = jnp.where(here, side, face)
        partner = jnp.where(here, other, partner)
        along = jnp.where(here, links[side, 2, block], along)
        across = jnp.where(here, links[side, 3, block], across)
    position = lax.rem(device, CHAIN)
    segment = jnp.int32(0)
    for s in range(SEGS):
        segment = jnp.where(block_map[s * CHAIN + position] == partner, s, segment)
    return face, segment, along, across


def face_source(face, across, first_layer):
    lane = lanes_of()
    layer = jnp.where(lane >= CROSS, 1, 0)
    place = lane - layer * CROSS
    place = jnp.where(across == 1, CROSS - 1 - place, place)
    depth = first_layer + layer
    depth = jnp.where((face == 3) | (face == 5), CROSS - 1 - depth, depth)
    return jnp.where(face <= 3, depth * CROSS + place, place * CROSS + depth)


def gather_face(load, source):
    index, owner = source & 127, source >> 7
    found = None
    for t in range(TILES):
        picked = gather_lanes(load(t), index)
        if found is None:
            found = picked
        else:
            inside = owner == t
            if picked.shape[0] == LEN:
                inside = jnp.concatenate([inside, inside], axis=0)
            found = jnp.where(inside, picked, found)
    return found


def write_chain(field, even_ref, odd_ref, position):
    even = lax.rem(position, 2) == 0
    for c in range(4):
        low, high = field[c, 0:2, :], field[c, LEN - 2 : LEN, :]
        even_ref[2 * c : 2 * c + 2, 0:CELLS] = jnp.where(even, high, low)
        odd_ref[2 * c : 2 * c + 2, 0:CELLS] = jnp.where(even, low, high)


def first_kernel(
    q_hbm, metric_hbm, map_hbm, links_hbm, q, metric, joint_ref, even_ref, odd_ref, meta, block_map, links, edges, sem
):
    copies = [
        pltpu.make_async_copy(source, target, sem.at[n])
        for n, (source, target) in enumerate(
            ((links_hbm, links), (map_hbm, block_map), (q_hbm, q), (metric_hbm, metric))
        )
    ]
    for copy in copies:
        copy.start()
    segment, position = lax.axis_index("seg"), lax.axis_index("blk")
    copies[0].wait()
    copies[1].wait()
    here = segment * CHAIN + position
    other = (segment ^ 4) * CHAIN + position
    before, after = jnp.where(position > 0, -1, 0), jnp.where(position < CHAIN - 1, 1, 0)
    face, partner, along, across = joined_face(here, block_map, links)
    low_face, low_partner, _, low_across = joined_face(here + before, block_map, links)
    high_face, high_partner, _, high_across = joined_face(here + after, block_map, links)
    own = (partner, low_partner, high_partner)
    mates = [joined_face(other + shift, block_map, links)[1] for shift in (0, before, after)]
    meta[FACE] = face
    meta[ALONG] = along
    meta[ACROSS] = across
    meta[POSITION] = position
    block = block_map[here]
    meta[HAS_LOW] = jnp.where(links[0, 0, block] >= 0, 1, 0)
    meta[HAS_HIGH] = jnp.where(links[1, 0, block] >= 0, 1, 0)
    for n in range(3):
        meta[OWN + n] = jnp.where(own[n] // 4 == segment // 4, (own[n] ^ segment) & 3, 0)
        meta[MATE + n] = (mates[n] ^ segment) & 3
    copies[2].wait()
    write_chain(q, even_ref, odd_ref, position)

    where = lambda t: slice(128 * t, 128 * t + 128)
    lane = lanes_of(LEN)
    near, deep = face_source(face, across, 0), face_source(face, across, 2)
    below, above = face_source(low_face, low_across, 0), face_source(high_face, high_across, 0)
    turned = lambda values: jnp.where(along == 1, reversed_rows(values), values)
    face_q = [gather_face(lambda t: q[c, :, where(t)], near) for c in range(4)]
    deeper = [gather_face(lambda t: q[c, :, where(t)], deep) for c in range(4)]
    for c in range(4):
        low_rows = gather_face(lambda t: q[c, 0:8, where(t)], below)
        joint_ref[BELOW + 2 * c : BELOW + 2 * c + 2, :] = low_rows[0:2]
        high_rows = gather_face(lambda t: q[c, 8:16, where(t)], above)
        joint_ref[ABOVE + 2 * c : ABOVE + 2 * c + 2, :] = high_rows[6:8]
    copies[3].wait()
    normal = jnp.where(face <= 3, 1, 2)
    inward = jnp.where((face == 3) | (face == 5), -1.0, 1.0)
    forward = jnp.where(along == 1, -1.0, 1.0)
    sideways = jnp.where(across == 1, -1.0, 1.0)
    geometry = []
    for row, sign in ((0, 1.0), (3 * normal, inward), (3 * (3 - normal), sideways)):
        for b in range(3):
            geometry.append(sign * gather_face(lambda t: metric[row + b, :, where(t)], near))
    part = own_face(face_q, deeper, geometry, meta)
    edges[...] = jnp.zeros((LEN, 128), jnp.float32)
    for n in range(3):
        values = forward * turned(geometry[n])
        edges[4 * n : 4 * n + 2, :] = values[0:2]
        edges[4 * n + 2 : 4 * n + 4, :] = values[14:16]
    packed = (turned(part[2]), turned(part[3]), edges[...])
    for n, values in enumerate(face_q + geometry[3:6] + part[:2]):
        third = pltpu.roll(packed[n // 3], USED - SPARE * (n % 3), 1)
        joint_ref[LEN * n : LEN * n + LEN, :] = jnp.where(lane < USED, turned(values), third)


def unpacked(main, n):
    lane = lanes_of(LEN)
    thirds = [
        pltpu.roll(main[LEN * (3 * n + h) : LEN * (3 * n + h) + LEN, :], (SPARE * h - USED) % 128, 1) for h in range(3)
    ]
    return jnp.where(lane < SPARE, thirds[0], jnp.where(lane < 2 * SPARE, thirds[1], thirds[2]))


def own_face(face_q, deeper, geometry, meta):
    lane = lanes_of(LEN)
    row = lax.broadcasted_iota(jnp.int32, (8, 128), 0)
    place = jnp.where(lane >= CROSS, lane - CROSS, lane)
    outer = lane < CROSS
    open_low = jnp.where(meta[HAS_LOW] == 0, 1.0, 0.0)
    open_high = jnp.where(meta[HAS_HIGH] == 0, 1.0, 0.0)
    stencils = []
    for c in range(4):
        here, deep = face_q[c], deeper[c]
        top, bottom = here[0:8], here[8:16]
        low = -SIGN[c] * open_low * jnp.where(row == 7, pltpu.roll(top, 7, 0), pltpu.roll(top, 5, 0))
        high = -SIGN[c] * open_high * jnp.where(row == 0, pltpu.roll(bottom, 1, 0), pltpu.roll(bottom, 3, 0))
        rows = jnp.concatenate([low, here, high], axis=0)
        along_i = [shifted_rows(rows, s) for s in (-2, -1)] + [here] + [shifted_rows(rows, s) for s in (1, 2)]
        normal = [
            jnp.zeros((LEN, 128), jnp.float32),
            jnp.where(outer, 0.0, pltpu.roll(here, 48, 1)),
            here,
            jnp.where(outer, pltpu.roll(here, 80, 1), pltpu.roll(deep, 48, 1)),
            deep,
        ]
        raw = [pltpu.roll(here, (-s) % 128, 1) if s else here for s in range(-2, 3)]
        wall = SIGN[c] * here
        second = SIGN[c] * jnp.where((place == 0) | (place == 46), raw[3], raw[1])
        sideways = [
            jnp.where(place < 2, second, raw[0]),
            jnp.where(place == 0, wall, raw[1]),
            here,
            jnp.where(place == 47, wall, raw[3]),
            jnp.where(place >= 46, second, raw[4]),
        ]
        stencils.append((along_i, normal, sideways))
    return advance(stencils, geometry)


def copy_part(choice, refs, rows, out):
    for n, ref in enumerate(refs):

        @pl.when(choice == n)
        def _(ref=ref):
            out[...] = ref[rows[0] : rows[1], :]


def pick_kernel(own, one, two, three, meta, out):
    for n, rows in enumerate(PARTS):
        copy_part(meta[MATE + n], (own, one, two, three), rows, out.at[rows[0] : rows[1], :])


def shifted_lanes(before, here, after, shift):
    lane = lanes_of(LEN)
    if shift > 0:
        return jnp.where(
            lane < 128 - shift, pltpu.roll(here, 128 - shift, 1), pltpu.roll(after, 128 - shift, 1)
        )
    return jnp.where(lane >= -shift, pltpu.roll(here, -shift, 1), pltpu.roll(before, -shift, 1))


def shifted_rows(padded, shift):
    return pltpu.roll(padded, (-shift) % 32, 0)[8:24]


def differences(m2, m1, here, p1, p2):
    return 8.0 * (p1 - m1) - (p2 - m2)


def bends(m2, m1, here, p1, p2):
    return 16.0 * (p1 + m1) - (p2 + m2) - 30.0 * here


def advance(stencils, geometry):
    here = [stencils[c][0][2] for c in range(4)]
    moves = [-(time_step / 12.0) * geometry[n] for n in range(9)]
    result = list(here)
    fall = None
    for a in range(3):
        g = geometry[3 * a : 3 * a + 3]
        n = moves[3 * a : 3 * a + 3]
        speed = n[0] * here[0] + n[1] * here[1] + n[2] * here[2]
        spread = (viscosity * time_step / 12.0) * (g[0] * g[0] + g[1] * g[1] + g[2] * g[2])
        drop = differences(*stencils[3][a])
        for b in range(3):
            slope = differences(*stencils[b][a])
            result[b] = result[b] + speed * slope + n[b] * drop + spread * bends(*stencils[b][a])
            term = n[b] * slope
            fall = term if fall is None else fall + term
    result[3] = result[3] + compress * fall
    return result


def chain_ghosts(q, even_in, odd_in, meta, low_ref, high_ref):
    even = lax.rem(meta[POSITION], 2) == 0
    for c in range(4):
        rows = slice(2 * c, 2 * c + 2)
        from_even, from_odd = even_in[rows, :], odd_in[rows, :]
        low_ref[c, 6:8, :] = jnp.where(even, from_odd, from_even)
        high_ref[c, 0:2, :] = jnp.where(even, from_even, from_odd)

    @pl.when(meta[HAS_LOW] == 0)
    def _():
        for c in range(4):
            low_ref[c, 7:8, :] = -SIGN[c] * q[c, 0:1, :]
            low_ref[c, 6:7, :] = -SIGN[c] * q[c, 1:2, :]

    @pl.when(meta[HAS_HIGH] == 0)
    def _():
        for c in range(4):
            high_ref[c, 0:1, :] = -SIGN[c] * q[c, LEN - 1 : LEN, :]
            high_ref[c, 1:2, :] = -SIGN[c] * q[c, LEN - 2 : LEN - 1, :]


def bulk_kernel(last, q, metric, *rest):
    if last:
        first, meta, out = rest
    else:
        even_in, odd_in, meta, out, low_ref, high_ref = rest
        chain_ghosts(q, even_in, odd_in, meta, low_ref, high_ref)
    lane = lanes_of(LEN)
    row = lax.broadcasted_iota(jnp.int32, (8, 128), 0)
    face, ends = meta[FACE], (meta[HAS_LOW] == 0, meta[HAS_HIGH] == 0)
    load = lambda c, t: q[c, :, 128 * t : 128 * t + 128]
    before_first, after_last = [], []
    for c in range(4):
        head = jnp.where(face == 2, 0.0, SIGN[c]) * load(c, 0)
        before_first.append(jnp.where(lane >= 80, pltpu.roll(head, 80, 1), pltpu.roll(head, 112, 1)))
        tail = jnp.where(face == 3, 0.0, SIGN[c]) * load(c, TILES - 1)
        after_last.append(jnp.where(lane < CROSS, pltpu.roll(tail, 48, 1), pltpu.roll(tail, 16, 1)))

    def tile(c, t):
        return before_first[c] if t < 0 else after_last[c] if t >= TILES else load(c, t)

    low_scale = jnp.where(face == 4, 0.0, 1.0)
    high_scale = jnp.where(face == 5, 0.0, 1.0)
    open_low = jnp.where(ends[0], 1.0, 0.0)
    open_high = jnp.where(ends[1], 1.0, 0.0)
    for t in range(TILES):
        flat = 128 * t + lane
        k = flat - (flat // CROSS) * CROSS
        scale = jnp.where(k < 2, low_scale, high_scale)
        where = slice(128 * t, 128 * t + 128)
        stencils = []
        for c in range(4):
            before, here, after = tile(c, t - 1), tile(c, t), tile(c, t + 1)
            if last:
                top, bottom = here[0:8], here[8:16]
                low = -SIGN[c] * open_low * jnp.where(row == 7, pltpu.roll(top, 7, 0), pltpu.roll(top, 5, 0))
                high = -SIGN[c] * open_high * jnp.where(row == 0, pltpu.roll(bottom, 1, 0), pltpu.roll(bottom, 3, 0))
            else:
                low, high = low_ref[c, :, where], high_ref[c, :, where]
            rows = jnp.concatenate([low, here, high], axis=0)
            along_i = [shifted_rows(rows, s) for s in (-2, -1)] + [here] + [shifted_rows(rows, s) for s in (1, 2)]
            along_j = [shifted_lanes(before, here, after, CROSS * s) if s else here for s in range(-2, 3)]
            raw = [shifted_lanes(before, here, after, s) if s else here for s in range(-2, 3)]
            factor = SIGN[c] * scale
            nearest = factor * here
            second = factor * jnp.where((k == 0) | (k == 46), raw[3], raw[1])
            along_k = [
                jnp.where(k < 2, second, raw[0]),
                jnp.where(k == 0, nearest, raw[1]),
                here,
                jnp.where(k == 47, nearest, raw[3]),
                jnp.where(k >= 46, second, raw[4]),
            ]
            stencils.append((along_i, along_j, along_k))
        values = advance(stencils, [metric[n, :, where] for n in range(9)])
        for c in range(4):
            kept = 0.5 * first[c, :, where] + 0.5 * values[c] if last else values[c]
            out[c, :, where] = kept


def edge_terms(here, geometry, slopes, curves, scale):
    moves = [-(scale * time_step / 12.0) * g for g in geometry]
    speed = moves[0] * here[0] + moves[1] * here[1] + moves[2] * here[2]
    squares = geometry[0] * geometry[0] + geometry[1] * geometry[1] + geometry[2] * geometry[2]
    spread = (scale * viscosity * time_step / 12.0) * squares
    added = [speed * slopes[b] + moves[b] * slopes[3] + spread * curves[b] for b in range(3)]
    added.append(compress * (moves[0] * slopes[0] + moves[1] * slopes[1] + moves[2] * slopes[2]))
    return added


def partner_face(sent, main, ends_ref, from_low, from_high, meta, ghost_ref):
    row = lax.broadcasted_iota(jnp.int32, (8, 128), 0)
    along = meta[ALONG] == 1
    has_low = jnp.where(jnp.where(along, meta[HAS_HIGH], meta[HAS_LOW]) == 1, 1.0, 0.0)
    has_high = jnp.where(jnp.where(along, meta[HAS_LOW], meta[HAS_HIGH]) == 1, 1.0, 0.0)
    rows_of = lambda n: main[LEN * n : LEN * n + LEN, :]
    here = [rows_of(c) for c in range(4)]
    slopes, curves = [], []
    for c in range(4):
        slope, curve = face_stencil(turned_back(sent[LEN * c : LEN * c + LEN, :], meta))
        slopes.append(slope)
        curves.append(curve)
    added = edge_terms(here, [rows_of(4 + n) for n in range(3)], slopes, curves, 1.0)
    parts = [rows_of(7), rows_of(8), unpacked(main, 0), unpacked(main, 1)]

    ends_ref[...] = jnp.zeros((7, 8, 128), jnp.float32)
    metric_ends = unpacked(main, 2)
    for n in range(3):
        ends_ref[4 + n, 0:2, :] = metric_ends[4 * n : 4 * n + 2]
        ends_ref[4 + n, 6:8, :] = metric_ends[4 * n + 2 : 4 * n + 4]
    for c in range(4):
        below, above = from_low[2 * c : 2 * c + 2, :], from_high[2 * c : 2 * c + 2, :]
        ends_ref[c, 0:1, :] = has_low * jnp.where(along, above[1:2], below[0:1])
        ends_ref[c, 1:2, :] = has_low * jnp.where(along, above[0:1], below[1:2])
        ends_ref[c, 6:7, :] = has_high * jnp.where(along, below[1:2], above[0:1])
        ends_ref[c, 7:8, :] = has_high * jnp.where(along, below[0:1], above[1:2])
    slopes, curves = [], []
    for c in range(4):
        slope, curve = chain_stencil(ends_ref[c], row)
        slopes.append(slope)
        curves.append(curve)
    start = row < 4
    at_ends = [jnp.where(start, here[c][0:8], here[c][8:16]) for c in range(4)]
    more = edge_terms(at_ends, [ends_ref[4 + n] for n in range(3)], slopes, curves, 1.0)
    for c in range(4):
        values = parts[c] + added[c]
        ghost_ref[LEN * c : LEN * c + 8, :] = values[0:8] + jnp.where(start, more[c], 0.0)
        ghost_ref[LEN * c + 8 : LEN * c + LEN, :] = values[8:16] + jnp.where(start, 0.0, more[c])


def chain_stencil(second, row):
    first = jnp.where(row == 0, pltpu.roll(second, 7, 0), jnp.where(row == 7, pltpu.roll(second, 1, 0), 0.0))
    return jnp.where(row < 4, -1.0, 1.0) * (8.0 * first - second), 16.0 * first - second


def chain_terms(q, metric, chain_ref, scale, tiles, base, out):
    row = lax.broadcasted_iota(jnp.int32, (8, 128), 0)
    start = row < 4
    for t in tiles:
        where = slice(128 * t, 128 * t + 128)
        ends = lambda ref, n: jnp.where(start, ref[n, 0:8, where], ref[n, 8:16, where])
        slopes, curves = [], []
        for c in range(4):
            slope, curve = chain_stencil(chain_ref[c, :, where], row)
            slopes.append(slope)
            curves.append(curve)
        added = edge_terms([ends(q, c) for c in range(4)], [ends(metric, n) for n in range(3)], slopes, curves, scale)
        for c in range(4):
            out[c, 0:8, where] = base[c, 0:8, where] + jnp.where(start, added[c], 0.0)
            out[c, 8:16, where] = base[c, 8:16, where] + jnp.where(start, 0.0, added[c])


def joint_terms(q, metric, ghost_ref, face, scale, tiles, out):
    lane = lanes_of(LEN)

    def add(t, direction, slopes, curves):
        where = slice(128 * t, 128 * t + 128)
        here = [q[c, :, where] for c in range(4)]
        geometry = [metric[3 * direction + n, :, where] for n in range(3)]
        added = edge_terms(here, geometry, slopes, curves, scale)
        for c in range(4):
            out[c, :, where] = out[c, :, where] + added[c]

    ghost_of = lambda c: ghost_ref[16 * c : 16 * c + 16, :]
    if tiles[0] == 0:

        @pl.when(face == 2)
        def _():
            slopes, curves = [], []
            for c in range(4):
                ghost = ghost_of(c)
                first = jnp.where(lane < CROSS, ghost, 0.0)
                second = jnp.where(lane < CROSS, pltpu.roll(ghost, 80, 1), pltpu.roll(ghost, 48, 1))
                second = jnp.where(lane < 2 * CROSS, second, 0.0)
                slopes.append(second - 8.0 * first)
                curves.append(16.0 * first - second)
            add(0, 1, slopes, curves)

    if tiles[-1] == TILES - 1:

        @pl.when(face == 3)
        def _():
            slopes, curves = [], []
            for c in range(4):
                ghost = ghost_of(c)
                first = jnp.where(lane >= 80, pltpu.roll(ghost, 80, 1), 0.0)
                second = jnp.where(lane >= 32, pltpu.roll(ghost, 32, 1), 0.0)
                slopes.append(8.0 * first - second)
                curves.append(16.0 * first - second)
            add(TILES - 1, 1, slopes, curves)

    @pl.when(face >= 4)
    def _():
        toward = jnp.where(face == 4, -1.0, 1.0)
        for t in tiles:
            flat = 128 * t + lane
            j = flat // CROSS
            k = flat - j * CROSS
            depth = jnp.where(face == 4, k, CROSS - 1 - k)
            far = jnp.where(depth == 0, j + CROSS, j)[:8]
            slopes, curves = [], []
            for c in range(4):
                ghost = ghost_of(c)
                first = jnp.where(depth == 0, gather_lanes(ghost, j[:8]), 0.0)
                second = jnp.where(depth < 2, gather_lanes(ghost, far), 0.0)
                slopes.append(toward * (8.0 * first - second))
                curves.append(16.0 * first - second)
            add(t, 2, slopes, curves)


def turned_back(values, meta):
    lane = lanes_of()
    mirrored = jnp.where(lane < CROSS, CROSS - 1 - lane, jnp.where(lane < 2 * CROSS, 3 * CROSS - 1 - lane, lane))
    values = jnp.where(meta[ACROSS] == 1, gather_lanes(values, mirrored), values)
    return jnp.where(meta[ALONG] == 1, reversed_rows(values), values)


def face_stencil(ghost):
    lane = lanes_of(LEN)
    first = jnp.where(lane < CROSS, ghost, 0.0)
    second = jnp.where(lane < CROSS, pltpu.roll(ghost, 80, 1), pltpu.roll(ghost, 48, 1))
    second = jnp.where(lane < 2 * CROSS, second, 0.0)
    return second - 8.0 * first, 16.0 * first - second


def joint_kernel(bulk, sent, one, two, three, mate, meta, out, even_ref, odd_ref, ghost_ref, below, above):
    received = (mate, one, two, three)
    copy_part(meta[OWN], received, (0, GEOMETRY), ghost_ref)
    copy_part(meta[OWN + 1], received, PARTS[1], below)
    copy_part(meta[OWN + 2], received, PARTS[2], above)
    out[...] = bulk[...]
    face = meta[FACE]
    lane = lanes_of(LEN)
    mine = [turned_back(sent[LEN * n : LEN * n + LEN, :], meta) for n in range(7)]
    stencils = [face_stencil(ghost_ref[LEN * c : LEN * c + LEN, :]) for c in range(4)]
    slopes, curves = [one[0] for one in stencils], [one[1] for one in stencils]
    added = edge_terms(mine[:4], mine[4:], slopes, curves, 1.0)

    @pl.when(face == 2)
    def _():
        for c in range(4):
            out[c, :, 0:128] = out[c, :, 0:128] + jnp.where(lane < 2 * CROSS, added[c], 0.0)

    @pl.when(face == 3)
    def _():
        where = slice(128 * (TILES - 1), 128 * TILES)
        for c in range(4):
            value = jnp.where(lane >= 80, pltpu.roll(added[c], 80, 1), pltpu.roll(added[c], 112, 1))
            out[c, :, where] = out[c, :, where] + jnp.where(lane >= 32, value, 0.0)

    @pl.when(face >= 4)
    def _():
        for t in range(TILES):
            where = slice(128 * t, 128 * t + 128)
            flat = 128 * t + lane
            j = flat // CROSS
            k = flat - j * CROSS
            depth = jnp.where(face == 4, k, CROSS - 1 - k)
            index = jnp.where(depth == 0, j, j + CROSS)[:8]
            for c in range(4):
                value = jnp.where(depth < 2, gather_lanes(added[c], index), 0.0)
                out[c, :, where] = out[c, :, where] + value

    write_chain(out, even_ref, odd_ref, meta[POSITION])
    even = lax.rem(meta[POSITION], 2) == 0
    spare = slice(CELLS, CELLS + 128)
    even_ref[:, spare] = jnp.where(even, above[...], below[...])
    odd_ref[:, spare] = jnp.where(even, below[...], above[...])


def spread_ghosts(even_in, odd_in, meta, chain_ref):
    even = lax.rem(meta[POSITION], 2) == 0
    has_low = jnp.where(meta[HAS_LOW] == 1, 1.0, 0.0)
    has_high = jnp.where(meta[HAS_HIGH] == 1, 1.0, 0.0)
    for c in range(4):
        rows = slice(2 * c, 2 * c + 2)
        from_even, from_odd = even_in[rows, 0:CELLS], odd_in[rows, 0:CELLS]
        chain_ref[c, 2:6, :] = jnp.zeros((4, CELLS), jnp.float32)
        chain_ref[c, 0:2, :] = has_low * jnp.where(even, from_odd, from_even)
        chain_ref[c, 6:8, :] = has_high * jnp.where(even, from_even, from_odd)


def last_kernel(part, sent, q, metric, one, two, three, mate, even_in, odd_in, meta, out_hbm, *scratch):
    chain_ref, ghost_ref, main, ends_ref, out, sem = scratch
    even = lax.rem(meta[POSITION], 2) == 0
    copy_part(meta[OWN], (mate, one, two, three), PARTS[0], main)
    spare = slice(CELLS, CELLS + 128)
    from_even, from_odd = even_in[:, spare], odd_in[:, spare]
    from_low, from_high = jnp.where(even, from_odd, from_even), jnp.where(even, from_even, from_odd)
    partner_face(sent, main, ends_ref, from_low, from_high, meta, ghost_ref)
    spread_ghosts(even_in, odd_in, meta, chain_ref)
    copies = []
    for n in range(TILES // GROUP):
        tiles = range(GROUP * n, GROUP * n + GROUP)
        chain_terms(q, metric, chain_ref, 0.5, tiles, part, out)
        joint_terms(q, metric, ghost_ref, meta[FACE], 0.5, tiles, out)
        where = slice(128 * GROUP * n, 128 * GROUP * (n + 1))
        copies.append(pltpu.make_async_copy(out.at[:, :, where], out_hbm.at[:, :, where], sem.at[n]))
        copies[-1].start()
    for copy in copies:
        copy.wait()


f32 = functools.partial(jax.ShapeDtypeStruct, dtype=jnp.float32)
PARAMS = pltpu.CompilerParams(vmem_limit_bytes=24 * 1024 * 1024)
FIELD = f32((4, LEN, CELLS))
JOINT = f32((ROWS, 128))
CHAIN_TILES = pltpu.VMEM((4, 8, CELLS), jnp.float32)
GHOST = pltpu.VMEM((GEOMETRY, 128), jnp.float32)
TILE = pltpu.VMEM((8, 128), jnp.float32)


def local(kernel, shapes, operands, scratch=(), flops=1_000_000, **options):
    options.setdefault("out_specs", [VMEM] * len(shapes))
    return pl.pallas_call(
        kernel,
        out_shape=shapes,
        in_specs=[VMEM] * (len(operands) - 1) + [SMEM],
        scratch_shapes=list(scratch),
        compiler_params=PARAMS,
        cost_estimate=pl.CostEstimate(flops=flops, bytes_accessed=flops, transcendentals=0),
        **options,
    )(*operands)


def bulk(last, *operands):
    kernel = functools.partial(bulk_kernel, last)
    return local(kernel, [FIELD], operands, [] if last else [CHAIN_TILES] * 2, flops=12_000_000)[0]


def along_chain(even, odd):
    pairs = [(i, i + 1) for i in range(1, CHAIN - 1, 2)]
    from_odd = lax.ppermute(odd, "blk", pairs + [(b, a) for a, b in pairs])
    return lax.ppermute(even, "blk", [(i, i ^ 1) for i in range(CHAIN)]), from_odd


def on_device(state, metric, block_map, links):
    HBM = pl.BlockSpec(memory_space=pltpu.HBM)
    held = lambda x: pltpu.with_memory_space_constraint(x, pltpu.HBM)
    arrays = (state.reshape(4, LEN, CELLS), metric.reshape(9, LEN, CELLS), block_map, jnp.transpose(links, (1, 2, 0)))
    q, geometry, joint, even, odd, meta = pl.pallas_call(
        first_kernel,
        out_shape=[FIELD, f32((9, LEN, CELLS)), JOINT] + [f32((8, CELLS))] * 2 + [jax.ShapeDtypeStruct((16,), jnp.int32)],
        in_specs=[HBM] * 4,
        out_specs=[VMEM] * 5 + [SMEM],
        scratch_shapes=[
            pltpu.SMEM((SEGS * CHAIN,), jnp.int32),
            pltpu.SMEM((6, 4, SEGS * CHAIN), jnp.int32),
            pltpu.VMEM((LEN, 128), jnp.float32),
            pltpu.SemaphoreType.DMA((4,)),
        ],
        compiler_params=PARAMS,
    )(*map(held, arrays))
    across = lambda value, s: lax.ppermute(value, "seg", [(i, i ^ s) for i in range(SEGS)])
    from_even, from_odd = along_chain(even, odd)
    two, three = across(joint, 2), across(joint, 3)
    later, from_odd = lax.optimization_barrier((joint, from_odd))
    one = across(later, 1)
    one, two, three, from_even = lax.optimization_barrier((one, two, three, from_even))
    (picked,) = local(pick_kernel, [JOINT], (joint, one, two, three, meta))
    mate = lax.ppermute(picked, "seg", [(i, i ^ 4) for i in range(SEGS)])
    from_even, from_odd, _ = lax.optimization_barrier((from_even, from_odd, picked))
    part = bulk(False, q, geometry, from_even, from_odd, meta)
    q1, even, odd = local(
        joint_kernel,
        [FIELD] + [f32((8, CELLS + 128))] * 2,
        (part, joint, one, two, three, mate, meta),
        [GHOST, TILE, TILE],
    )
    from_even, from_odd = along_chain(even, odd)
    part = bulk(True, q1, geometry, q, meta)
    (advanced,) = local(
        last_kernel,
        [FIELD],
        (part, joint, q1, geometry, one, two, three, mate, from_even, from_odd, meta),
        [CHAIN_TILES, GHOST, pltpu.VMEM((BELOW, 128), jnp.float32), pltpu.VMEM((7, 8, 128), jnp.float32)]
        + [pltpu.VMEM((4, LEN, CELLS), jnp.float32), pltpu.SemaphoreType.DMA((TILES // GROUP,))],
        out_specs=[HBM],
    )
    return advanced.reshape(state.shape)


def solution(mesh):
    in_specs = (P(("seg", "blk"), None, None, None), P(("seg", "blk"), None, None, None), P(), P())
    out_specs = P(("seg", "blk"), None, None, None)
    return jax.shard_map(
        on_device, mesh=mesh, in_specs=in_specs, out_specs=out_specs, check_vma=False
    )
```

```python
import functools
import jax
import jax.numpy as jnp
from jax import lax
from jax.experimental import pallas as pl
from jax.experimental.pallas import tpu as pltpu
from jax.sharding import PartitionSpec as P

LEN, CROSS, CELLS, TILES = 16, 48, 2304, 18
GROUP = 6
GEOMETRY, BELOW, ABOVE, ROWS = 64, 144, 152, 160
USED, SPARE = 96, 32
FACE, ALONG, ACROSS, POSITION, HAS_LOW, HAS_HIGH, OWN, MATE = 0, 1, 2, 3, 4, 5, 6, 9
PARTS = ((0, BELOW), (BELOW, ABOVE), (ABOVE, ROWS))
SEGS, CHAIN = 8, 32
time_step = 0.05
viscosity = 0.2
compress = 1.0
SIGN = (-1.0, -1.0, -1.0, 1.0)
VMEM = pl.BlockSpec(memory_space=pltpu.VMEM)
SMEM = pl.BlockSpec(memory_space=pltpu.SMEM)


def lanes_of(rows=8):
    return lax.broadcasted_iota(jnp.int32, (rows, 128), 1)


def gather_lanes(values, index):
    parts = [
        jnp.take_along_axis(values[r : r + 8], index, axis=1, mode="promise_in_bounds")
        for r in range(0, values.shape[0], 8)
    ]
    return parts[0] if len(parts) == 1 else jnp.concatenate(parts, axis=0)


def reversed_rows(values):
    index = 7 - lax.broadcasted_iota(jnp.int32, (8, 128), 0)
    flip = lambda part: jnp.take_along_axis(part, index, axis=0, mode="promise_in_bounds")
    return jnp.concatenate([flip(values[8:16]), flip(values[0:8])], axis=0)


def joined_face(device, block_map, links):
    block = block_map[device]
    face, partner, along, across = jnp.int32(0), jnp.int32(-1), jnp.int32(0), jnp.int32(0)
    for side in range(2, 6):
        other = links[side, 0, block]
        here = other >= 0
        face = jnp.where(here, side, face)
        partner = jnp.where(here, other, partner)
        along = jnp.where(here, links[side, 2, block], along)
        across = jnp.where(here, links[side, 3, block], across)
    position = lax.rem(device, CHAIN)
    segment = jnp.int32(0)
    for s in range(SEGS):
        segment = jnp.where(block_map[s * CHAIN + position] == partner, s, segment)
    return face, segment, along, across


def face_source(face, across, first_layer):
    lane = lanes_of()
    layer = jnp.where(lane >= CROSS, 1, 0)
    place = lane - layer * CROSS
    place = jnp.where(across == 1, CROSS - 1 - place, place)
    depth = first_layer + layer
    depth = jnp.where((face == 3) | (face == 5), CROSS - 1 - depth, depth)
    return jnp.where(face <= 3, depth * CROSS + place, place * CROSS + depth)


def gather_face(load, source):
    index, owner = source & 127, source >> 7
    found = None
    for t in range(TILES):
        picked = gather_lanes(load(t), index)
        if found is None:
            found = picked
        else:
            inside = owner == t
            if picked.shape[0] == LEN:
                inside = jnp.concatenate([inside, inside], axis=0)
            found = jnp.where(inside, picked, found)
    return found


def write_chain(field, even_ref, odd_ref, position):
    even = lax.rem(position, 2) == 0
    for c in range(4):
        low, high = field[c, 0:2, :], field[c, LEN - 2 : LEN, :]
        even_ref[2 * c : 2 * c + 2, 0:CELLS] = jnp.where(even, high, low)
        odd_ref[2 * c : 2 * c + 2, 0:CELLS] = jnp.where(even, low, high)


def first_kernel(
    q_hbm, metric_hbm, map_hbm, links_hbm, q, metric, joint_ref, even_ref, odd_ref, meta, block_map, links, edges, sem
):
    copies = [
        pltpu.make_async_copy(source, target, sem.at[n])
        for n, (source, target) in enumerate(
            ((links_hbm, links), (map_hbm, block_map), (q_hbm, q), (metric_hbm, metric))
        )
    ]
    for copy in copies:
        copy.start()
    segment, position = lax.axis_index("seg"), lax.axis_index("blk")
    copies[0].wait()
    copies[1].wait()
    here = segment * CHAIN + position
    other = (segment ^ 4) * CHAIN + position
    before, after = jnp.where(position > 0, -1, 0), jnp.where(position < CHAIN - 1, 1, 0)
    face, partner, along, across = joined_face(here, block_map, links)
    low_face, low_partner, _, low_across = joined_face(here + before, block_map, links)
    high_face, high_partner, _, high_across = joined_face(here + after, block_map, links)
    own = (partner, low_partner, high_partner)
    mates = [joined_face(other + shift, block_map, links)[1] for shift in (0, before, after)]
    meta[FACE] = face
    meta[ALONG] = along
    meta[ACROSS] = across
    meta[POSITION] = position
    block = block_map[here]
    meta[HAS_LOW] = jnp.where(links[0, 0, block] >= 0, 1, 0)
    meta[HAS_HIGH] = jnp.where(links[1, 0, block] >= 0, 1, 0)
    for n in range(3):
        meta[OWN + n] = jnp.where(own[n] // 4 == segment // 4, (own[n] ^ segment) & 3, 0)
        meta[MATE + n] = (mates[n] ^ segment) & 3
    copies[2].wait()
    write_chain(q, even_ref, odd_ref, position)

    where = lambda t: slice(128 * t, 128 * t + 128)
    lane = lanes_of(LEN)
    near, deep = face_source(face, across, 0), face_source(face, across, 2)
    below, above = face_source(low_face, low_across, 0), face_source(high_face, high_across, 0)
    turned = lambda values: jnp.where(along == 1, reversed_rows(values), values)
    face_q = [gather_face(lambda t: q[c, :, where(t)], near) for c in range(4)]
    deeper = [gather_face(lambda t: q[c, :, where(t)], deep) for c in range(4)]
    for c in range(4):
        low_rows = gather_face(lambda t: q[c, 0:8, where(t)], below)
        joint_ref[BELOW + 2 * c : BELOW + 2 * c + 2, :] = low_rows[0:2]
        high_rows = gather_face(lambda t: q[c, 8:16, where(t)], above)
        joint_ref[ABOVE + 2 * c : ABOVE + 2 * c + 2, :] = high_rows[6:8]
    copies[3].wait()
    normal = jnp.where(face <= 3, 1, 2)
    inward = jnp.where((face == 3) | (face == 5), -1.0, 1.0)
    forward = jnp.where(along == 1, -1.0, 1.0)
    sideways = jnp.where(across == 1, -1.0, 1.0)
    geometry = []
    for row, sign in ((0, 1.0), (3 * normal, inward), (3 * (3 - normal), sideways)):
        for b in range(3):
            geometry.append(sign * gather_face(lambda t: metric[row + b, :, where(t)], near))
    part = own_face(face_q, deeper, geometry, meta)
    edges[...] = jnp.zeros((LEN, 128), jnp.float32)
    for n in range(3):
        values = forward * turned(geometry[n])
        edges[4 * n : 4 * n + 2, :] = values[0:2]
        edges[4 * n + 2 : 4 * n + 4, :] = values[14:16]
    packed = (turned(part[2]), turned(part[3]), edges[...])
    for n, values in enumerate(face_q + geometry[3:6] + part[:2]):
        third = pltpu.roll(packed[n // 3], USED - SPARE * (n % 3), 1)
        joint_ref[LEN * n : LEN * n + LEN, :] = jnp.where(lane < USED, turned(values), third)


def unpacked(main, n):
    lane = lanes_of(LEN)
    thirds = [
        pltpu.roll(main[LEN * (3 * n + h) : LEN * (3 * n + h) + LEN, :], (SPARE * h - USED) % 128, 1) for h in range(3)
    ]
    return jnp.where(lane < SPARE, thirds[0], jnp.where(lane < 2 * SPARE, thirds[1], thirds[2]))


def own_face(face_q, deeper, geometry, meta):
    lane = lanes_of(LEN)
    row = lax.broadcasted_iota(jnp.int32, (8, 128), 0)
    place = jnp.where(lane >= CROSS, lane - CROSS, lane)
    outer = lane < CROSS
    open_low = jnp.where(meta[HAS_LOW] == 0, 1.0, 0.0)
    open_high = jnp.where(meta[HAS_HIGH] == 0, 1.0, 0.0)
    stencils = []
    for c in range(4):
        here, deep = face_q[c], deeper[c]
        top, bottom = here[0:8], here[8:16]
        low = -SIGN[c] * open_low * jnp.where(row == 7, pltpu.roll(top, 7, 0), pltpu.roll(top, 5, 0))
        high = -SIGN[c] * open_high * jnp.where(row == 0, pltpu.roll(bottom, 1, 0), pltpu.roll(bottom, 3, 0))
        rows = jnp.concatenate([low, here, high], axis=0)
        along_i = [shifted_rows(rows, s) for s in (-2, -1)] + [here] + [shifted_rows(rows, s) for s in (1, 2)]
        normal = [
            jnp.zeros((LEN, 128), jnp.float32),
            jnp.where(outer, 0.0, pltpu.roll(here, 48, 1)),
            here,
            jnp.where(outer, pltpu.roll(here, 80, 1), pltpu.roll(deep, 48, 1)),
            deep,
        ]
        raw = [pltpu.roll(here, (-s) % 128, 1) if s else here for s in range(-2, 3)]
        wall = SIGN[c] * here
        second = SIGN[c] * jnp.where((place == 0) | (place == 46), raw[3], raw[1])
        sideways = [
            jnp.where(place < 2, second, raw[0]),
            jnp.where(place == 0, wall, raw[1]),
            here,
            jnp.where(place == 47, wall, raw[3]),
            jnp.where(place >= 46, second, raw[4]),
        ]
        stencils.append((along_i, normal, sideways))
    return advance(stencils, geometry)


def copy_part(choice, refs, rows, out):
    for n, ref in enumerate(refs):

        @pl.when(choice == n)
        def _(ref=ref):
            out[...] = ref[rows[0] : rows[1], :]


def pick_kernel(own, one, two, three, meta, out):
    for n, rows in enumerate(PARTS):
        copy_part(meta[MATE + n], (own, one, two, three), rows, out.at[rows[0] : rows[1], :])


def shifted_lanes(before, here, after, shift):
    lane = lanes_of(LEN)
    if shift > 0:
        return jnp.where(
            lane < 128 - shift, pltpu.roll(here, 128 - shift, 1), pltpu.roll(after, 128 - shift, 1)
        )
    return jnp.where(lane >= -shift, pltpu.roll(here, -shift, 1), pltpu.roll(before, -shift, 1))


def shifted_rows(padded, shift):
    return pltpu.roll(padded, (-shift) % 32, 0)[8:24]


def differences(m2, m1, here, p1, p2):
    return 8.0 * (p1 - m1) - (p2 - m2)


def bends(m2, m1, here, p1, p2):
    return 16.0 * (p1 + m1) - (p2 + m2) - 30.0 * here


def advance(stencils, geometry):
    here = [stencils[c][0][2] for c in range(4)]
    moves = [-(time_step / 12.0) * geometry[n] for n in range(9)]
    result = list(here)
    fall = None
    for a in range(3):
        g = geometry[3 * a : 3 * a + 3]
        n = moves[3 * a : 3 * a + 3]
        speed = n[0] * here[0] + n[1] * here[1] + n[2] * here[2]
        spread = (viscosity * time_step / 12.0) * (g[0] * g[0] + g[1] * g[1] + g[2] * g[2])
        drop = differences(*stencils[3][a])
        for b in range(3):
            slope = differences(*stencils[b][a])
            result[b] = result[b] + speed * slope + n[b] * drop + spread * bends(*stencils[b][a])
            term = n[b] * slope
            fall = term if fall is None else fall + term
    result[3] = result[3] + compress * fall
    return result


def chain_ghosts(q, even_in, odd_in, meta, low_ref, high_ref):
    even = lax.rem(meta[POSITION], 2) == 0
    for c in range(4):
        rows = slice(2 * c, 2 * c + 2)
        from_even, from_odd = even_in[rows, :], odd_in[rows, :]
        low_ref[c, 6:8, :] = jnp.where(even, from_odd, from_even)
        high_ref[c, 0:2, :] = jnp.where(even, from_even, from_odd)

    @pl.when(meta[HAS_LOW] == 0)
    def _():
        for c in range(4):
            low_ref[c, 7:8, :] = -SIGN[c] * q[c, 0:1, :]
            low_ref[c, 6:7, :] = -SIGN[c] * q[c, 1:2, :]

    @pl.when(meta[HAS_HIGH] == 0)
    def _():
        for c in range(4):
            high_ref[c, 0:1, :] = -SIGN[c] * q[c, LEN - 1 : LEN, :]
            high_ref[c, 1:2, :] = -SIGN[c] * q[c, LEN - 2 : LEN - 1, :]


def bulk_kernel(last, q, metric, *rest):
    if last:
        first, meta, out = rest
    else:
        even_in, odd_in, meta, out, low_ref, high_ref = rest
        chain_ghosts(q, even_in, odd_in, meta, low_ref, high_ref)
    lane = lanes_of(LEN)
    row = lax.broadcasted_iota(jnp.int32, (8, 128), 0)
    face, ends = meta[FACE], (meta[HAS_LOW] == 0, meta[HAS_HIGH] == 0)
    load = lambda c, t: q[c, :, 128 * t : 128 * t + 128]
    before_first, after_last = [], []
    for c in range(4):
        head = jnp.where(face == 2, 0.0, SIGN[c]) * load(c, 0)
        before_first.append(jnp.where(lane >= 80, pltpu.roll(head, 80, 1), pltpu.roll(head, 112, 1)))
        tail = jnp.where(face == 3, 0.0, SIGN[c]) * load(c, TILES - 1)
        after_last.append(jnp.where(lane < CROSS, pltpu.roll(tail, 48, 1), pltpu.roll(tail, 16, 1)))

    def tile(c, t):
        return before_first[c] if t < 0 else after_last[c] if t >= TILES else load(c, t)

    low_scale = jnp.where(face == 4, 0.0, 1.0)
    high_scale = jnp.where(face == 5, 0.0, 1.0)
    open_low = jnp.where(ends[0], 1.0, 0.0)
    open_high = jnp.where(ends[1], 1.0, 0.0)
    for t in range(TILES):
        flat = 128 * t + lane
        k = flat - (flat // CROSS) * CROSS
        scale = jnp.where(k < 2, low_scale, high_scale)
        where = slice(128 * t, 128 * t + 128)
        stencils = []
        for c in range(4):
            before, here, after = tile(c, t - 1), tile(c, t), tile(c, t + 1)
            if last:
                top, bottom = here[0:8], here[8:16]
                low = -SIGN[c] * open_low * jnp.where(row == 7, pltpu.roll(top, 7, 0), pltpu.roll(top, 5, 0))
                high = -SIGN[c] * open_high * jnp.where(row == 0, pltpu.roll(bottom, 1, 0), pltpu.roll(bottom, 3, 0))
            else:
                low, high = low_ref[c, :, where], high_ref[c, :, where]
            rows = jnp.concatenate([low, here, high], axis=0)
            along_i = [shifted_rows(rows, s) for s in (-2, -1)] + [here] + [shifted_rows(rows, s) for s in (1, 2)]
            along_j = [shifted_lanes(before, here, after, CROSS * s) if s else here for s in range(-2, 3)]
            raw = [shifted_lanes(before, here, after, s) if s else here for s in range(-2, 3)]
            factor = SIGN[c] * scale
            nearest = factor * here
            second = factor * jnp.where((k == 0) | (k == 46), raw[3], raw[1])
            along_k = [
                jnp.where(k < 2, second, raw[0]),
                jnp.where(k == 0, nearest, raw[1]),
                here,
                jnp.where(k == 47, nearest, raw[3]),
                jnp.where(k >= 46, second, raw[4]),
            ]
            stencils.append((along_i, along_j, along_k))
        values = advance(stencils, [metric[n, :, where] for n in range(9)])
        for c in range(4):
            kept = 0.5 * first[c, :, where] + 0.5 * values[c] if last else values[c]
            out[c, :, where] = kept


def edge_terms(here, geometry, slopes, curves, scale):
    moves = [-(scale * time_step / 12.0) * g for g in geometry]
    speed = moves[0] * here[0] + moves[1] * here[1] + moves[2] * here[2]
    squares = geometry[0] * geometry[0] + geometry[1] * geometry[1] + geometry[2] * geometry[2]
    spread = (scale * viscosity * time_step / 12.0) * squares
    added = [speed * slopes[b] + moves[b] * slopes[3] + spread * curves[b] for b in range(3)]
    added.append(compress * (moves[0] * slopes[0] + moves[1] * slopes[1] + moves[2] * slopes[2]))
    return added


def partner_face(sent, main, ends_ref, from_low, from_high, meta, ghost_ref):
    row = lax.broadcasted_iota(jnp.int32, (8, 128), 0)
    along = meta[ALONG] == 1
    has_low = jnp.where(jnp.where(along, meta[HAS_HIGH], meta[HAS_LOW]) == 1, 1.0, 0.0)
    has_high = jnp.where(jnp.where(along, meta[HAS_LOW], meta[HAS_HIGH]) == 1, 1.0, 0.0)
    rows_of = lambda n: main[LEN * n : LEN * n + LEN, :]
    here = [rows_of(c) for c in range(4)]
    slopes, curves = [], []
    for c in range(4):
        slope, curve = face_stencil(turned_back(sent[LEN * c : LEN * c + LEN, :], meta))
        slopes.append(slope)
        curves.append(curve)
    added = edge_terms(here, [rows_of(4 + n) for n in range(3)], slopes, curves, 1.0)
    parts = [rows_of(7), rows_of(8), unpacked(main, 0), unpacked(main, 1)]

    ends_ref[...] = jnp.zeros((7, 8, 128), jnp.float32)
    metric_ends = unpacked(main, 2)
    for n in range(3):
        ends_ref[4 + n, 0:2, :] = metric_ends[4 * n : 4 * n + 2]
        ends_ref[4 + n, 6:8, :] = metric_ends[4 * n + 2 : 4 * n + 4]
    for c in range(4):
        below, above = from_low[2 * c : 2 * c + 2, :], from_high[2 * c : 2 * c + 2, :]
        ends_ref[c, 0:1, :] = has_low * jnp.where(along, above[1:2], below[0:1])
        ends_ref[c, 1:2, :] = has_low * jnp.where(along, above[0:1], below[1:2])
        ends_ref[c, 6:7, :] = has_high * jnp.where(along, below[1:2], above[0:1])
        ends_ref[c, 7:8, :] = has_high * jnp.where(along, below[0:1], above[1:2])
    slopes, curves = [], []
    for c in range(4):
        slope, curve = chain_stencil(ends_ref[c], row)
        slopes.append(slope)
        curves.append(curve)
    start = row < 4
    at_ends = [jnp.where(start, here[c][0:8], here[c][8:16]) for c in range(4)]
    more = edge_terms(at_ends, [ends_ref[4 + n] for n in range(3)], slopes, curves, 1.0)
    for c in range(4):
        values = parts[c] + added[c]
        ghost_ref[LEN * c : LEN * c + 8, :] = values[0:8] + jnp.where(start, more[c], 0.0)
        ghost_ref[LEN * c + 8 : LEN * c + LEN, :] = values[8:16] + jnp.where(start, 0.0, more[c])


def chain_stencil(second, row):
    first = jnp.where(row == 0, pltpu.roll(second, 7, 0), jnp.where(row == 7, pltpu.roll(second, 1, 0), 0.0))
    return jnp.where(row < 4, -1.0, 1.0) * (8.0 * first - second), 16.0 * first - second


def chain_terms(q, metric, chain_ref, scale, tiles, base, out):
    row = lax.broadcasted_iota(jnp.int32, (8, 128), 0)
    start = row < 4
    for t in tiles:
        where = slice(128 * t, 128 * t + 128)
        ends = lambda ref, n: jnp.where(start, ref[n, 0:8, where], ref[n, 8:16, where])
        slopes, curves = [], []
        for c in range(4):
            slope, curve = chain_stencil(chain_ref[c, :, where], row)
            slopes.append(slope)
            curves.append(curve)
        added = edge_terms([ends(q, c) for c in range(4)], [ends(metric, n) for n in range(3)], slopes, curves, scale)
        for c in range(4):
            out[c, 0:8, where] = base[c, 0:8, where] + jnp.where(start, added[c], 0.0)
            out[c, 8:16, where] = base[c, 8:16, where] + jnp.where(start, 0.0, added[c])


def joint_terms(q, metric, ghost_ref, spread_ref, face, scale, tiles, out):
    lane = lanes_of(LEN)

    def add(t, direction, slopes, curves):
        where = slice(128 * t, 128 * t + 128)
        here = [q[c, :, where] for c in range(4)]
        geometry = [metric[3 * direction + n, :, where] for n in range(3)]
        added = edge_terms(here, geometry, slopes, curves, scale)
        for c in range(4):
            out[c, :, where] = out[c, :, where] + added[c]

    ghost_of = lambda c: ghost_ref[16 * c : 16 * c + 16, :]
    if tiles[0] == 0:

        @pl.when(face == 2)
        def _():
            slopes, curves = [], []
            for c in range(4):
                ghost = ghost_of(c)
                first = jnp.where(lane < CROSS, ghost, 0.0)
                second = jnp.where(lane < CROSS, pltpu.roll(ghost, 80, 1), pltpu.roll(ghost, 48, 1))
                second = jnp.where(lane < 2 * CROSS, second, 0.0)
                slopes.append(second - 8.0 * first)
                curves.append(16.0 * first - second)
            add(0, 1, slopes, curves)

    if tiles[-1] == TILES - 1:

        @pl.when(face == 3)
        def _():
            slopes, curves = [], []
            for c in range(4):
                ghost = ghost_of(c)
                first = jnp.where(lane >= 80, pltpu.roll(ghost, 80, 1), 0.0)
                second = jnp.where(lane >= 32, pltpu.roll(ghost, 32, 1), 0.0)
                slopes.append(8.0 * first - second)
                curves.append(16.0 * first - second)
            add(TILES - 1, 1, slopes, curves)

    @pl.when(face >= 4)
    def _():
        for t in tiles:
            where = slice(128 * t, 128 * t + 128)
            flat = 128 * t + lane
            j = flat // CROSS
            k = flat - j * CROSS
            depth = jnp.where(face == 4, k, CROSS - 1 - k)
            index = jnp.where(depth == 0, j, j + CROSS)[:8]
            for c in range(4):
                value = gather_lanes(spread_ref[LEN * c : LEN * c + LEN, :], index)
                out[c, :, where] = out[c, :, where] + jnp.where(depth < 2, value, 0.0)


def turned_back(values, meta):
    lane = lanes_of()
    mirrored = jnp.where(lane < CROSS, CROSS - 1 - lane, jnp.where(lane < 2 * CROSS, 3 * CROSS - 1 - lane, lane))
    values = jnp.where(meta[ACROSS] == 1, gather_lanes(values, mirrored), values)
    return jnp.where(meta[ALONG] == 1, reversed_rows(values), values)


def face_stencil(ghost):
    lane = lanes_of(LEN)
    first = jnp.where(lane < CROSS, ghost, 0.0)
    second = jnp.where(lane < CROSS, pltpu.roll(ghost, 80, 1), pltpu.roll(ghost, 48, 1))
    second = jnp.where(lane < 2 * CROSS, second, 0.0)
    return second - 8.0 * first, 16.0 * first - second


def joint_kernel(bulk, sent, one, two, three, mate, meta, out, even_ref, odd_ref, ghost_ref, below, above):
    received = (mate, one, two, three)
    copy_part(meta[OWN], received, (0, GEOMETRY), ghost_ref)
    copy_part(meta[OWN + 1], received, PARTS[1], below)
    copy_part(meta[OWN + 2], received, PARTS[2], above)
    out[...] = bulk[...]
    face = meta[FACE]
    lane = lanes_of(LEN)
    mine = [turned_back(sent[LEN * n : LEN * n + LEN, :], meta) for n in range(7)]
    stencils = [face_stencil(ghost_ref[LEN * c : LEN * c + LEN, :]) for c in range(4)]
    slopes, curves = [one[0] for one in stencils], [one[1] for one in stencils]
    added = edge_terms(mine[:4], mine[4:], slopes, curves, 1.0)

    @pl.when(face == 2)
    def _():
        for c in range(4):
            out[c, :, 0:128] = out[c, :, 0:128] + jnp.where(lane < 2 * CROSS, added[c], 0.0)

    @pl.when(face == 3)
    def _():
        where = slice(128 * (TILES - 1), 128 * TILES)
        for c in range(4):
            value = jnp.where(lane >= 80, pltpu.roll(added[c], 80, 1), pltpu.roll(added[c], 112, 1))
            out[c, :, where] = out[c, :, where] + jnp.where(lane >= 32, value, 0.0)

    @pl.when(face >= 4)
    def _():
        for t in range(TILES):
            where = slice(128 * t, 128 * t + 128)
            flat = 128 * t + lane
            j = flat // CROSS
            k = flat - j * CROSS
            depth = jnp.where(face == 4, k, CROSS - 1 - k)
            index = jnp.where(depth == 0, j, j + CROSS)[:8]
            for c in range(4):
                value = jnp.where(depth < 2, gather_lanes(added[c], index), 0.0)
                out[c, :, where] = out[c, :, where] + value

    write_chain(out, even_ref, odd_ref, meta[POSITION])
    even = lax.rem(meta[POSITION], 2) == 0
    spare = slice(CELLS, CELLS + 128)
    even_ref[:, spare] = jnp.where(even, above[...], below[...])
    odd_ref[:, spare] = jnp.where(even, below[...], above[...])


def spread_ghosts(even_in, odd_in, meta, chain_ref):
    even = lax.rem(meta[POSITION], 2) == 0
    has_low = jnp.where(meta[HAS_LOW] == 1, 1.0, 0.0)
    has_high = jnp.where(meta[HAS_HIGH] == 1, 1.0, 0.0)
    for c in range(4):
        rows = slice(2 * c, 2 * c + 2)
        from_even, from_odd = even_in[rows, 0:CELLS], odd_in[rows, 0:CELLS]
        chain_ref[c, 2:6, :] = jnp.zeros((4, CELLS), jnp.float32)
        chain_ref[c, 0:2, :] = has_low * jnp.where(even, from_odd, from_even)
        chain_ref[c, 6:8, :] = has_high * jnp.where(even, from_even, from_odd)


def last_kernel(part, sent, q, metric, one, two, three, mate, even_in, odd_in, meta, out_hbm, *scratch):
    chain_ref, ghost_ref, spread_ref, main, ends_ref, out, sem = scratch
    even = lax.rem(meta[POSITION], 2) == 0
    copy_part(meta[OWN], (mate, one, two, three), PARTS[0], main)
    spare = slice(CELLS, CELLS + 128)
    from_even, from_odd = even_in[:, spare], odd_in[:, spare]
    from_low, from_high = jnp.where(even, from_odd, from_even), jnp.where(even, from_even, from_odd)
    partner_face(sent, main, ends_ref, from_low, from_high, meta, ghost_ref)

    @pl.when(meta[FACE] >= 4)
    def _():
        source = face_source(meta[FACE], 0, 0)
        own = [gather_face(lambda t: q[c, :, 128 * t : 128 * t + 128], source) for c in range(4)]
        inward = [turned_back(sent[LEN * n : LEN * n + LEN, :], meta) for n in range(4, 7)]
        stencils = [face_stencil(ghost_ref[LEN * c : LEN * c + LEN, :]) for c in range(4)]
        added = edge_terms(own, inward, [pair[0] for pair in stencils], [pair[1] for pair in stencils], 0.5)
        for c in range(4):
            spread_ref[LEN * c : LEN * c + LEN, :] = added[c]

    spread_ghosts(even_in, odd_in, meta, chain_ref)
    copies = []
    for n in range(TILES // GROUP):
        tiles = range(GROUP * n, GROUP * n + GROUP)
        chain_terms(q, metric, chain_ref, 0.5, tiles, part, out)
        joint_terms(q, metric, ghost_ref, spread_ref, meta[FACE], 0.5, tiles, out)
        where = slice(128 * GROUP * n, 128 * GROUP * (n + 1))
        copies.append(pltpu.make_async_copy(out.at[:, :, where], out_hbm.at[:, :, where], sem.at[n]))
        copies[-1].start()
    for copy in copies:
        copy.wait()


f32 = functools.partial(jax.ShapeDtypeStruct, dtype=jnp.float32)
PARAMS = pltpu.CompilerParams(vmem_limit_bytes=24 * 1024 * 1024)
FIELD = f32((4, LEN, CELLS))
JOINT = f32((ROWS, 128))
CHAIN_TILES = pltpu.VMEM((4, 8, CELLS), jnp.float32)
GHOST = pltpu.VMEM((GEOMETRY, 128), jnp.float32)
TILE = pltpu.VMEM((8, 128), jnp.float32)


def local(kernel, shapes, operands, scratch=(), flops=1_000_000, **options):
    options.setdefault("out_specs", [VMEM] * len(shapes))
    return pl.pallas_call(
        kernel,
        out_shape=shapes,
        in_specs=[VMEM] * (len(operands) - 1) + [SMEM],
        scratch_shapes=list(scratch),
        compiler_params=PARAMS,
        cost_estimate=pl.CostEstimate(flops=flops, bytes_accessed=flops, transcendentals=0),
        **options,
    )(*operands)


def bulk(last, *operands):
    kernel = functools.partial(bulk_kernel, last)
    return local(kernel, [FIELD], operands, [] if last else [CHAIN_TILES] * 2, flops=12_000_000)[0]


def along_chain(even, odd):
    pairs = [(i, i + 1) for i in range(1, CHAIN - 1, 2)]
    from_odd = lax.ppermute(odd, "blk", pairs + [(b, a) for a, b in pairs])
    return lax.ppermute(even, "blk", [(i, i ^ 1) for i in range(CHAIN)]), from_odd


def on_device(state, metric, block_map, links):
    HBM = pl.BlockSpec(memory_space=pltpu.HBM)
    held = lambda x: pltpu.with_memory_space_constraint(x, pltpu.HBM)
    arrays = (state.reshape(4, LEN, CELLS), metric.reshape(9, LEN, CELLS), block_map, jnp.transpose(links, (1, 2, 0)))
    q, geometry, joint, even, odd, meta = pl.pallas_call(
        first_kernel,
        out_shape=[FIELD, f32((9, LEN, CELLS)), JOINT] + [f32((8, CELLS))] * 2 + [jax.ShapeDtypeStruct((16,), jnp.int32)],
        in_specs=[HBM] * 4,
        out_specs=[VMEM] * 5 + [SMEM],
        scratch_shapes=[
            pltpu.SMEM((SEGS * CHAIN,), jnp.int32),
            pltpu.SMEM((6, 4, SEGS * CHAIN), jnp.int32),
            pltpu.VMEM((LEN, 128), jnp.float32),
            pltpu.SemaphoreType.DMA((4,)),
        ],
        compiler_params=PARAMS,
    )(*map(held, arrays))
    across = lambda value, s: lax.ppermute(value, "seg", [(i, i ^ s) for i in range(SEGS)])
    from_even, from_odd = along_chain(even, odd)
    two, three = across(joint, 2), across(joint, 3)
    later, from_odd = lax.optimization_barrier((joint, from_odd))
    one = across(later, 1)
    one, two, three, from_even = lax.optimization_barrier((one, two, three, from_even))
    (picked,) = local(pick_kernel, [JOINT], (joint, one, two, three, meta))
    mate = lax.ppermute(picked, "seg", [(i, i ^ 4) for i in range(SEGS)])
    from_even, from_odd, _ = lax.optimization_barrier((from_even, from_odd, picked))
    part = bulk(False, q, geometry, from_even, from_odd, meta)
    q1, even, odd = local(
        joint_kernel,
        [FIELD] + [f32((8, CELLS + 128))] * 2,
        (part, joint, one, two, three, mate, meta),
        [GHOST, TILE, TILE],
    )
    from_even, from_odd = along_chain(even, odd)
    part = bulk(True, q1, geometry, q, meta)
    (advanced,) = local(
        last_kernel,
        [FIELD],
        (part, joint, q1, geometry, one, two, three, mate, from_even, from_odd, meta),
        [CHAIN_TILES, GHOST, GHOST, pltpu.VMEM((BELOW, 128), jnp.float32), pltpu.VMEM((7, 8, 128), jnp.float32)]
        + [pltpu.VMEM((4, LEN, CELLS), jnp.float32), pltpu.SemaphoreType.DMA((TILES // GROUP,))],
        out_specs=[HBM],
    )
    return advanced.reshape(state.shape)


def solution(mesh):
    in_specs = (P(("seg", "blk"), None, None, None), P(("seg", "blk"), None, None, None), P(), P())
    out_specs = P(("seg", "blk"), None, None, None)
    return jax.shard_map(
        on_device, mesh=mesh, in_specs=in_specs, out_specs=out_specs, check_vma=False
    )
```
